32 devices in a mesh: leaf: 2 (over x), row: 4 (over y, core), col: 4 (over z).
Axes of the slice: x: 2, y: 2, z: 4, core: 2. Of those that a mesh axis runs over, the one named last changes fastest.
Arguments:
- tokens: bfloat16 [20480, 1152], P(('leaf', 'col'), 'row'), parts along dimension 0, may hold values from -6 to 6
- attention_gain: bfloat16 [1152], P('row'), may hold values from 0.5 to 1.5
- joint_weight: bfloat16 [1152, 1920], P('row', 'col'), may hold values from -0.1875 to 0.1875
- output_weight: bfloat16 [1152, 1152], P('col', 'row'), may hold values from -4 to 4
- feed_gain: bfloat16 [1152], P('row'), may hold values from 0.5 to 1.5
- gate_weight: bfloat16 [1152, 3072], P('row', 'col'), may hold values from -0.1875 to 0.1875
- up_weight: bfloat16 [1152, 3072], P('row', 'col'), may hold values from -0.1875 to 0.1875
- down_weight: bfloat16 [3072, 1152], P('col', 'row'), may hold values from -0.109375 to 0.109375
- cotangent: bfloat16 [20480, 1152], P(('leaf', 'col'), 'row'), parts along dimension 0, may hold values from -6 to 6
- segment_lengths: int32 [26], P('leaf'), parts along dimension 0, may hold values from 256 to 4096, as said below
- parents: int32 [26], P('leaf'), parts along dimension 0, may hold values from 0 to 4, as said below
Outputs:
- layer_output: bfloat16 [20480, 1152], P(('leaf', 'col'), 'row'), parts along dimension 0
- input_gradient: float32 [20480, 1152], P(('leaf', 'col'), 'row'), parts along dimension 0
- attention_gain_gradient: float32 [2304], P(('leaf', 'row')), parts along dimension 0
- joint_gradient: float32 [2304, 1920], P(('leaf', 'row'), 'col'), parts along dimension 0
- output_gradient: float32 [2304, 1152], P(('leaf', 'col'), 'row'), parts along dimension 0
- feed_gain_gradient: float32 [2304], P(('leaf', 'row')), parts along dimension 0
- gate_gradient: float32 [2304, 3072], P(('leaf', 'row'), 'col'), parts along dimension 0
- up_gradient: float32 [2304, 3072], P(('leaf', 'row'), 'col'), parts along dimension 0
- down_gradient: float32 [6144, 1152], P(('leaf', 'col'), 'row'), parts along dimension 0
The draws below stay inside these ranges and needn't reach their ends.
There are 2 independent parts, one for each index of `leaf`. The reference program is written for one: setup_inputs(seed, part) draws one part's arguments, and reference() takes and returns one part's arrays. A program takes and returns all parts, laid end to end along the dimension named above; an argument that names none is the same for every part. Nothing has to cross between parts.
Inputs may be any that keep to these rules, and one draw needn't show every extreme that they name: `segment_lengths`: each tree has 13 segments laid out in this order: a trunk of 4096 tokens, four branches, eight leaves; each tree holds 10240 tokens. `parents`: segment numbers count from 0 within each part. A trunk is its own parent, every branch's parent is its tree's trunk, and each branch is the parent of two leaves of its tree.
All inputs are finite; a program needn't handle non-finite values.
Results may differ from the reference program's by a relative error of at most 0.035.
Values may be sent and summed in bfloat16 or wider, within the bound.
No kernel may reach another device: no remote copies, remote signals or barrier semaphores. Data moves between devices by JAX's collectives and lax.ppermute only.
A program may use at most 384 MiB of HBM per device.

```python
import jax
import jax.numpy as jnp
from jax import lax

D = 1152
HEADS = 18
KV_HEADS = 6
HEAD_DIM = 64
FF = 3072
TRUNK = 4096
SEG = 512
TREES = 1
TOKENS = 10240
ATT = 1152
QKV = 1920


def tree_layout(key):
    base = jax.random.fold_in(key, 4099)
    length_key, sign_key, order_key = jax.random.split(base, 3)
    shifts = jax.random.randint(length_key, (TREES, 6), -(SEG // 2), SEG // 2 + 1)
    signs = jax.random.randint(sign_key, (TREES,), 0, 2) * 2 - 1
    shifts = shifts.at[:, 2].set(signs * (SEG // 2))
    paired = jnp.stack([SEG + shifts, SEG - shifts], axis=2).reshape(TREES, 12)
    trunk = jnp.full((TREES, 1), TRUNK, jnp.int32)
    lengths = jnp.concatenate([trunk, paired.astype(jnp.int32)], axis=1).reshape(TREES * 13)
    ranks = jax.random.randint(order_key, (TREES, 8), 0, 1 << 20) * 8 + jnp.arange(8, dtype=jnp.int32)[None, :]
    order = jnp.argsort(ranks, axis=1, stable=True)
    base_index = (jnp.arange(TREES, dtype=jnp.int32) * 13)[:, None]
    leaf_parents = base_index + 1 + order // 2
    upper = jnp.broadcast_to(base_index, (TREES, 5))
    parents = jnp.concatenate([upper, leaf_parents], axis=1).reshape(TREES * 13)
    return (lengths.astype(jnp.int32), parents.astype(jnp.int32))


def draw_segment_lengths(key, part):
    return tree_layout(key)[0]


def draw_parents(key, part):
    return tree_layout(key)[1]


def levels(rng, shape, pieces, least, top_value):
    level, own = 1.0, jax.random.fold_in(rng, 6)
    for position, blocks in pieces:
        draws = jnp.exp(jax.random.uniform(jax.random.fold_in(own, position), (blocks,), jnp.float32, least / len(pieces), top_value / len(pieces)))
        level = level * jnp.repeat(draws, shape[position] // blocks).reshape([-1 if axis == position else 1 for axis in range(len(shape))])
    return level


def gaussian(key, extent, width, most, cuts=(), kind=jnp.bfloat16):
    values = jax.random.normal(key, extent, jnp.float32) * width
    if len(cuts) > 0:
        values = levels(key, extent, cuts, -0.22, 0.18) * values
    return jnp.clip(values, min=-most, max=most).astype(kind)


def setup_inputs(seed: int = 0, part: int = 0) -> dict:
    streams_of = jax.random.split(jax.random.key(seed), 12)
    own_keys = jax.random.split(jax.random.fold_in(streams_of[11], part), 12)
    tokens = gaussian(own_keys[0], (TOKENS, D), 1.0, 6.0, ((0, 4), (1, 4)))
    attention_gain = jnp.clip(1.0 + 0.1 * jax.random.normal(streams_of[1], (D,), jnp.float32), 0.5, 1.5).astype(jnp.bfloat16)
    joint_weight = gaussian(streams_of[2], (D, QKV), D ** -0.5, 0.1875, ((0, 4), (1, 4)))
    output_weight = gaussian(streams_of[3], (ATT, D), (max(ATT // 512, 1)) ** -0.5, 4.0, ((0, 4), (1, 4)))
    feed_gain = jnp.clip(1.0 + 0.1 * jax.random.normal(streams_of[4], (D,), jnp.float32), 0.5, 1.5).astype(jnp.bfloat16)
    gate_weight = gaussian(streams_of[5], (D, FF), D ** -0.5, 0.1875, ((0, 4), (1, 4)))
    up_weight = gaussian(streams_of[6], (D, FF), D ** -0.5, 0.1875, ((0, 4), (1, 4)))
    down_weight = gaussian(streams_of[7], (FF, D), FF ** -0.5, 0.109375, ((0, 4), (1, 4)))
    cotangent = gaussian(own_keys[8], (TOKENS, D), 1.0, 6.0, ((0, 4), (1, 4)))
    segment_lengths = draw_segment_lengths(jax.random.fold_in(jax.random.fold_in(streams_of[11], part), 71), part)
    parents = draw_parents(jax.random.fold_in(jax.random.fold_in(streams_of[11], part), 71), part)
    return dict(tokens=tokens, attention_gain=attention_gain, joint_weight=joint_weight, output_weight=output_weight, feed_gain=feed_gain, gate_weight=gate_weight, up_weight=up_weight, down_weight=down_weight, cotangent=cotangent, segment_lengths=segment_lengths, parents=parents)


EPSILON = 1e-05
THETA = 10000.0

@jax.custom_vjp
def low(v):
    return lax.optimization_barrier(v.astype(jnp.bfloat16)).astype(jnp.float32)

@jax.custom_vjp
def low_back(v):
    return v

def low_keep(v):
    return (low(v), None)

def low_pass(kept, grad):
    return (grad,)

def back_keep(v):
    return (v, None)

def back_low(kept, grad):
    return (low(grad),)
low.defvjp(low_keep, low_pass)
low_back.defvjp(back_keep, back_low)

def tree_tables(segment_lengths, parents):
    count = segment_lengths.shape[0]
    ends = jnp.cumsum(segment_lengths).astype(jnp.int32)
    starts = (ends - segment_lengths).astype(jnp.int32)
    labels = jnp.arange(count, dtype=jnp.int32)
    grand = parents[parents.astype(jnp.int32)].astype(jnp.int32)
    self_mark = labels[:, None] == labels[None, :]
    parent_mark = parents[:, None] == labels[None, :]
    grand_mark = grand[:, None] == labels[None, :]
    ancestry = (self_mark | parent_mark | grand_mark).astype(jnp.float32)
    strict = (parent_mark | grand_mark) & jnp.logical_not(self_mark)
    offsets = lax.optimization_barrier(jnp.sum(jnp.where(strict, segment_lengths[None, :], 0), axis=1)).astype(jnp.int32)
    return (ends, starts, ancestry, offsets)

def token_info(index, tables):
    ends, starts, ancestry, offsets = tables
    count = ends.shape[0]
    segment = lax.optimization_barrier(jnp.sum((index[:, None] >= ends[None, :]).astype(jnp.int32), axis=1)).astype(jnp.int32)
    segment_hot = segment[:, None] == jnp.arange(count, dtype=jnp.int32)[None, :]
    shift = lax.optimization_barrier(jnp.sum(jnp.where(segment_hot, (offsets - starts)[None, :], 0), axis=1)).astype(jnp.int32)
    depth = (index + shift).astype(jnp.int32)
    return (segment_hot.astype(jnp.float32), depth, segment)

def rotary_tables(depth):
    half = HEAD_DIM // 2
    rates = THETA ** (-jnp.arange(half, dtype=jnp.float32) / half)
    angles = depth.astype(jnp.float32)[:, None] * rates[None, :]
    return (jnp.cos(angles), jnp.sin(angles))

def turn(value, cosines, sines):
    half = value.shape[-1] // 2
    former, latter = (value[..., :half], value[..., half:])
    cos_part = cosines[:, None, :]
    sin_part = sines[:, None, :]
    return jnp.concatenate([former * cos_part - latter * sin_part, latter * cos_part + former * sin_part], axis=-1)

def root_norm(value, gain):
    return value * lax.rsqrt(lax.optimization_barrier(jnp.mean(value * value, axis=-1, keepdims=True)) + EPSILON) * gain[None, :]

def forward(tokens, attention_gain, joint_weight, output_weight, feed_gain, gate_weight, up_weight, down_weight, reach, key_hot, index, cosines, sines):
    highest = lax.Precision.HIGHEST
    attend_width = HEADS * HEAD_DIM
    key_width = KV_HEADS * HEAD_DIM
    repeat = HEADS // KV_HEADS
    scale = HEAD_DIM ** (-0.5)
    normed_one = low(root_norm(tokens, attention_gain))
    joint = low(low_back(jnp.dot(normed_one, joint_weight, precision=highest)))
    queries = low(turn(joint[:, :attend_width].reshape(TOKENS, HEADS, HEAD_DIM), cosines, sines))
    queries = queries.reshape(TOKENS, KV_HEADS, repeat, HEAD_DIM)
    keys = low(turn(joint[:, attend_width:attend_width + key_width].reshape(TOKENS, KV_HEADS, HEAD_DIM), cosines, sines))
    values = joint[:, attend_width + key_width:].reshape(TOKENS, KV_HEADS, HEAD_DIM)
    span = min(512, TOKENS)
    count = TOKENS // span

    def one_block(item):
        block_queries, block_reach, block_index = item
        scores = low_back(jnp.einsum('qgrd,kgd->grqk', block_queries, keys, precision=highest) * scale)
        allowed = (jnp.dot(block_reach, key_hot.T, precision=highest) > 0.5) & (index[None, :] <= block_index[:, None])
        chances = low(jax.nn.softmax(jnp.where(allowed[None, None], scores, -jnp.inf), axis=-1))
        return low(low_back(jnp.einsum('grqk,kgd->qgrd', chances, values, precision=highest)))
    attended = lax.map(jax.checkpoint(one_block), (queries.reshape(count, span, KV_HEADS, repeat, HEAD_DIM), reach.reshape(count, span, reach.shape[1]), index.reshape(count, span)))
    attended = attended.reshape(TOKENS, attend_width)
    hidden = tokens + low_back(jnp.dot(attended, output_weight, precision=highest))
    normed_two = low(root_norm(hidden, feed_gain))
    gate = low_back(jnp.dot(normed_two, gate_weight, precision=highest))
    up_value = low_back(jnp.dot(normed_two, up_weight, precision=highest))
    mixed = low(jax.nn.silu(gate) * up_value)
    return hidden + low_back(jnp.dot(mixed, down_weight, precision=highest))

def reference(tokens, attention_gain, joint_weight, output_weight, feed_gain, gate_weight, up_weight, down_weight, cotangent, segment_lengths, parents):
    tables = tree_tables(segment_lengths, parents)
    index = jnp.arange(TOKENS, dtype=jnp.int32)
    key_hot, depth, segment = token_info(index, tables)
    reach = tables[2][segment.astype(jnp.int32)]
    cosines, sines = rotary_tables(depth)

    def layer(*weights):
        return forward(*weights, reach, key_hot, index, cosines, sines)
    inputs = (tokens, attention_gain, joint_weight, output_weight, feed_gain, gate_weight, up_weight, down_weight)
    inputs = tuple((value.astype(jnp.float32) for value in inputs))
    result, pullback = jax.vjp(layer, *inputs)
    grads = pullback(cotangent.astype(jnp.float32))
    return (result.astype(jnp.bfloat16), grads[0], grads[1], grads[2], grads[3], grads[4], grads[5], grads[6], grads[7])
```

```python
import functools

import jax
import jax.numpy as jnp
from jax import lax
from jax.experimental import pallas as pl
from jax.experimental.pallas import tpu as pltpu
from jax.sharding import Mesh
from jax.sharding import PartitionSpec as P

D = 1152
HEADS = 18
KV_HEADS = 6
HEAD_DIM = 64
REPEAT = HEADS // KV_HEADS
ATT = HEADS * HEAD_DIM
KEYS = KV_HEADS * HEAD_DIM

EPSILON = 1e-05
THETA = 10000.0
BIG = 2.0**30
LOG2E = 1.4426950408889634
KEY_BLOCK = 256
UNROLL = 8
BF16 = jnp.bfloat16
F32 = jnp.float32
NT = (((1,), (1,)), ((), ()))
NN = (((1,), (0,)), ((), ()))


def dg(a, b, dims):
    return lax.dot_general(a, b, dims, preferred_element_type=F32)


def tree_tables(segment_lengths, parents):
    count = segment_lengths.shape[0]
    labels = jnp.arange(count, dtype=jnp.int32)
    ends = jnp.sum(jnp.where(labels[None, :] <= labels[:, None], segment_lengths[None, :], 0), axis=1)
    starts = ends - segment_lengths
    parent_hot = parents[:, None] == labels[None, :]
    grand = jnp.sum(jnp.where(parent_hot, parents[None, :], 0), axis=1)
    self_mark = labels[:, None] == labels[None, :]
    grand_mark = grand[:, None] == labels[None, :]
    ancestry = (self_mark | parent_hot | grand_mark).astype(F32)
    strict = (parent_hot | grand_mark) & jnp.logical_not(self_mark)
    offsets = jnp.sum(jnp.where(strict, segment_lengths[None, :], 0), axis=1)
    return (ends, starts, ancestry, offsets)


def segment_hot(index, tables):
    ends, starts, _, _ = tables
    return (index[:, None] >= starts[None, :]) & (index[:, None] < ends[None, :])


def rotary_tables(index, tables):
    hot = segment_hot(index, tables)
    depth = index + jnp.sum(jnp.where(hot, (tables[3] - tables[1])[None, :], 0), axis=1)
    half = HEAD_DIM // 2
    rates = THETA ** (-jnp.arange(half, dtype=F32) / half)
    angles = depth.astype(F32)[:, None] * rates[None, :]
    return (jnp.cos(angles), jnp.sin(angles))


def turn(value, cosines, sines):
    half = value.shape[-1] // 2
    former, latter = (value[..., :half], value[..., half:])
    cos_part = cosines[:, None, :]
    sin_part = sines[:, None, :]
    return jnp.concatenate(
        [former * cos_part - latter * sin_part, latter * cos_part + former * sin_part], axis=-1
    )


def block_lists(first, blocks, block, total, tables):
    ends, starts, ancestry, _ = tables
    key_count = total // KEY_BLOCK
    low = first + jnp.arange(blocks, dtype=jnp.int32) * block
    high = low + block
    query_has = ((starts[None, :] < high[:, None]) & (ends[None, :] > low[:, None])).astype(F32)
    key_low = jnp.arange(key_count, dtype=jnp.int32) * KEY_BLOCK
    key_has = ((starts[None, :] < key_low[:, None] + KEY_BLOCK) & (ends[None, :] > key_low[:, None])).astype(F32)
    reach = jnp.sum(query_has[:, :, None] * ancestry[None], axis=1)
    seen = jnp.sum(reach[:, None, :] * key_has[None], axis=2) > 0.5
    seen = seen & (key_low[None, :] < high[:, None])
    labels = jnp.arange(key_count, dtype=jnp.int32)
    before = labels[None, :] < labels[:, None]
    rank = jnp.sum((seen[:, None, :] & before[None]).astype(jnp.int32), axis=2)
    place = seen[:, None, :] & (rank[:, None, :] == labels[None, :, None])
    lists = jnp.sum(jnp.where(place, labels[None, None, :], 0), axis=2)
    counts = jnp.sum(seen.astype(jnp.int32), axis=1) - 1
    return (lists.reshape(-1).astype(jnp.int32), counts.astype(jnp.int32))


def cascade(count, unroll, steps):
    def body(i, c):
        steps(i * unroll, unroll)
        return c

    whole = count // unroll
    lax.fori_loop(0, whole, body, 0)
    start = whole * unroll
    size = unroll // 2
    while size:
        some = ((count - start) // size) > 0
        pl.when(some)(functools.partial(steps, start, size))
        start = start + jnp.where(some, size, 0)
        size //= 2


def causal(scores, gap, heads):
    rows = gap + lax.broadcasted_iota(jnp.int32, scores.shape, 0)
    columns = lax.rem(lax.broadcasted_iota(jnp.int32, scores.shape, 1), scores.shape[1] // heads)
    return jnp.where(rows <= columns, scores, -BIG)


def left_half(shape):
    return lax.broadcasted_iota(jnp.int32, shape, 1) < HEAD_DIM


def forward_kernel(lists, counts, first, q_ref, kv_ref, mark_ref, o_ref, lse_ref, top_ref, sum_ref, vt_ref):
    block = pl.program_id(1)
    heads, rows = q_ref.shape[1], q_ref.shape[2]
    total = kv_ref.shape[1]
    stride = total // KEY_BLOCK
    place = first[0] + block * rows
    count = counts[block]

    @pl.when(block == 0)
    def _():
        def flip(i, c):
            k0 = pl.multiple_of(i * KEY_BLOCK, KEY_BLOCK)
            turned = kv_ref[0, pl.ds(k0, KEY_BLOCK), :].T
            vt_ref[:HEAD_DIM, pl.ds(k0, KEY_BLOCK)] = turned[HEAD_DIM:]
            return c

        lax.fori_loop(0, stride, flip, 0)
        tail = (vt_ref.shape[0] - HEAD_DIM, total)
        vt_ref[HEAD_DIM:] = jnp.where(lax.broadcasted_iota(jnp.int32, tail, 0) == 0, 1.0, 0.0).astype(BF16)

    def queries():
        return q_ref[0].reshape(heads * rows, 2 * HEAD_DIM)

    def blocks(start, n):
        offs = [pl.multiple_of(lists[block * stride + start + u] * KEY_BLOCK, KEY_BLOCK) for u in range(n)]
        kv = jnp.concatenate([kv_ref[0, pl.ds(k0, KEY_BLOCK), :] for k0 in offs], axis=0)
        mark = jnp.concatenate([mark_ref[pl.ds(k0, KEY_BLOCK), :] for k0 in offs], axis=0)
        vt = jnp.concatenate([vt_ref[:, pl.ds(k0, KEY_BLOCK)] for k0 in offs], axis=1)
        return offs, jnp.where(left_half(kv.shape), kv, mark), vt

    offs, k, vt = blocks(count, 1)
    scores = causal(dg(k, queries(), NT), offs[0] - place, heads)
    top = jnp.max(scores, axis=0, keepdims=True)
    top_ref[...] = top
    sum_ref[...] = dg(vt, jnp.exp2(scores - top).astype(BF16), NN)

    def steps(start, n):
        _, k, vt = blocks(start, n)
        weights = jnp.exp2(dg(k, queries(), NT) - top_ref[...]).astype(BF16)
        sum_ref[...] += dg(vt, weights, NN)

    cascade(count, UNROLL, steps)

    @pl.when(jnp.logical_not(jnp.max(sum_ref[HEAD_DIM : HEAD_DIM + 1, :]) < 2.0**100))
    def _():
        top_ref[...] = jnp.full(top_ref.shape, -4.0 * BIG, F32)
        sum_ref[...] = jnp.zeros(sum_ref.shape, F32)

        def online(n, c):
            offs, k, vt = blocks(n, 1)
            scores = causal(dg(k, queries(), NT), offs[0] - place, heads)
            old = top_ref[...]
            new = jnp.maximum(old, jnp.max(scores, axis=0, keepdims=True))
            top_ref[...] = new
            sum_ref[...] = sum_ref[...] * jnp.exp2(old - new) + dg(vt, jnp.exp2(scores - new).astype(BF16), NN)
            return c

        lax.fori_loop(0, count + 1, online, 0)

    total_row = sum_ref[HEAD_DIM : HEAD_DIM + 1, :]
    o_ref[0] = (sum_ref[:HEAD_DIM, :] / total_row).T.astype(BF16).reshape(heads, rows, HEAD_DIM)
    lse_ref[0, 0] = top_ref[...] + jnp.log2(total_row)


def attention_forward(lists, counts, first, q, kv, marks):
    groups, heads, tokens, wide = q.shape
    total = kv.shape[1]
    blocks = counts.shape[0]
    rows = tokens // blocks
    tall = HEAD_DIM + 16
    return pl.pallas_call(
        forward_kernel,
        grid_spec=pltpu.PrefetchScalarGridSpec(
            num_scalar_prefetch=3,
            grid=(groups, blocks),
            in_specs=[
                pl.BlockSpec((1, heads, rows, wide), lambda g, b, *_: (g, 0, b, 0)),
                pl.BlockSpec((1, total, wide), lambda g, b, *_: (g, 0, 0)),
                pl.BlockSpec((total, wide), lambda g, b, *_: (0, 0)),
            ],
            out_specs=[
                pl.BlockSpec((1, heads, rows, HEAD_DIM), lambda g, b, *_: (g, 0, b, 0)),
                pl.BlockSpec((1, 1, 1, heads * rows), lambda g, b, *_: (g, b, 0, 0)),
            ],
            scratch_shapes=[
                pltpu.VMEM((1, heads * rows), F32),
                pltpu.VMEM((tall, heads * rows), F32),
                pltpu.VMEM((tall, total), BF16),
            ],
        ),
        out_shape=[
            jax.ShapeDtypeStruct((groups, heads, tokens, HEAD_DIM), BF16),
            jax.ShapeDtypeStruct((groups, blocks, 1, heads * rows), F32),
        ],
        compiler_params=pltpu.CompilerParams(vmem_limit_bytes=48 * 2**20),
        cost_estimate=pl.CostEstimate(
            flops=groups * heads * tokens * total * 256, bytes_accessed=groups * total * 512, transcendentals=0
        ),
        name="attention_forward",
    )(lists, counts, first, q, kv, marks)


def backward_kernel(
    lists, counts, first, q_ref, do_ref, kv_ref, mark_ref, lse_ref, delta_ref, dq_ref, dkv_ref, dq_sum, dkv_sum, kt_ref
):
    block = pl.program_id(1)
    heads, rows = q_ref.shape[1], q_ref.shape[2]
    total = kv_ref.shape[1]
    stride = total // KEY_BLOCK
    place = first[0] + block * rows
    count = counts[block]

    @pl.when(block == 0)
    def _():
        dkv_sum[...] = jnp.zeros(dkv_sum.shape, F32)

        def flip(i, c):
            k0 = pl.multiple_of(i * KEY_BLOCK, KEY_BLOCK)
            turned = kv_ref[0, pl.ds(k0, KEY_BLOCK), :].T
            kt_ref[:, pl.ds(k0, KEY_BLOCK)] = turned[:HEAD_DIM]
            return c

        lax.fori_loop(0, stride, flip, 0)

    dq_sum[...] = jnp.zeros(dq_sum.shape, F32)

    def steps(start, n, masked):
        q = q_ref[0].reshape(heads * rows, 2 * HEAD_DIM)
        do = do_ref[0].reshape(heads * rows, 2 * HEAD_DIM)
        offs = [pl.multiple_of(lists[block * stride + start + u] * KEY_BLOCK, KEY_BLOCK) for u in range(n)]
        kv = jnp.concatenate([kv_ref[0, pl.ds(k0, KEY_BLOCK), :] for k0 in offs], axis=0)
        mark = jnp.concatenate([mark_ref[pl.ds(k0, KEY_BLOCK), :] for k0 in offs], axis=0)
        kt = jnp.concatenate([kt_ref[:, pl.ds(k0, KEY_BLOCK)] for k0 in offs], axis=1)
        scores = dg(jnp.where(left_half(kv.shape), kv, mark), q, NT) - lse_ref[0, 0]
        if masked:
            scores = causal(scores, offs[0] - place, heads)
        chances = jnp.exp2(scores)
        back = dg(kv, do, NT) - delta_ref[0, 0]
        score_back = (chances * back).astype(BF16)
        only_q = jnp.where(left_half(q.shape), q, jnp.zeros_like(q))
        update = dg(score_back, only_q, NN) + dg(chances.astype(BF16), do, NN)
        dq_sum[...] += dg(kt, score_back, NN)
        for u in range(n):
            dkv_sum[pl.ds(offs[u], KEY_BLOCK), :] += update[u * KEY_BLOCK : (u + 1) * KEY_BLOCK]

    steps(count, 1, True)
    cascade(count, UNROLL, lambda start, n: steps(start, n, False))
    dq_ref[0] = (dq_sum[...] * HEAD_DIM**-0.5).T.astype(BF16).reshape(heads, rows, HEAD_DIM)

    @pl.when(block == pl.num_programs(1) - 1)
    def _():
        summed = dkv_sum[...]
        dkv_ref[0] = jnp.where(left_half(summed.shape), summed * (1.0 / LOG2E), summed).astype(BF16)


def attention_backward(lists, counts, first, q, do, kv, marks, lse, delta):
    groups, heads, tokens, wide = q.shape
    total = kv.shape[1]
    blocks = counts.shape[0]
    rows = tokens // blocks
    return pl.pallas_call(
        backward_kernel,
        grid_spec=pltpu.PrefetchScalarGridSpec(
            num_scalar_prefetch=3,
            grid=(groups, blocks),
            in_specs=[
                pl.BlockSpec((1, heads, rows, wide), lambda g, b, *_: (g, 0, b, 0)),
                pl.BlockSpec((1, heads, rows, wide), lambda g, b, *_: (g, 0, b, 0)),
                pl.BlockSpec((1, total, wide), lambda g, b, *_: (g, 0, 0)),
                pl.BlockSpec((total, wide), lambda g, b, *_: (0, 0)),
                pl.BlockSpec((1, 1, 1, heads * rows), lambda g, b, *_: (g, b, 0, 0)),
                pl.BlockSpec((1, 1, 1, heads * rows), lambda g, b, *_: (g, b, 0, 0)),
            ],
            out_specs=[
                pl.BlockSpec((1, heads, rows, HEAD_DIM), lambda g, b, *_: (g, 0, b, 0)),
                pl.BlockSpec((1, total, wide), lambda g, b, *_: (g, 0, 0)),
            ],
            scratch_shapes=[
                pltpu.VMEM((HEAD_DIM, heads * rows), F32),
                pltpu.VMEM((total, wide), F32),
                pltpu.VMEM((HEAD_DIM, total), BF16),
            ],
        ),
        out_shape=[
            jax.ShapeDtypeStruct((groups, heads, tokens, HEAD_DIM), BF16),
            jax.ShapeDtypeStruct((groups, total, wide), BF16),
        ],
        compiler_params=pltpu.CompilerParams(vmem_limit_bytes=60 * 2**20),
        cost_estimate=pl.CostEstimate(
            flops=groups * heads * tokens * total * 640, bytes_accessed=groups * total * 1024, transcendentals=0
        ),
        name="attention_backward",
    )(lists, counts, first, q, do, kv, marks, lse, delta)


def norm_apply(value, gain):
    scale_rows = lax.rsqrt(jnp.sum(value * value, axis=1) / D + EPSILON)
    normed = (value * scale_rows[:, None] * gain[None, :]).astype(BF16)
    return (normed, scale_rows)


def norm_back(upstream, value, scale_rows, gain):
    weighted = upstream * gain[None, :]
    inner = jnp.sum(weighted * value, axis=1)
    value_back = (
        scale_rows[:, None] * weighted
        - value * (scale_rows * scale_rows * scale_rows * inner / D)[:, None]
    )
    gain_back = jnp.sum(upstream * value * scale_rows[:, None], axis=0)
    return (value_back, gain_back)


ROW = ("high", "core")
ALL_ROW = ("high", "core", "col")
ALL_COL = ("col", "high", "core")


def gather(value, axes):
    return lax.all_gather(value, axes, axis=0, tiled=True)


def scatter(value, axes):
    return lax.psum_scatter(value, axes, scatter_dimension=0, tiled=True)


def per_device(
    tokens,
    attention_gain,
    joint_weight,
    output_weight,
    feed_gain,
    gate_weight,
    up_weight,
    down_weight,
    cotangent,
    segment_lengths,
    parents,
):
    rows = lax.axis_size(ROW)
    columns = lax.axis_size("col")
    cores = lax.axis_size("core")
    total = tokens.shape[0] * columns
    own = tokens.shape[0] // rows
    held = own * cores
    groups = KV_HEADS // cores
    tables = tree_tables(segment_lengths, parents)
    row = lax.axis_index(ROW)
    column = lax.axis_index("col")
    index = column * tokens.shape[0] + row * own + jnp.arange(own, dtype=jnp.int32)
    cosines, sines = rotary_tables(index, tables)
    first = column * tokens.shape[0] + lax.axis_index("high") * held
    query_block = 256 if held % 256 == 0 else 128
    lists, counts = block_lists(first, held // query_block, query_block, total, tables)
    first = jnp.reshape(first, (1,)).astype(jnp.int32)
    key_hot = segment_hot(jnp.arange(total, dtype=jnp.int32), tables).astype(F32)
    marks = jnp.pad(key_hot, ((0, 0), (HEAD_DIM, HEAD_DIM - key_hot.shape[1]))).astype(BF16)
    held_hot = segment_hot(first[0] + jnp.arange(held, dtype=jnp.int32), tables).astype(F32)
    reach = jnp.sum(held_hot[:, :, None] * tables[2][None], axis=1)
    bars = jnp.pad((reach - 1.0) * BIG, ((0, 0), (0, HEAD_DIM - reach.shape[1]))).astype(BF16)

    def to_tokens(value):
        return lax.all_to_all(value, ROW, split_axis=0, concat_axis=1, tiled=True)

    def to_features(value):
        return lax.all_to_all(value, ROW, split_axis=1, concat_axis=0, tiled=True)

    def swap_cores(value):
        return lax.all_to_all(value, "core", split_axis=0, concat_axis=0, tiled=True)

    stream = to_tokens(tokens).astype(F32)
    gain_one = gather(attention_gain, ROW).astype(F32)
    gain_two = gather(feed_gain, ROW).astype(F32)
    joint_full = gather(joint_weight, ALL_COL).reshape(columns, D, -1)
    joint_full = joint_full.transpose(1, 0, 2).reshape(D, -1)

    normed_one, scale_one = norm_apply(stream, gain_one)
    joint = jnp.dot(normed_one, joint_full, preferred_element_type=F32).astype(BF16)
    raw = joint.astype(F32)
    queries = turn(raw[:, :ATT].reshape(own, HEADS, HEAD_DIM), cosines, sines)
    queries = (queries * (LOG2E * HEAD_DIM**-0.5)).astype(BF16).reshape(own, cores, -1)
    keys = turn(raw[:, ATT : ATT + KEYS].reshape(own, KV_HEADS, HEAD_DIM), cosines, sines).astype(BF16)
    values = joint[:, ATT + KEYS :].reshape(own, KV_HEADS, HEAD_DIM)
    pairs = jnp.concatenate([keys, values], axis=2).reshape(own, cores, -1)
    packed = jnp.concatenate([queries, pairs], axis=2).transpose(1, 0, 2)
    packed = swap_cores(packed).reshape(held, -1)
    wide = groups * REPEAT * HEAD_DIM
    queries = packed[:, :wide].reshape(held, groups, REPEAT, HEAD_DIM).transpose(1, 2, 0, 3)
    queries = jnp.concatenate([queries, jnp.broadcast_to(bars, queries.shape)], axis=3)
    pairs = packed[:, wide:].reshape(held, groups, 2 * HEAD_DIM)
    all_pairs = [gather(pairs[:, g], ("col", "high")) for g in range(groups)]
    results = [
        attention_forward(lists, counts, first, queries[g : g + 1], all_pairs[g][None], marks) for g in range(groups)
    ]
    attended = jnp.concatenate([r[0] for r in results], axis=0)
    lse = [r[1] for r in results]
    by_core = attended.reshape(groups * REPEAT, cores, own, HEAD_DIM).transpose(1, 2, 0, 3)
    attended_rows = swap_cores(by_core.reshape(cores, own, -1)).transpose(1, 0, 2).reshape(own, ATT)

    output_full = gather(output_weight, ALL_ROW).reshape(rows, ATT, -1)
    output_full = output_full.transpose(1, 0, 2).reshape(ATT, D)
    gate_full = gather(gate_weight, ALL_COL).reshape(columns, D, -1)
    up_full = gather(up_weight, ALL_COL).reshape(columns, D, -1)
    down_full = gather(down_weight, ALL_ROW).reshape(rows, -1, D // rows)
    down_full = down_full.transpose(1, 0, 2).reshape(-1, D)
    gate_full = gate_full.transpose(1, 0, 2).reshape(D, -1)
    up_full = up_full.transpose(1, 0, 2).reshape(D, -1)
    hidden = stream + jnp.dot(attended_rows, output_full, preferred_element_type=F32)
    normed_two, scale_two = norm_apply(hidden, gain_two)
    gate = jnp.dot(normed_two, gate_full, preferred_element_type=F32)
    up_value = jnp.dot(normed_two, up_full, preferred_element_type=F32)
    sigmoid = jax.nn.sigmoid(gate)
    mixed = (gate * sigmoid * up_value).astype(BF16)
    output = hidden + jnp.dot(mixed, down_full, preferred_element_type=F32)
    layer_output = to_features(output.astype(BF16))

    upstream = to_tokens(cotangent)
    mixed_back = dg(upstream, down_full, NT)
    gate_back = (mixed_back * up_value * (sigmoid * (1.0 + gate * (1.0 - sigmoid)))).astype(BF16)
    up_back = (mixed_back * gate * sigmoid).astype(BF16)

    def by_columns(left, right):
        part = lax.dot_general(left, right, (((0,), (0,)), ((), ())), preferred_element_type=F32).astype(BF16)
        part = part.reshape(part.shape[0], columns, -1).transpose(1, 0, 2)
        return scatter(part.reshape(-1, part.shape[2]), ALL_COL).astype(F32)

    def by_rows(left, right):
        part = lax.dot_general(left, right, (((0,), (0,)), ((), ())), preferred_element_type=F32).astype(BF16)
        part = part.reshape(part.shape[0], rows, -1).transpose(1, 0, 2)
        return scatter(part.reshape(-1, part.shape[2]), ALL_ROW).astype(F32)

    down_gradient = by_rows(mixed, upstream)
    gate_gradient = by_columns(normed_two, gate_back)
    up_gradient = by_columns(normed_two, up_back)
    normed_two_back = dg(gate_back, gate_full, NT) + dg(up_back, up_full, NT)
    hidden_part, gain_two_part = norm_back(normed_two_back, hidden, scale_two, gain_two)
    hidden_back = upstream.astype(F32) + hidden_part
    hidden_low = hidden_back.astype(BF16)
    attended_back = dg(hidden_low, output_full, NT).astype(BF16)
    output_gradient = by_rows(attended_rows, hidden_low)

    heads_back = swap_cores(attended_back.reshape(own, cores, -1).transpose(1, 0, 2)).reshape(held, -1)
    heads_back = heads_back.reshape(held, groups, REPEAT, HEAD_DIM).transpose(1, 2, 0, 3)
    delta = jnp.sum(heads_back.astype(F32) * attended.astype(F32), axis=3)
    delta = delta.reshape(groups, REPEAT, -1, query_block).transpose(0, 2, 1, 3)
    delta = delta.reshape(groups, -1, 1, REPEAT * query_block)
    heads_back = jnp.pad(heads_back, ((0, 0), (0, 0), (0, 0), (HEAD_DIM, 0)))
    backs = [
        attention_backward(
            lists,
            counts,
            first,
            queries[g : g + 1],
            heads_back[g : g + 1],
            all_pairs[g][None],
            marks,
            lse[g],
            delta[g : g + 1],
        )
        for g in range(groups)
    ]
    query_back = jnp.concatenate([b[0] for b in backs], axis=0)
    query_back = query_back.reshape(groups * REPEAT, held, HEAD_DIM).transpose(1, 0, 2).reshape(held, -1)
    pair_back = [scatter(b[1][0], ("col", "high")) for b in backs]
    packed = jnp.concatenate([query_back, *pair_back], axis=1).reshape(cores, own, -1)
    packed = swap_cores(packed)
    query_back = packed[:, :, :wide].transpose(1, 0, 2).reshape(own, HEADS, HEAD_DIM)
    pair_back = packed[:, :, wide:].transpose(1, 0, 2).reshape(own, KV_HEADS, 2 * HEAD_DIM)
    query_back = turn(query_back.astype(F32), cosines, -sines).astype(BF16).reshape(own, ATT)
    key_back = turn(pair_back[:, :, :HEAD_DIM].astype(F32), cosines, -sines).astype(BF16).reshape(own, KEYS)
    value_back = pair_back[:, :, HEAD_DIM:].reshape(own, KEYS)
    joint_back = jnp.concatenate([query_back, key_back, value_back], axis=1)
    normed_one_back = dg(joint_back, joint_full, NT)
    joint_gradient = by_columns(normed_one, joint_back)
    stream_part, gain_one_part = norm_back(normed_one_back, stream, scale_one, gain_one)
    input_gradient = to_features((hidden_back + stream_part).astype(BF16)).astype(F32)
    gains = lax.psum(jnp.stack([gain_one_part, gain_two_part]), ALL_COL)
    gains = lax.dynamic_slice_in_dim(gains, row * (D // rows), D // rows, 1)
    return (
        layer_output,
        input_gradient,
        gains[0],
        joint_gradient,
        output_gradient,
        gains[1],
        gate_gradient,
        up_gradient,
        down_gradient,
    )


def solution(mesh):
    leaves, rows, columns = (mesh.shape[name] for name in ("leaf", "row", "col"))
    split = Mesh(mesh.devices.reshape(leaves, rows // 2, 2, columns), ("leaf", "high", "core", "col"))
    return jax.shard_map(
        per_device,
        mesh=split,
        in_specs=(
            P(("leaf", "col"), ROW),
            P(ROW),
            P(ROW, "col"),
            P("col", ROW),
            P(ROW),
            P(ROW, "col"),
            P(ROW, "col"),
            P("col", ROW),
            P(("leaf", "col"), ROW),
            P("leaf"),
            P("leaf"),
        ),
        out_specs=(
            P(("leaf", "col"), ROW),
            P(("leaf", "col"), ROW),
            P(("leaf", *ROW)),
            P(("leaf", *ROW), "col"),
            P(("leaf", "col"), ROW),
            P(("leaf", *ROW)),
            P(("leaf", *ROW), "col"),
            P(("leaf", *ROW), "col"),
            P(("leaf", "col"), ROW),
        ),
        check_vma=False,
    )
```

```python
import functools

import jax
import jax.numpy as jnp
from jax import lax
from jax.experimental import pallas as pl
from jax.experimental.pallas import tpu as pltpu
from jax.sharding import Mesh
from jax.sharding import PartitionSpec as P

D = 1152
HEADS = 18
KV_HEADS = 6
HEAD_DIM = 64
REPEAT = HEADS // KV_HEADS
ATT = HEADS * HEAD_DIM
KEYS = KV_HEADS * HEAD_DIM

EPSILON = 1e-05
THETA = 10000.0
BIG = 2.0**30
LOG2E = 1.4426950408889634
UNROLL = 8
BF16 = jnp.bfloat16
F32 = jnp.float32
NT = (((1,), (1,)), ((), ()))
NN = (((1,), (0,)), ((), ()))


def dg(a, b, dims):
    return lax.dot_general(a, b, dims, preferred_element_type=F32)


def tree_tables(segment_lengths, parents):
    count = segment_lengths.shape[0]
    labels = jnp.arange(count, dtype=jnp.int32)
    ends = jnp.sum(jnp.where(labels[None, :] <= labels[:, None], segment_lengths[None, :], 0), axis=1)
    starts = ends - segment_lengths
    parent_hot = parents[:, None] == labels[None, :]
    grand = jnp.sum(jnp.where(parent_hot, parents[None, :], 0), axis=1)
    self_mark = labels[:, None] == labels[None, :]
    grand_mark = grand[:, None] == labels[None, :]
    ancestry = (self_mark | parent_hot | grand_mark).astype(F32)
    strict = (parent_hot | grand_mark) & jnp.logical_not(self_mark)
    offsets = jnp.sum(jnp.where(strict, segment_lengths[None, :], 0), axis=1)
    return (ends, starts, ancestry, offsets)


def segment_hot(index, tables):
    ends, starts, _, _ = tables
    return (index[:, None] >= starts[None, :]) & (index[:, None] < ends[None, :])


def rotary_tables(index, tables):
    hot = segment_hot(index, tables)
    depth = index + jnp.sum(jnp.where(hot, (tables[3] - tables[1])[None, :], 0), axis=1)
    half = HEAD_DIM // 2
    rates = THETA ** (-jnp.arange(half, dtype=F32) / half)
    angles = depth.astype(F32)[:, None] * rates[None, :]
    return (jnp.cos(angles), jnp.sin(angles))


def turn(value, cosines, sines):
    half = value.shape[-1] // 2
    former, latter = (value[..., :half], value[..., half:])
    cos_part = cosines[:, None, :]
    sin_part = sines[:, None, :]
    return jnp.concatenate(
        [former * cos_part - latter * sin_part, latter * cos_part + former * sin_part], axis=-1
    )


def block_lists(first, key_index, block, held, tables):
    ends, starts, ancestry, _ = tables
    blocks = held // block
    key_low = key_index[::block]
    labels = jnp.arange(key_low.shape[0], dtype=jnp.int32)
    low = first + jnp.arange(blocks, dtype=jnp.int32) * block
    high = low + block
    query_has = ((starts[None, :] < high[:, None]) & (ends[None, :] > low[:, None])).astype(F32)
    key_has = ((starts[None, :] < key_low[:, None] + block) & (ends[None, :] > key_low[:, None])).astype(F32)
    reach = jnp.sum(query_has[:, :, None] * ancestry[None], axis=1)
    seen = jnp.sum(reach[:, None, :] * key_has[None], axis=2) > 0.5
    seen = seen & (key_low[None, :] < low[:, None])
    before = labels[None, :] < labels[:, None]
    rank = jnp.sum((seen[:, None, :] & before[None]).astype(jnp.int32), axis=2)
    place = seen[:, None, :] & (rank[:, None, :] == labels[None, :, None])
    lists = jnp.sum(jnp.where(place, labels[None, None, :], 0), axis=2)
    counts = jnp.sum(seen.astype(jnp.int32), axis=1)
    own = jnp.sum(jnp.where(key_low[None, :] == low[:, None], labels[None, :], 0), axis=1)
    lists = jnp.where(labels[None, :] == counts[:, None], own[:, None], lists)
    return (lists.reshape(-1).astype(jnp.int32), counts.astype(jnp.int32))


def cascade(count, unroll, steps):
    def body(i, c):
        steps(i * unroll, unroll)
        return c

    whole = count // unroll
    lax.fori_loop(0, whole, body, 0)
    start = whole * unroll
    size = unroll // 2
    while size:
        some = ((count - start) // size) > 0
        pl.when(some)(functools.partial(steps, start, size))
        start = start + jnp.where(some, size, 0)
        size //= 2


def causal(scores, heads):
    rows = lax.broadcasted_iota(jnp.int32, scores.shape, 0)
    columns = lax.rem(lax.broadcasted_iota(jnp.int32, scores.shape, 1), scores.shape[1] // heads)
    return jnp.where(rows <= columns, scores, -BIG)


def left_half(shape):
    return lax.broadcasted_iota(jnp.int32, shape, 1) < HEAD_DIM


def fetch(pieces, group, kv_ref, sems):
    copies, start = [], 0
    for i, piece in enumerate(pieces):
        lanes = pl.ds(pl.multiple_of(group * 2 * HEAD_DIM, 2 * HEAD_DIM), 2 * HEAD_DIM)
        target = kv_ref.at[pl.ds(start, piece.shape[0])]
        copies.append(pltpu.make_async_copy(piece.at[:, lanes], target, sems.at[i]))
        start += piece.shape[0]
    for copy in copies:
        copy.start()
    for copy in copies:
        copy.wait()


def forward_kernel(lists, counts, q_ref, mark_ref, *refs):
    *pieces, o_ref, lse_ref, top_ref, sum_ref, kv_ref, vt_ref, sems = refs
    block = pl.program_id(1)
    heads, rows = q_ref.shape[1], q_ref.shape[2]
    total = kv_ref.shape[0]
    stride = total // rows
    count = counts[block]

    @pl.when(block == 0)
    def _():
        fetch(pieces, pl.program_id(0), kv_ref, sems)

        def flip(i, c):
            k0 = pl.multiple_of(i * rows, rows)
            turned = kv_ref[pl.ds(k0, rows), :].T
            vt_ref[:HEAD_DIM, pl.ds(k0, rows)] = turned[HEAD_DIM:]
            return c

        lax.fori_loop(0, stride, flip, 0)
        tail = (vt_ref.shape[0] - HEAD_DIM, total)
        vt_ref[HEAD_DIM:] = jnp.where(lax.broadcasted_iota(jnp.int32, tail, 0) == 0, 1.0, 0.0).astype(BF16)

    def queries():
        return q_ref[0].reshape(heads * rows, 2 * HEAD_DIM)

    def blocks(start, n):
        offs = [pl.multiple_of(lists[block * stride + start + u] * rows, rows) for u in range(n)]
        kv = jnp.concatenate([kv_ref[pl.ds(k0, rows), :] for k0 in offs], axis=0)
        mark = jnp.concatenate([mark_ref[pl.ds(k0, rows), :] for k0 in offs], axis=0)
        vt = jnp.concatenate([vt_ref[:, pl.ds(k0, rows)] for k0 in offs], axis=1)
        return jnp.where(left_half(kv.shape), kv, mark), vt

    def begin():
        k, vt = blocks(count, 1)
        scores = causal(dg(k, queries(), NT), heads)
        top = jnp.max(scores, axis=0, keepdims=True)
        top_ref[...] = top
        sum_ref[...] = dg(vt, jnp.exp2(scores - top).astype(BF16), NN)

    def steps(start, n):
        k, vt = blocks(start, n)
        weights = jnp.exp2(dg(k, queries(), NT) - top_ref[...]).astype(BF16)
        sum_ref[...] += dg(vt, weights, NN)

    begin()
    cascade(count, UNROLL, steps)

    @pl.when(jnp.logical_not(jnp.max(sum_ref[HEAD_DIM : HEAD_DIM + 1, :]) < 2.0**100))
    def _():
        begin()

        def online(n, c):
            k, vt = blocks(n, 1)
            scores = dg(k, queries(), NT)
            old = top_ref[...]
            new = jnp.maximum(old, jnp.max(scores, axis=0, keepdims=True))
            top_ref[...] = new
            sum_ref[...] = sum_ref[...] * jnp.exp2(old - new) + dg(vt, jnp.exp2(scores - new).astype(BF16), NN)
            return c

        lax.fori_loop(0, count, online, 0)

    total_row = sum_ref[HEAD_DIM : HEAD_DIM + 1, :]
    o_ref[0] = (sum_ref[:HEAD_DIM, :] / total_row).T.astype(BF16).reshape(heads, rows, HEAD_DIM)
    lse_ref[0, 0] = top_ref[...] + jnp.log2(total_row)


def attention_forward(lists, counts, q, pieces, marks):
    groups, heads, tokens, wide = q.shape
    total = marks.shape[0]
    blocks = counts.shape[0]
    rows = tokens // blocks
    tall = HEAD_DIM + 16
    return pl.pallas_call(
        forward_kernel,
        grid_spec=pltpu.PrefetchScalarGridSpec(
            num_scalar_prefetch=2,
            grid=(groups, blocks),
            in_specs=[
                pl.BlockSpec((1, heads, rows, wide), lambda g, b, *_: (g, 0, b, 0)),
                pl.BlockSpec((total, wide), lambda g, b, *_: (0, 0)),
                *(pl.BlockSpec(memory_space=pl.ANY) for _ in pieces),
            ],
            out_specs=[
                pl.BlockSpec((1, heads, rows, HEAD_DIM), lambda g, b, *_: (g, 0, b, 0)),
                pl.BlockSpec((1, 1, 1, heads * rows), lambda g, b, *_: (g, b, 0, 0)),
            ],
            scratch_shapes=[
                pltpu.VMEM((1, heads * rows), F32),
                pltpu.VMEM((tall, heads * rows), F32),
                pltpu.VMEM((total, wide), BF16),
                pltpu.VMEM((tall, total), BF16),
                pltpu.SemaphoreType.DMA((len(pieces),)),
            ],
        ),
        out_shape=[
            jax.ShapeDtypeStruct((groups, heads, tokens, HEAD_DIM), BF16),
            jax.ShapeDtypeStruct((groups, blocks, 1, heads * rows), F32),
        ],
        compiler_params=pltpu.CompilerParams(vmem_limit_bytes=48 * 2**20),
        cost_estimate=pl.CostEstimate(
            flops=groups * heads * tokens * total * 256, bytes_accessed=groups * total * 512, transcendentals=0
        ),
        name="attention_forward",
    )(lists, counts, q, marks, *pieces)


def backward_kernel(group, lists, counts, q_ref, do_ref, mark_ref, lse_ref, delta_ref, *refs):
    *pieces, dq_ref, dkv_ref, dq_sum, dkv_sum, kv_ref, kt_ref, sems = refs
    block = pl.program_id(0)
    heads, rows = q_ref.shape[1], q_ref.shape[2]
    total = kv_ref.shape[0]
    stride = total // rows
    count = counts[block]

    @pl.when(block == 0)
    def _():
        dkv_sum[...] = jnp.zeros(dkv_sum.shape, F32)
        fetch(pieces, group, kv_ref, sems)

        def flip(i, c):
            k0 = pl.multiple_of(i * rows, rows)
            turned = kv_ref[pl.ds(k0, rows), :].T
            kt_ref[:, pl.ds(k0, rows)] = turned[:HEAD_DIM]
            return c

        lax.fori_loop(0, stride, flip, 0)

    dq_sum[...] = jnp.zeros(dq_sum.shape, F32)

    def steps(start, n, masked):
        q = q_ref[0].reshape(heads * rows, 2 * HEAD_DIM)
        do = do_ref[0].reshape(heads * rows, 2 * HEAD_DIM)
        offs = [pl.multiple_of(lists[block * stride + start + u] * rows, rows) for u in range(n)]
        kv = jnp.concatenate([kv_ref[pl.ds(k0, rows), :] for k0 in offs], axis=0)
        mark = jnp.concatenate([mark_ref[pl.ds(k0, rows), :] for k0 in offs], axis=0)
        kt = jnp.concatenate([kt_ref[:, pl.ds(k0, rows)] for k0 in offs], axis=1)
        scores = dg(jnp.where(left_half(kv.shape), kv, mark), q, NT) - lse_ref[0, 0]
        if masked:
            scores = causal(scores, heads)
        chances = jnp.exp2(scores)
        back = dg(kv, do, NT) - delta_ref[0, 0]
        score_back = (chances * back).astype(BF16)
        only_q = jnp.where(left_half(q.shape), q, jnp.zeros_like(q))
        update = dg(score_back, only_q, NN) + dg(chances.astype(BF16), do, NN)
        dq_sum[...] += dg(kt, score_back, NN)
        for u in range(n):
            dkv_sum[pl.ds(offs[u], rows), :] += update[u * rows : (u + 1) * rows]

    steps(count, 1, True)
    cascade(count, UNROLL, lambda start, n: steps(start, n, False))
    dq_ref[0] = (dq_sum[...] * HEAD_DIM**-0.5).T.astype(BF16).reshape(heads, rows, HEAD_DIM)

    @pl.when(block == pl.num_programs(0) - 1)
    def _():
        summed = dkv_sum[...]
        dkv_ref[...] = jnp.where(left_half(summed.shape), summed * (1.0 / LOG2E), summed).astype(BF16)


def attention_backward(group, lists, counts, q, do, pieces, marks, lse, delta):
    _, heads, tokens, wide = q.shape
    total = marks.shape[0]
    blocks = counts.shape[0]
    rows = tokens // blocks
    return pl.pallas_call(
        functools.partial(backward_kernel, group),
        grid_spec=pltpu.PrefetchScalarGridSpec(
            num_scalar_prefetch=2,
            grid=(blocks,),
            in_specs=[
                pl.BlockSpec((1, heads, rows, wide), lambda b, *_: (group, 0, b, 0)),
                pl.BlockSpec((1, heads, rows, wide), lambda b, *_: (group, 0, b, 0)),
                pl.BlockSpec((total, wide), lambda b, *_: (0, 0)),
                pl.BlockSpec((1, 1, 1, heads * rows), lambda b, *_: (group, b, 0, 0)),
                pl.BlockSpec((1, 1, 1, heads * rows), lambda b, *_: (group, b, 0, 0)),
                *(pl.BlockSpec(memory_space=pl.ANY) for _ in pieces),
            ],
            out_specs=[
                pl.BlockSpec((1, heads, rows, HEAD_DIM), lambda b, *_: (0, 0, b, 0)),
                pl.BlockSpec((total, wide), lambda b, *_: (0, 0)),
            ],
            scratch_shapes=[
                pltpu.VMEM((HEAD_DIM, heads * rows), F32),
                pltpu.VMEM((total, wide), F32),
                pltpu.VMEM((total, wide), BF16),
                pltpu.VMEM((HEAD_DIM, total), BF16),
                pltpu.SemaphoreType.DMA((len(pieces),)),
            ],
        ),
        out_shape=[
            jax.ShapeDtypeStruct((1, heads, tokens, HEAD_DIM), BF16),
            jax.ShapeDtypeStruct((total, wide), BF16),
        ],
        compiler_params=pltpu.CompilerParams(vmem_limit_bytes=60 * 2**20),
        cost_estimate=pl.CostEstimate(flops=heads * tokens * total * 640, bytes_accessed=total * 1024, transcendentals=0),
        name="attention_backward",
    )(lists, counts, q, do, marks, lse, delta, *pieces)


def feed_kernel(normed_ref, back_ref, gate_ref, up_ref, down_ref, mixed_ref, gate_back_ref, up_back_ref, out_ref, normed_back_ref):
    @pl.when((pl.program_id(0) == 0) & (pl.program_id(1) == 0))
    def _():
        out_ref[...] = jnp.zeros(out_ref.shape, F32)
        normed_back_ref[...] = jnp.zeros(normed_back_ref.shape, F32)

    gate = dg(normed_ref[...], gate_ref[0], NN)
    up_value = dg(normed_ref[...], up_ref[0], NN)
    mixed_back = dg(back_ref[...], down_ref[0], NN)
    sigmoid = jax.nn.sigmoid(gate)
    silu = gate * sigmoid
    mixed = (silu * up_value).astype(BF16)
    gate_back = (mixed_back * up_value * (sigmoid * (1.0 + gate * (1.0 - sigmoid)))).astype(BF16)
    up_back = (mixed_back * silu).astype(BF16)
    mixed_ref[...] = mixed
    gate_back_ref[...] = gate_back
    up_back_ref[...] = up_back
    out_ref[...] += dg(mixed, down_ref[0], NT)
    normed_back_ref[...] += dg(gate_back, gate_ref[0], NT) + dg(up_back, up_ref[0], NT)


def feed_forward(normed, back, pair, down):
    tokens = normed.shape[0]
    columns, _, width = down.shape
    parts = 2 if width % 256 == 0 else 1
    part = width // parts
    whole = pl.BlockSpec((tokens, D), lambda c, j: (0, 0))
    block = pl.BlockSpec((1, D, part), lambda c, j: (c, 0, j))
    out = pl.BlockSpec((tokens, part), lambda c, j: (0, c * parts + j))
    return pl.pallas_call(
        feed_kernel,
        grid=(columns, parts),
        in_specs=[whole, whole, block, pl.BlockSpec((1, D, part), lambda c, j: (c, 0, j + parts)), block],
        out_specs=[out, out, out, whole, whole],
        out_shape=[jax.ShapeDtypeStruct((tokens, columns * width), BF16)] * 3 + [jax.ShapeDtypeStruct((tokens, D), F32)] * 2,
        compiler_params=pltpu.CompilerParams(vmem_limit_bytes=56 * 2**20),
        cost_estimate=pl.CostEstimate(
            flops=12 * tokens * D * columns * width, bytes_accessed=6 * D * columns * width, transcendentals=0
        ),
        name="feed_forward",
    )(normed, back, pair, pair, down)


def gradient_kernel(rights, summed, order, left_ref, *refs):
    right_refs, refs = refs[:rights], refs[rights:]
    sums_ref = refs[0] if summed else None
    refs = refs[1:] if summed else refs
    (mine_ref, other_ref), (lefts, *held) = refs[:2], refs[2:]
    step = pl.program_id(0)
    features = lefts.shape[2]

    @pl.when(step == 0)
    def _():
        for r in range(lefts.shape[0]):
            lefts[r] = left_ref[:, r * features : (r + 1) * features]
        if held:
            width = held[0].shape[2]
            for c in range(held[0].shape[0]):
                held[0][c] = right_refs[0][:, c * width : (c + 1) * width]

    steps = pl.num_programs(0)
    column, row, core = order[step], order[steps + step] * 2, order[2 * steps]
    start = 0
    for right in right_refs:
        value = held[0][column] if held else right[...]
        width = value.shape[1]
        for target, r in ((mine_ref, row + core), (other_ref, row + 1 - core)):
            part = lax.dot_general(lefts[r], value, (((0,), (0,)), ((), ())), preferred_element_type=F32)
            target[0, :features, start : start + width] = part.astype(BF16)
        start += width
    if sums_ref is not None:
        for target, r in ((mine_ref, row + core), (other_ref, row + 1 - core)):
            target[0, features:, :] = sums_ref[r].astype(BF16)


def gradient_parts(order, left, *rights, sums=None):
    tokens = left.shape[0]
    steps = (order.shape[0] - 1) // 2
    columns = steps // 2
    width = rights[0].shape[1] // columns
    features = left.shape[1] // 4
    aligned = width % 128 == 0
    if aligned:
        right_spec = pl.BlockSpec((tokens, width), lambda s, order: (0, order[s]))
    else:
        right_spec = pl.BlockSpec(rights[0].shape, lambda s, order: (0, 0))
    wide = width * len(rights)
    tall = features if sums is None else features + 16
    out = pl.BlockSpec((1, tall, wide), lambda s, order: (s, 0, 0))
    shape = jax.ShapeDtypeStruct((steps, tall, wide), BF16)
    held = [] if aligned else [pltpu.VMEM((columns, tokens, width), BF16)]
    more, more_specs = [], []
    if sums is not None:
        lines = -(-features // wide)
        more = [jnp.pad(sums.reshape(4, lines, -1), ((0, 0), (0, 16 - lines), (0, wide - features // lines)))]
        more_specs = [pl.BlockSpec((4, 16, wide), lambda s, order: (0, 0, 0))]
    return pl.pallas_call(
        functools.partial(gradient_kernel, len(rights), sums is not None),
        grid_spec=pltpu.PrefetchScalarGridSpec(
            num_scalar_prefetch=1,
            grid=(steps,),
            in_specs=[
                pl.BlockSpec(left.shape, lambda s, order: (0, 0)),
                *(right_spec for _ in rights),
                *more_specs,
            ],
            out_specs=[out, out],
            scratch_shapes=[pltpu.VMEM((4, tokens, features), BF16), *held],
        ),
        out_shape=[shape, shape],
        compiler_params=pltpu.CompilerParams(vmem_limit_bytes=56 * 2**20),
        cost_estimate=pl.CostEstimate(
            flops=2 * tokens * left.shape[1] * wide * columns, bytes_accessed=2 * left.shape[1] * wide * columns, transcendentals=0
        ),
        name="gradient_parts",
    )(order, left, *rights, *more)


def norm_apply(value, gain):
    scale_rows = lax.rsqrt(jnp.sum(value * value, axis=1) / D + EPSILON)
    normed = (value * scale_rows[:, None] * gain[None, :]).astype(BF16)
    return (normed, scale_rows)


def norm_back(upstream, value, scale_rows, gain):
    weighted = upstream * gain[None, :]
    inner = jnp.sum(weighted * value, axis=1)
    value_back = (
        scale_rows[:, None] * weighted
        - value * (scale_rows * scale_rows * scale_rows * inner / D)[:, None]
    )
    gain_back = jnp.sum(upstream * value * scale_rows[:, None], axis=0)
    return (value_back, gain_back)


ROW = ("high", "core")
ALL_ROW = ("high", "core", "col")
ALL_COL = ("col", "high", "core")
RING = ("high", "col")


def ring_steps(columns):
    path = [*range(columns), *reversed(range(columns, 2 * columns))]
    ahead = [(path[i], path[(i + 1) % len(path)]) for i in range(len(path))]
    return ahead, [(b, a) for a, b in ahead]


def ring_gather(value, columns):
    ahead, behind = ring_steps(columns)
    count = 2 * columns
    to_next, to_last = value, value
    fronts, backs = [], []
    for _ in range(count // 2 - 1):
        to_next = lax.ppermute(to_next, RING, ahead)
        to_last = lax.ppermute(to_last, RING, behind)
        fronts.append(to_next)
        backs.append(to_last)
    half = value.shape[0] // 2
    upper = lax.ppermute(to_next[:half], RING, ahead)
    lower = lax.ppermute(to_last[half:], RING, behind)
    return [value, *backs, upper, lower, *reversed(fronts)]


class RingScatter:
    def __init__(self, part, columns):
        self.part, (self.ahead, self.behind), self.count = part, ring_steps(columns), 2 * columns
        self.left = self.count // 2
        self.send(part(self.left, 0), part(self.left, 1))

    def send(self, out, back):
        out, back = lax.optimization_barrier((out.astype(BF16), back.astype(BF16)))
        self.arrived = (lax.ppermute(out, RING, self.ahead), lax.ppermute(back, RING, self.behind))
        self.left -= 1

    def step(self):
        out, back = self.part(self.left, None), self.part(self.count - self.left, None)
        front, rear = (v.astype(F32) for v in self.arrived)
        if front.shape[0] == out.shape[0]:
            self.send(out + front, back + rear)
        else:
            half = front.shape[0]
            out = jnp.concatenate([out[:half] + front, out[half:]], axis=0)
            self.send(out, jnp.concatenate([back[:half], back[half:] + rear], axis=0))

    def finish(self):
        while self.left:
            self.step()
        return self.part(0, None) + self.arrived[0].astype(F32) + self.arrived[1].astype(F32)


def after(value, rings):
    value, arrived = lax.optimization_barrier((value, [r.arrived for r in rings]))
    for ring, a in zip(rings, arrived, strict=True):
        ring.arrived = a
    return value


def halves(value, half):
    if half is None:
        return value
    middle = value.shape[0] // 2
    return value[middle:] if half else value[:middle]


def gather(value, axes):
    return lax.all_gather(value, axes, axis=0, tiled=True)


def per_device(
    tokens,
    attention_gain,
    joint_weight,
    output_weight,
    feed_gain,
    gate_weight,
    up_weight,
    down_weight,
    cotangent,
    segment_lengths,
    parents,
):
    rows = lax.axis_size(ROW)
    columns = lax.axis_size("col")
    cores = lax.axis_size("core")
    own = tokens.shape[0] // rows
    held = own * cores
    groups = KV_HEADS // cores
    tables = tree_tables(segment_lengths, parents)
    row = lax.axis_index(ROW)
    column = lax.axis_index("col")
    high = lax.axis_index("high")
    core = lax.axis_index("core")
    index = column * tokens.shape[0] + row * own + jnp.arange(own, dtype=jnp.int32)
    cosines, sines = rotary_tables(index, tables)
    first = column * tokens.shape[0] + high * held

    spot = jnp.where(high == 0, column, 2 * columns - 1 - column)
    spots = lax.rem(spot + jnp.arange(2 * columns, dtype=jnp.int32), 2 * columns)
    far = spots >= columns
    ring_column = jnp.where(far, 2 * columns - 1 - spots, spots)
    ring_high = far.astype(jnp.int32)
    order = jnp.concatenate([ring_column, ring_high, jnp.reshape(core, (1,))]).astype(jnp.int32)
    key_first = ring_column * tokens.shape[0] + ring_high * held
    key_index = (key_first[:, None] + jnp.arange(held, dtype=jnp.int32)[None, :]).reshape(-1)

    block = 256 if held % 256 == 0 else 128
    lists, counts = block_lists(first, key_index, block, held, tables)
    key_hot = segment_hot(key_index, tables).astype(F32)
    marks = jnp.pad(key_hot, ((0, 0), (HEAD_DIM, HEAD_DIM - key_hot.shape[1]))).astype(BF16)
    held_hot = segment_hot(first + jnp.arange(held, dtype=jnp.int32), tables).astype(F32)
    reach = jnp.sum(held_hot[:, :, None] * tables[2][None], axis=1)
    bars = jnp.pad((reach - 1.0) * BIG, ((0, 0), (0, HEAD_DIM - reach.shape[1]))).astype(BF16)

    def to_tokens(value):
        return lax.all_to_all(value, ROW, split_axis=0, concat_axis=1, tiled=True)

    def to_features(value):
        return lax.all_to_all(value, ROW, split_axis=1, concat_axis=0, tiled=True)

    def swap_cores(value):
        return lax.all_to_all(value, "core", split_axis=0, concat_axis=0, tiled=True)

    joint_full = gather(joint_weight, ALL_COL).reshape(columns, D, -1)
    joint_full = joint_full.transpose(1, 0, 2).reshape(D, -1)
    gains = jnp.broadcast_to(jnp.stack([attention_gain, feed_gain])[None], (rows, 2, attention_gain.shape[0]))
    extended = jnp.concatenate([tokens.reshape(rows, own, -1), jnp.pad(gains, ((0, 0), (0, 14), (0, 0)))], axis=1)
    extended = to_tokens(extended.reshape(rows * (own + 16), -1))
    stream = extended[:own].astype(F32)
    gain_one = extended[own].astype(F32)
    gain_two = extended[own + 1].astype(F32)

    normed_one, scale_one = norm_apply(stream, gain_one)
    joint = jnp.dot(normed_one, joint_full, preferred_element_type=F32).astype(BF16)
    raw = joint.astype(F32)
    queries = turn(raw[:, :ATT].reshape(own, HEADS, HEAD_DIM), cosines, sines)
    queries = (queries * (LOG2E * HEAD_DIM**-0.5)).astype(BF16).reshape(own, cores, -1)
    keys = turn(raw[:, ATT : ATT + KEYS].reshape(own, KV_HEADS, HEAD_DIM), cosines, sines).astype(BF16)
    values = joint[:, ATT + KEYS :].reshape(own, KV_HEADS, HEAD_DIM)
    pairs = jnp.concatenate([keys, values], axis=2).reshape(own, cores, -1)
    packed = jnp.concatenate([queries, pairs], axis=2).transpose(1, 0, 2)
    packed = swap_cores(packed).reshape(held, -1)
    wide = groups * REPEAT * HEAD_DIM
    pieces = ring_gather(packed[:, wide:], columns)
    queries = packed[:, :wide].reshape(held, groups, REPEAT, HEAD_DIM).transpose(1, 2, 0, 3)
    queries = jnp.concatenate([queries, jnp.broadcast_to(bars, queries.shape)], axis=3)
    attended, lse = attention_forward(lists, counts, queries, pieces, marks)
    by_core = attended.reshape(groups * REPEAT, cores, own, HEAD_DIM).transpose(1, 2, 0, 3)
    attended_rows = swap_cores(by_core.reshape(cores, own, -1)).transpose(1, 0, 2).reshape(own, ATT)

    output_full = gather(output_weight, ALL_ROW).reshape(rows, ATT, -1)
    output_full = output_full.transpose(1, 0, 2).reshape(ATT, D)
    pair_full = gather(jnp.concatenate([gate_weight, up_weight], axis=1), ALL_COL).reshape(columns, D, -1)
    down_full = gather(down_weight.T, ALL_COL).reshape(columns, D, -1)
    upstream = to_tokens(cotangent)
    hidden = stream + jnp.dot(attended_rows, output_full, preferred_element_type=F32)
    normed_two, scale_two = norm_apply(hidden, gain_two)
    mixed, gate_back, up_back, feed_out, normed_two_back = feed_forward(normed_two, upstream, pair_full, down_full)
    layer_output = to_features((hidden + feed_out).astype(BF16))

    def scatter_gradient(left, *rights, sums=None):
        mine, other = gradient_parts(order, left, *rights, sums=sums)
        other = lax.ppermute(other, "core", [(0, 1), (1, 0)])

        def part(s, half):
            return halves(mine[s], half).astype(F32) + halves(other[s], half).astype(F32)

        return RingScatter(part, columns)

    down_ring = scatter_gradient(upstream, mixed)
    pair_ring = scatter_gradient(normed_two, gate_back, up_back)
    hidden_part, gain_two_part = norm_back(normed_two_back, hidden, scale_two, gain_two)
    hidden_back = upstream.astype(F32) + hidden_part
    hidden_low = hidden_back.astype(BF16)
    attended_back = dg(hidden_low, output_full, NT).astype(BF16)
    output_ring = scatter_gradient(hidden_low, attended_rows, sums=gain_two_part)

    heads_back = swap_cores(attended_back.reshape(own, cores, -1).transpose(1, 0, 2)).reshape(held, -1)
    heads_back = heads_back.reshape(held, groups, REPEAT, HEAD_DIM).transpose(1, 2, 0, 3)
    delta = jnp.sum(heads_back.astype(F32) * attended.astype(F32), axis=3)
    delta = delta.reshape(groups, REPEAT, -1, block).transpose(0, 2, 1, 3)
    delta = delta.reshape(groups, -1, 1, REPEAT * block)
    heads_back = jnp.pad(heads_back, ((0, 0), (0, 0), (0, 0), (HEAD_DIM, 0)))
    query_backs, pair_rings = [], []
    down_ring.step()
    down_ring.step()
    for g in range(groups):
        if g == 0:
            heads_back = after(heads_back, [down_ring, pair_ring])
            down_ring.step()
            pair_ring.step()
        else:
            rings = [pair_ring, output_ring, *pair_rings] + ([down_ring] if g == 1 else [])
            heads_back = after(heads_back, rings)
            for ring in (pair_ring, output_ring, *pair_rings):
                if ring.left and (ring is not pair_ring or g < 2):
                    ring.step()
        query_back, pair_back = attention_backward(g, lists, counts, queries, heads_back, pieces, marks, lse, delta)
        pair_back = pair_back.reshape(2 * columns, held, -1)
        query_backs.append(query_back)
        pair_rings.append(RingScatter(lambda s, half, v=pair_back: halves(v[s], half).astype(F32), columns))
    pair_backs = [ring.finish() for ring in pair_rings]
    pair_backs[0] = after(pair_backs[0], [pair_ring, output_ring])
    held_pairs = jnp.concatenate([p.astype(BF16) for p in pair_backs], axis=1)
    held_pairs = after(held_pairs, [pair_ring, output_ring])
    query_back = jnp.concatenate(query_backs, axis=0)
    query_back = query_back.reshape(groups * REPEAT, held, HEAD_DIM).transpose(1, 0, 2).reshape(held, -1)
    packed = jnp.concatenate([query_back, held_pairs], axis=1).reshape(cores, own, -1)
    packed = swap_cores(packed)
    query_back = packed[:, :, :wide].transpose(1, 0, 2).reshape(own, HEADS, HEAD_DIM)
    pair_back = packed[:, :, wide:].transpose(1, 0, 2).reshape(own, KV_HEADS, 2 * HEAD_DIM)
    query_back = turn(query_back.astype(F32), cosines, -sines).astype(BF16).reshape(own, ATT)
    key_back = turn(pair_back[:, :, :HEAD_DIM].astype(F32), cosines, -sines).astype(BF16).reshape(own, KEYS)
    value_back = pair_back[:, :, HEAD_DIM:].reshape(own, KEYS)
    joint_back = jnp.concatenate([query_back, key_back, value_back], axis=1)
    normed_one_back = dg(joint_back, joint_full, NT)
    stream_part, gain_one_part = norm_back(normed_one_back, stream, scale_one, gain_one)
    joint_ring = scatter_gradient(normed_one, joint_back, sums=gain_one_part)
    input_gradient = to_features((hidden_back + stream_part).astype(BF16)).astype(F32)
    down_gradient = down_ring.finish().T
    pair_gradient = pair_ring.finish()
    output_summed = output_ring.finish()
    joint_summed = joint_ring.finish()
    features = D // rows

    def carried(summed):
        lines = -(-features // summed.shape[1])
        return summed[features : features + lines, : features // lines].reshape(-1)

    width = gate_weight.shape[1]
    return (
        layer_output,
        input_gradient,
        carried(joint_summed),
        joint_summed[:features],
        output_summed[:features].T,
        carried(output_summed),
        pair_gradient[:, :width],
        pair_gradient[:, width:],
        down_gradient,
    )


def solution(mesh):
    leaves, rows, columns = (mesh.shape[name] for name in ("leaf", "row", "col"))
    split = Mesh(mesh.devices.reshape(leaves, rows // 2, 2, columns), ("leaf", "high", "core", "col"))
    return jax.shard_map(
        per_device,
        mesh=split,
        in_specs=(
            P(("leaf", "col"), ROW),
            P(ROW),
            P(ROW, "col"),
            P("col", ROW),
            P(ROW),
            P(ROW, "col"),
            P(ROW, "col"),
            P("col", ROW),
            P(("leaf", "col"), ROW),
            P("leaf"),
            P("leaf"),
        ),
        out_specs=(
            P(("leaf", "col"), ROW),
            P(("leaf", "col"), ROW),
            P(("leaf", *ROW)),
            P(("leaf", *ROW), "col"),
            P(("leaf", "col"), ROW),
            P(("leaf", *ROW)),
            P(("leaf", *ROW), "col"),
            P(("leaf", *ROW), "col"),
            P(("leaf", "col"), ROW),
        ),
        check_vma=False,
    )
```

```python
import functools

import jax
import jax.numpy as jnp
from jax import lax
from jax.experimental import pallas as pl
from jax.experimental.pallas import tpu as pltpu
from jax.sharding import Mesh
from jax.sharding import PartitionSpec as P

D = 1152
HEADS = 18
KV_HEADS = 6
HEAD_DIM = 64
REPEAT = HEADS // KV_HEADS
ATT = HEADS * HEAD_DIM
KEYS = KV_HEADS * HEAD_DIM

EPSILON = 1e-05
THETA = 10000.0
BIG = 2.0**30
LOG2E = 1.4426950408889634
UNROLL = 8
BF16 = jnp.bfloat16
F32 = jnp.float32
NT = (((1,), (1,)), ((), ()))
NN = (((1,), (0,)), ((), ()))


def dg(a, b, dims):
    return lax.dot_general(a, b, dims, preferred_element_type=F32)


def tree_tables(segment_lengths, parents):
    count = segment_lengths.shape[0]
    labels = jnp.arange(count, dtype=jnp.int32)
    ends = jnp.sum(jnp.where(labels[None, :] <= labels[:, None], segment_lengths[None, :], 0), axis=1)
    starts = ends - segment_lengths
    parent_hot = parents[:, None] == labels[None, :]
    grand = jnp.sum(jnp.where(parent_hot, parents[None, :], 0), axis=1)
    self_mark = labels[:, None] == labels[None, :]
    grand_mark = grand[:, None] == labels[None, :]
    ancestry = (self_mark | parent_hot | grand_mark).astype(F32)
    strict = (parent_hot | grand_mark) & jnp.logical_not(self_mark)
    offsets = jnp.sum(jnp.where(strict, segment_lengths[None, :], 0), axis=1)
    return (ends, starts, ancestry, offsets)


def segment_hot(index, tables):
    ends, starts, _, _ = tables
    return (index[:, None] >= starts[None, :]) & (index[:, None] < ends[None, :])


def rotary_tables(index, tables):
    hot = segment_hot(index, tables)
    depth = index + jnp.sum(jnp.where(hot, (tables[3] - tables[1])[None, :], 0), axis=1)
    half = HEAD_DIM // 2
    rates = THETA ** (-jnp.arange(half, dtype=F32) / half)
    angles = depth.astype(F32)[:, None] * rates[None, :]
    cosines, sines = jnp.cos(angles), jnp.sin(angles)
    return (jnp.concatenate([cosines] * 4, axis=1), jnp.concatenate([-sines, sines] * 2, axis=1))


def block_lists(first, key_index, block, held, tables):
    ends, starts, ancestry, _ = tables
    blocks = held // block
    key_low = key_index[::block]
    labels = jnp.arange(key_low.shape[0], dtype=jnp.int32)
    low = first + jnp.arange(blocks, dtype=jnp.int32) * block
    high = low + block
    query_has = ((starts[None, :] < high[:, None]) & (ends[None, :] > low[:, None])).astype(F32)
    key_has = ((starts[None, :] < key_low[:, None] + block) & (ends[None, :] > key_low[:, None])).astype(F32)
    reach = jnp.sum(query_has[:, :, None] * ancestry[None], axis=1)
    seen = jnp.sum(reach[:, None, :] * key_has[None], axis=2) > 0.5
    seen = seen & (key_low[None, :] < low[:, None])
    before = labels[None, :] < labels[:, None]
    rank = jnp.sum((seen[:, None, :] & before[None]).astype(jnp.int32), axis=2)
    place = seen[:, None, :] & (rank[:, None, :] == labels[None, :, None])
    lists = jnp.sum(jnp.where(place, labels[None, None, :], 0), axis=2)
    counts = jnp.sum(seen.astype(jnp.int32), axis=1)
    own = jnp.sum(jnp.where(key_low[None, :] == low[:, None], labels[None, :], 0), axis=1)
    lists = jnp.where(labels[None, :] == counts[:, None], own[:, None], lists)
    return (lists.reshape(-1).astype(jnp.int32), counts.astype(jnp.int32))


def cascade(count, unroll, steps):
    def body(i, c):
        steps(i * unroll, unroll)
        return c

    whole = count // unroll
    lax.fori_loop(0, whole, body, 0)
    start = whole * unroll
    size = unroll // 2
    while size:
        some = ((count - start) // size) > 0
        pl.when(some)(functools.partial(steps, start, size))
        start = start + jnp.where(some, size, 0)
        size //= 2


def causal(scores, heads):
    rows = lax.broadcasted_iota(jnp.int32, scores.shape, 0)
    columns = lax.rem(lax.broadcasted_iota(jnp.int32, scores.shape, 1), scores.shape[1] // heads)
    return jnp.where(rows <= columns, scores, -BIG)


def stacked(ref):
    value, wide = ref[...], 2 * HEAD_DIM
    return jnp.concatenate([value[:, h * wide : (h + 1) * wide] for h in range(value.shape[1] // wide)], axis=0)


def beside(value, heads):
    rows = value.shape[0] // heads
    return jnp.concatenate([value[h * rows : (h + 1) * rows] for h in range(heads)], axis=1)


def left_half(shape):
    return lax.broadcasted_iota(jnp.int32, shape, 1) < HEAD_DIM


def fetch(pieces, group, kv_ref, sems):
    copies, start = [], 0
    for i, piece in enumerate(pieces):
        lanes = pl.ds(pl.multiple_of(group * 2 * HEAD_DIM, 2 * HEAD_DIM), 2 * HEAD_DIM)
        target = kv_ref.at[pl.ds(start, piece.shape[0])]
        copies.append(pltpu.make_async_copy(piece.at[:, lanes], target, sems.at[i]))
        start += piece.shape[0]
    for copy in copies:
        copy.start()
    for copy in copies:
        copy.wait()


def forward_kernel(lists, counts, q_ref, mark_ref, *refs):
    *pieces, o_ref, lse_ref, top_ref, sum_ref, kv_ref, vt_ref, sems = refs
    block = pl.program_id(1)
    heads, rows = q_ref.shape[1] // (2 * HEAD_DIM), q_ref.shape[0]
    total = kv_ref.shape[0]
    stride = total // rows
    count = counts[block]

    @pl.when(block == 0)
    def _():
        fetch(pieces, pl.program_id(0), kv_ref, sems)

        def flip(i, c):
            k0 = pl.multiple_of(i * rows, rows)
            turned = kv_ref[pl.ds(k0, rows), :].T
            vt_ref[:HEAD_DIM, pl.ds(k0, rows)] = turned[HEAD_DIM:]
            return c

        lax.fori_loop(0, stride, flip, 0)
        tail = (vt_ref.shape[0] - HEAD_DIM, total)
        vt_ref[HEAD_DIM:] = jnp.where(lax.broadcasted_iota(jnp.int32, tail, 0) == 0, 1.0, 0.0).astype(BF16)

    def queries():
        return stacked(q_ref)

    def blocks(start, n):
        offs = [pl.multiple_of(lists[block * stride + start + u] * rows, rows) for u in range(n)]
        kv = jnp.concatenate([kv_ref[pl.ds(k0, rows), :] for k0 in offs], axis=0)
        mark = jnp.concatenate([mark_ref[pl.ds(k0, rows), :] for k0 in offs], axis=0)
        vt = jnp.concatenate([vt_ref[:, pl.ds(k0, rows)] for k0 in offs], axis=1)
        return jnp.where(left_half(kv.shape), kv, mark), vt

    def begin():
        k, vt = blocks(count, 1)
        scores = causal(dg(k, queries(), NT), heads)
        top = jnp.max(scores, axis=0, keepdims=True)
        top_ref[...] = top
        sum_ref[...] = dg(vt, jnp.exp2(scores - top).astype(BF16), NN)

    def steps(start, n):
        k, vt = blocks(start, n)
        weights = jnp.exp2(dg(k, queries(), NT) - top_ref[...]).astype(BF16)
        sum_ref[...] += dg(vt, weights, NN)

    begin()
    cascade(count, UNROLL, steps)

    @pl.when(jnp.logical_not(jnp.max(sum_ref[HEAD_DIM : HEAD_DIM + 1, :]) < 2.0**100))
    def _():
        begin()

        def online(n, c):
            k, vt = blocks(n, 1)
            scores = dg(k, queries(), NT)
            old = top_ref[...]
            new = jnp.maximum(old, jnp.max(scores, axis=0, keepdims=True))
            top_ref[...] = new
            sum_ref[...] = sum_ref[...] * jnp.exp2(old - new) + dg(vt, jnp.exp2(scores - new).astype(BF16), NN)
            return c

        lax.fori_loop(0, count, online, 0)

    total_row = sum_ref[HEAD_DIM : HEAD_DIM + 1, :]
    spread = jnp.concatenate([jnp.zeros((HEAD_DIM, heads * rows), F32), sum_ref[:HEAD_DIM, :] / total_row], axis=0)
    o_ref[...] = beside(spread.T.astype(BF16), heads)
    lse_ref[0, 0] = top_ref[...] + jnp.log2(total_row)


def attention_forward(lists, counts, q, pieces, marks):
    tokens, wide, heads = q.shape[0], 2 * HEAD_DIM, REPEAT
    groups = q.shape[1] // (wide * (heads + 1))
    total = marks.shape[0]
    blocks = counts.shape[0]
    rows = tokens // blocks
    tall = HEAD_DIM + 16
    return pl.pallas_call(
        forward_kernel,
        grid_spec=pltpu.PrefetchScalarGridSpec(
            num_scalar_prefetch=2,
            grid=(groups, blocks),
            in_specs=[
                pl.BlockSpec((rows, heads * wide), lambda g, b, *_: (b, g)),
                pl.BlockSpec((total, wide), lambda g, b, *_: (0, 0)),
                *(pl.BlockSpec(memory_space=pl.ANY) for _ in pieces),
            ],
            out_specs=[
                pl.BlockSpec((rows, heads * wide), lambda g, b, *_: (b, g)),
                pl.BlockSpec((1, 1, 1, heads * rows), lambda g, b, *_: (g, b, 0, 0)),
            ],
            scratch_shapes=[
                pltpu.VMEM((1, heads * rows), F32),
                pltpu.VMEM((tall, heads * rows), F32),
                pltpu.VMEM((total, wide), BF16),
                pltpu.VMEM((tall, total), BF16),
                pltpu.SemaphoreType.DMA((len(pieces),)),
            ],
        ),
        out_shape=[
            jax.ShapeDtypeStruct((tokens, groups * heads * wide), BF16),
            jax.ShapeDtypeStruct((groups, blocks, 1, heads * rows), F32),
        ],
        compiler_params=pltpu.CompilerParams(vmem_limit_bytes=48 * 2**20),
        cost_estimate=pl.CostEstimate(
            flops=groups * heads * tokens * total * 256, bytes_accessed=groups * total * 512, transcendentals=0
        ),
        name="attention_forward",
    )(lists, counts, q, marks, *pieces)


def stage_kernel(begins, ends, lists, counts, q_ref, mark_ref, *refs):
    refs = list(refs)
    sums_in, tops_in = ([refs.pop(0), refs.pop(0)] if not begins else (None, None))
    *pieces, first_ref, second_ref, top_ref, sum_ref, kv_ref, vt_ref, sems = refs
    block = pl.program_id(1)
    heads, rows = q_ref.shape[1] // (2 * HEAD_DIM), q_ref.shape[0]
    total = kv_ref.shape[0]
    stride = total // rows
    count = counts[block]

    @pl.when(block == 0)
    def _():
        fetch(pieces, pl.program_id(0), kv_ref, sems)

        def flip(i, c):
            k0 = pl.multiple_of(i * rows, rows)
            turned = kv_ref[pl.ds(k0, rows), :].T
            vt_ref[:HEAD_DIM, pl.ds(k0, rows)] = turned[HEAD_DIM:]
            return c

        lax.fori_loop(0, stride, flip, 0)
        tail = (vt_ref.shape[0] - HEAD_DIM, total)
        vt_ref[HEAD_DIM:] = jnp.where(lax.broadcasted_iota(jnp.int32, tail, 0) == 0, 1.0, 0.0).astype(BF16)

    def queries():
        return stacked(q_ref)

    def blocks(start, n):
        offs = [pl.multiple_of(lists[block * stride + start + u] * rows, rows) for u in range(n)]
        kv = jnp.concatenate([kv_ref[pl.ds(k0, rows), :] for k0 in offs], axis=0)
        mark = jnp.concatenate([mark_ref[pl.ds(k0, rows), :] for k0 in offs], axis=0)
        vt = jnp.concatenate([vt_ref[:, pl.ds(k0, rows)] for k0 in offs], axis=1)
        return jnp.where(left_half(kv.shape), kv, mark), vt

    if begins:
        k, vt = blocks(count, 1)
        scores = causal(dg(k, queries(), NT), heads)
        top = jnp.max(scores, axis=0, keepdims=True)
        top_ref[...] = top
        sum_ref[...] = dg(vt, jnp.exp2(scores - top).astype(BF16), NN)
    else:
        top_ref[...] = tops_in[0, 0]
        sum_ref[...] = sums_in[0, 0]

    def steps(start, n):
        k, vt = blocks(start, n)
        weights = jnp.exp2(dg(k, queries(), NT) - top_ref[...]).astype(BF16)
        sum_ref[...] += dg(vt, weights, NN)

    cascade(count, UNROLL, steps)
    if ends:
        total_row = sum_ref[HEAD_DIM : HEAD_DIM + 1, :]
        spread = jnp.concatenate([jnp.zeros((HEAD_DIM, heads * rows), F32), sum_ref[:HEAD_DIM, :] / total_row], axis=0)
        first_ref[...] = beside(spread.T.astype(BF16), heads)
        second_ref[0, 0] = jnp.where(total_row < 2.0**100, top_ref[...] + jnp.log2(total_row), jnp.nan)
    else:
        first_ref[0, 0] = sum_ref[...]
        second_ref[0, 0] = top_ref[...]


def attention_stage(lists, counts, q, pieces, marks, state, ends):
    tokens, wide, heads = q.shape[0], 2 * HEAD_DIM, REPEAT
    groups = q.shape[1] // (wide * (heads + 1))
    total = marks.shape[0]
    blocks = counts.shape[0]
    rows = tokens // blocks
    tall = HEAD_DIM + 16
    lanes = heads * rows
    held_specs = [
        pl.BlockSpec((1, 1, tall, lanes), lambda g, b, *_: (g, b, 0, 0)),
        pl.BlockSpec((1, 1, 1, lanes), lambda g, b, *_: (g, b, 0, 0)),
    ]
    tops = jax.ShapeDtypeStruct((groups, blocks, 1, lanes), F32)
    if ends:
        out_specs = [pl.BlockSpec((rows, heads * wide), lambda g, b, *_: (b, g)), held_specs[1]]
        out_shape = [jax.ShapeDtypeStruct((tokens, groups * heads * wide), BF16), tops]
    else:
        out_specs = held_specs
        out_shape = [jax.ShapeDtypeStruct((groups, blocks, tall, lanes), F32), tops]
    return pl.pallas_call(
        functools.partial(stage_kernel, state is None, ends),
        grid_spec=pltpu.PrefetchScalarGridSpec(
            num_scalar_prefetch=2,
            grid=(groups, blocks),
            in_specs=[
                pl.BlockSpec((rows, heads * wide), lambda g, b, *_: (b, g)),
                pl.BlockSpec((total, wide), lambda g, b, *_: (0, 0)),
                *([] if state is None else held_specs),
                *(pl.BlockSpec(memory_space=pl.ANY) for _ in pieces),
            ],
            out_specs=out_specs,
            scratch_shapes=[
                pltpu.VMEM((1, lanes), F32),
                pltpu.VMEM((tall, lanes), F32),
                pltpu.VMEM((total, wide), BF16),
                pltpu.VMEM((tall, total), BF16),
                pltpu.SemaphoreType.DMA((len(pieces),)),
            ],
        ),
        out_shape=out_shape,
        compiler_params=pltpu.CompilerParams(vmem_limit_bytes=40 * 2**20),
        cost_estimate=pl.CostEstimate(
            flops=groups * heads * tokens * total * 256, bytes_accessed=groups * total * 512, transcendentals=0
        ),
        name="attention_stage",
    )(lists, counts, q, marks, *(() if state is None else state), *pieces)


def backward_kernel(group, lists, counts, q_ref, do_ref, o_ref, mark_ref, lse_ref, *refs):
    *pieces, dq_ref, dkv_ref, dq_sum, dkv_sum, kv_ref, kt_ref, delta_ref, sems = refs
    block = pl.program_id(0)
    heads, rows = q_ref.shape[1] // (2 * HEAD_DIM), q_ref.shape[0]
    total = kv_ref.shape[0]
    stride = total // rows
    count = counts[block]

    @pl.when(block == 0)
    def _():
        dkv_sum[...] = jnp.zeros(dkv_sum.shape, F32)
        fetch(pieces, group, kv_ref, sems)

        def flip(i, c):
            k0 = pl.multiple_of(i * rows, rows)
            turned = kv_ref[pl.ds(k0, rows), :].T
            kt_ref[:, pl.ds(k0, rows)] = turned[:HEAD_DIM]
            return c

        lax.fori_loop(0, stride, flip, 0)

    dq_sum[...] = jnp.zeros(dq_sum.shape, F32)
    products = stacked(do_ref).astype(F32) * stacked(o_ref).astype(F32)
    delta_ref[...] = jnp.sum(products.T, axis=0, keepdims=True)

    def steps(start, n, masked):
        q, do = stacked(q_ref), stacked(do_ref)
        offs = [pl.multiple_of(lists[block * stride + start + u] * rows, rows) for u in range(n)]
        kv = jnp.concatenate([kv_ref[pl.ds(k0, rows), :] for k0 in offs], axis=0)
        mark = jnp.concatenate([mark_ref[pl.ds(k0, rows), :] for k0 in offs], axis=0)
        kt = jnp.concatenate([kt_ref[:, pl.ds(k0, rows)] for k0 in offs], axis=1)
        scores = dg(jnp.where(left_half(kv.shape), kv, mark), q, NT) - lse_ref[0, 0]
        if masked:
            scores = causal(scores, heads)
        chances = jnp.exp2(scores)
        back = dg(kv, do, NT) - delta_ref[...]
        score_back = (chances * back).astype(BF16)
        only_q = jnp.where(left_half(q.shape), q, jnp.zeros_like(q))
        update = dg(score_back, only_q, NN) + dg(chances.astype(BF16), do, NN)
        dq_sum[...] += dg(kt, score_back, NN)
        for u in range(n):
            dkv_sum[pl.ds(offs[u], rows), :] += update[u * rows : (u + 1) * rows]

    steps(count, 1, True)
    cascade(count, UNROLL, lambda start, n: steps(start, n, False))
    spread = jnp.concatenate([dq_sum[...] * HEAD_DIM**-0.5, jnp.zeros(dq_sum.shape, F32)], axis=0)
    dq_ref[...] = beside(spread.T.astype(BF16), heads)

    @pl.when(block == pl.num_programs(0) - 1)
    def _():
        summed = dkv_sum[...]
        dkv_ref[...] = jnp.where(left_half(summed.shape), summed * (1.0 / LOG2E), summed).astype(BF16)


def attention_backward(group, lists, counts, q, do, o, pieces, marks, lse):
    tokens, wide, heads = q.shape[0], 2 * HEAD_DIM, REPEAT
    total = marks.shape[0]
    blocks = counts.shape[0]
    rows = tokens // blocks
    block = pl.BlockSpec((rows, heads * wide), lambda b, *_: (b, group))
    return pl.pallas_call(
        functools.partial(backward_kernel, group),
        grid_spec=pltpu.PrefetchScalarGridSpec(
            num_scalar_prefetch=2,
            grid=(blocks,),
            in_specs=[
                block,
                block,
                block,
                pl.BlockSpec((total, wide), lambda b, *_: (0, 0)),
                pl.BlockSpec((1, 1, 1, heads * rows), lambda b, *_: (group, b, 0, 0)),
                *(pl.BlockSpec(memory_space=pl.ANY) for _ in pieces),
            ],
            out_specs=[
                pl.BlockSpec((rows, heads * wide), lambda b, *_: (b, 0)),
                pl.BlockSpec((total, wide), lambda b, *_: (0, 0)),
            ],
            scratch_shapes=[
                pltpu.VMEM((HEAD_DIM, heads * rows), F32),
                pltpu.VMEM((total, wide), F32),
                pltpu.VMEM((total, wide), BF16),
                pltpu.VMEM((HEAD_DIM, total), BF16),
                pltpu.VMEM((1, heads * rows), F32),
                pltpu.SemaphoreType.DMA((len(pieces),)),
            ],
        ),
        out_shape=[
            jax.ShapeDtypeStruct((tokens, heads * wide), BF16),
            jax.ShapeDtypeStruct((total, wide), BF16),
        ],
        compiler_params=pltpu.CompilerParams(vmem_limit_bytes=60 * 2**20),
        cost_estimate=pl.CostEstimate(flops=heads * tokens * total * 640, bytes_accessed=total * 1024, transcendentals=0),
        name="attention_backward",
    )(lists, counts, q, do, o, marks, lse, *pieces)


def roll_half(value):
    return pltpu.roll(value, HEAD_DIM, 1)


def swap_quarters(value):
    quarter = HEAD_DIM // 2
    lane = lax.broadcasted_iota(jnp.int32, value.shape, 1)
    first = lax.rem(lane, HEAD_DIM) < quarter
    return jnp.where(first, pltpu.roll(value, value.shape[1] - quarter, 1), pltpu.roll(value, quarter, 1))


def root_mean(value):
    return lax.rsqrt(jnp.sum(value * value, axis=1, keepdims=True) / D + EPSILON)


def project_kernel(x4_ref, w_ref, cos_ref, sin_ref, bars_ref, x_ref, xa_ref, full_ref, packed_ref, gains_ref, joint_ref):
    own = x_ref.shape[0]
    wide = 2 * HEAD_DIM
    x = jnp.concatenate([x4_ref[r, :own, :] for r in range(x4_ref.shape[0])], axis=1)
    gains = jnp.concatenate([x4_ref[r, own : own + 16, :] for r in range(x4_ref.shape[0])], axis=1).astype(F32)
    x_ref[...] = x
    gains_ref[...] = gains[:8]
    value = x.astype(F32)
    xa_ref[...] = (value * root_mean(value) * gains[0:1]).astype(BF16)
    full_ref[...] = jnp.concatenate([w_ref[c] for c in range(w_ref.shape[0])], axis=1)
    joint_ref[...] = dg(xa_ref[...], full_ref[...], NN).astype(BF16)
    left = left_half((own, wide))
    bars = bars_ref[...].astype(F32)
    heads, pairs = HEADS // 2, KV_HEADS // 2

    def part(i):
        return joint_ref[:, i * wide : (i + 1) * wide].astype(F32)

    def turned(i):
        value = part(i)
        return value * cos_ref[...] + swap_quarters(value) * sin_ref[...]

    for i in range(HEADS // 2):
        value = turned(i) * (LOG2E * HEAD_DIM**-0.5)
        for j, head in ((2 * i, value), (2 * i + 1, roll_half(value))):
            start = (j % heads) * wide
            packed_ref[j // heads, :, start : start + wide] = jnp.where(left, head, bars).astype(BF16)
    for i in range(KV_HEADS // 2):
        key = turned(HEADS // 2 + i)
        value = part(HEADS // 2 + KV_HEADS // 2 + i)
        for j, both in (
            (2 * i, jnp.where(left, key, roll_half(value))),
            (2 * i + 1, jnp.where(left, roll_half(key), value)),
        ):
            start = heads * wide + (j % pairs) * wide
            packed_ref[j // pairs, :, start : start + wide] = both.astype(BF16)


def project_in(x4, weight, cosines, sines, bars):
    own = cosines.shape[0]
    shapes = [
        jax.ShapeDtypeStruct((own, D), BF16),
        jax.ShapeDtypeStruct((own, D), BF16),
        jax.ShapeDtypeStruct((D, ATT + 2 * KEYS), BF16),
        jax.ShapeDtypeStruct((2, own, ATT + KEYS), BF16),
        jax.ShapeDtypeStruct((8, D), F32),
    ]
    return pl.pallas_call(
        project_kernel,
        out_shape=shapes,
        scratch_shapes=[pltpu.VMEM((own, ATT + 2 * KEYS), BF16)],
        compiler_params=pltpu.CompilerParams(vmem_limit_bytes=56 * 2**20),
        cost_estimate=pl.CostEstimate(flops=2 * own * D * (ATT + 2 * KEYS), bytes_accessed=2**24, transcendentals=0),
        name="project_in",
    )(x4, weight, cosines, sines, bars)


def output_kernel(width, o_ref, w_ref, x_ref, gains_ref, rows_ref, hidden_ref, normed_ref, full_ref):
    wide = 2 * HEAD_DIM
    heads = HEADS // 2
    left = left_half((x_ref.shape[0], wide))
    for i in range(HEADS // 2):
        first, second = (
            o_ref[j // heads, :, (j % heads) * wide : (j % heads + 1) * wide] for j in (2 * i, 2 * i + 1)
        )
        first = roll_half(first.astype(F32))
        rows_ref[:, i * wide : (i + 1) * wide] = jnp.where(left, first, second.astype(F32)).astype(BF16)
    full_ref[...] = jnp.concatenate([w_ref[c, :, :width] for c in range(w_ref.shape[0])], axis=1)
    hidden = x_ref[...].astype(F32) + dg(rows_ref[...], full_ref[...], NT)
    hidden_ref[...] = hidden
    normed_ref[...] = (hidden * root_mean(hidden) * gains_ref[1:2]).astype(BF16)


def project_out(o, late, x, gains, width, padded):
    own = x.shape[0]
    place = late.shape[2] // padded - 1
    return pl.pallas_call(
        functools.partial(output_kernel, width),
        grid=(1,),
        in_specs=[
            pl.BlockSpec(o.shape, lambda i: (0, 0, 0)),
            pl.BlockSpec((late.shape[0], D, padded), lambda i: (0, 0, place)),
            pl.BlockSpec(x.shape, lambda i: (0, 0)),
            pl.BlockSpec(gains.shape, lambda i: (0, 0)),
        ],
        out_specs=[pl.BlockSpec((own, D), lambda i: (0, 0))] * 3 + [pl.BlockSpec((D, ATT), lambda i: (0, 0))],
        out_shape=[
            jax.ShapeDtypeStruct((own, ATT), BF16),
            jax.ShapeDtypeStruct((own, D), F32),
            jax.ShapeDtypeStruct((own, D), BF16),
            jax.ShapeDtypeStruct((D, ATT), BF16),
        ],
        compiler_params=pltpu.CompilerParams(vmem_limit_bytes=56 * 2**20),
        cost_estimate=pl.CostEstimate(flops=2 * own * D * ATT, bytes_accessed=2**24, transcendentals=0),
        name="project_out",
    )(o, late, x, gains)


def norm_back(upstream, value, gain):
    scale = root_mean(value)
    weighted = upstream * gain
    inner = jnp.sum(weighted * value, axis=1, keepdims=True)
    gain_back = jnp.sum(upstream * value * scale, axis=0, keepdims=True)
    return scale * weighted - value * (scale * scale * scale * inner / D), gain_back


def output_back_kernel(back_ref, hidden_ref, upstream_ref, gains_ref, full_ref, hidden_back_ref, low_ref, do_ref, sums_ref):
    wide = 2 * HEAD_DIM
    heads = HEADS // 2
    part, sums = norm_back(back_ref[...], hidden_ref[...], gains_ref[1:2])
    hidden_back = upstream_ref[...].astype(F32) + part
    hidden_back_ref[...] = hidden_back
    low_ref[...] = hidden_back.astype(BF16)
    sums_ref[...] = jnp.broadcast_to(sums, sums_ref.shape)
    attended_back = dg(low_ref[...], full_ref[...], NN)
    left = left_half((low_ref.shape[0], wide))
    for i in range(HEADS // 2):
        value = attended_back[:, i * wide : (i + 1) * wide]
        for j, head in ((2 * i, roll_half(value)), (2 * i + 1, value)):
            start = (j % heads) * wide
            do_ref[j // heads, :, start : start + wide] = jnp.where(left, 0.0, head).astype(BF16)


def output_back(back, hidden, upstream, gains, full):
    own = back.shape[0]
    return pl.pallas_call(
        output_back_kernel,
        out_shape=[
            jax.ShapeDtypeStruct((own, D), F32),
            jax.ShapeDtypeStruct((own, D), BF16),
            jax.ShapeDtypeStruct((2, own, ATT), BF16),
            jax.ShapeDtypeStruct((8, D), F32),
        ],
        compiler_params=pltpu.CompilerParams(vmem_limit_bytes=56 * 2**20),
        cost_estimate=pl.CostEstimate(flops=2 * own * D * ATT, bytes_accessed=2**24, transcendentals=0),
        name="output_back",
    )(back, hidden, upstream, gains, full)


def joint_back_kernel(packed_ref, cos_ref, sin_ref, full_ref, x_ref, gains_ref, hidden_back_ref, joint_ref, out_ref, sums_ref):
    wide = 2 * HEAD_DIM
    heads, pairs = HEADS // 2, KV_HEADS // 2
    left = left_half((x_ref.shape[0], wide))

    def queries(j):
        return packed_ref[j // heads, :, (j % heads) * wide : (j % heads + 1) * wide].astype(F32)

    def both(j):
        start = (heads + j % pairs) * wide
        return packed_ref[j // pairs, :, start : start + wide].astype(F32)

    def store(i, value):
        joint_ref[:, i * wide : (i + 1) * wide] = value.astype(BF16)

    def back(value):
        return value * cos_ref[...] - swap_quarters(value) * sin_ref[...]

    for i in range(HEADS // 2):
        store(i, back(jnp.where(left, queries(2 * i), roll_half(queries(2 * i + 1)))))
    for i in range(KV_HEADS // 2):
        first, second = both(2 * i), both(2 * i + 1)
        store(HEADS // 2 + i, back(jnp.where(left, first, roll_half(second))))
        store(HEADS // 2 + KV_HEADS // 2 + i, jnp.where(left, roll_half(first), second))
    upstream = dg(joint_ref[...], full_ref[...], NT)
    part, sums = norm_back(upstream, x_ref[...].astype(F32), gains_ref[0:1])
    total = (hidden_back_ref[...] + part).astype(BF16)
    features = out_ref.shape[2]
    for r in range(out_ref.shape[0]):
        out_ref[r] = total[:, r * features : (r + 1) * features]
    sums_ref[...] = jnp.broadcast_to(sums, sums_ref.shape)


def joint_back(packed, cosines, sines, full, x, gains, hidden_back, rows):
    own = x.shape[0]
    return pl.pallas_call(
        joint_back_kernel,
        out_shape=[
            jax.ShapeDtypeStruct((own, ATT + 2 * KEYS), BF16),
            jax.ShapeDtypeStruct((rows, own, D // rows), BF16),
            jax.ShapeDtypeStruct((8, D), F32),
        ],
        compiler_params=pltpu.CompilerParams(vmem_limit_bytes=56 * 2**20),
        cost_estimate=pl.CostEstimate(flops=2 * own * D * (ATT + 2 * KEYS), bytes_accessed=2**24, transcendentals=0),
        name="joint_back",
    )(packed, cosines, sines, full, x, gains, hidden_back)


def feed_part(width):
    return width // 2 if width % 256 == 0 else width


def feed_kernel(normed_ref, back_ref, gate_ref, up_ref, down_ref, mixed_ref, gate_back_ref, up_back_ref, out_ref, normed_back_ref):
    @pl.when((pl.program_id(0) == 0) & (pl.program_id(1) == 0))
    def _():
        out_ref[...] = jnp.zeros(out_ref.shape, F32)
        normed_back_ref[...] = jnp.zeros(normed_back_ref.shape, F32)

    gate = dg(normed_ref[...], gate_ref[0], NN)
    up_value = dg(normed_ref[...], up_ref[0], NN)
    mixed_back = dg(back_ref[...], down_ref[0], NN)
    sigmoid = jax.nn.sigmoid(gate)
    silu = gate * sigmoid
    mixed = (silu * up_value).astype(BF16)
    gate_back = (mixed_back * up_value * (sigmoid * (1.0 + gate * (1.0 - sigmoid)))).astype(BF16)
    up_back = (mixed_back * silu).astype(BF16)
    mixed_ref[...] = mixed
    gate_back_ref[...] = gate_back
    up_back_ref[...] = up_back
    out_ref[...] += dg(mixed, down_ref[0], NT)
    normed_back_ref[...] += dg(gate_back, gate_ref[0], NT) + dg(up_back, up_ref[0], NT)


def feed_forward(normed, back, late, width):
    tokens = normed.shape[0]
    columns = late.shape[0]
    part = feed_part(width)
    parts = width // part
    whole = pl.BlockSpec((tokens, D), lambda c, j: (0, 0))
    blocks = [pl.BlockSpec((1, D, part), lambda c, j, k=k: (c, 0, k * parts + j)) for k in range(3)]
    out = pl.BlockSpec((tokens, part), lambda c, j: (0, c * parts + j))
    return pl.pallas_call(
        feed_kernel,
        grid=(columns, parts),
        in_specs=[whole, whole, *blocks],
        out_specs=[out, out, out, whole, whole],
        out_shape=[jax.ShapeDtypeStruct((tokens, columns * width), BF16)] * 3 + [jax.ShapeDtypeStruct((tokens, D), F32)] * 2,
        compiler_params=pltpu.CompilerParams(vmem_limit_bytes=56 * 2**20),
        cost_estimate=pl.CostEstimate(
            flops=12 * tokens * D * columns * width, bytes_accessed=6 * D * columns * width, transcendentals=0
        ),
        name="feed_forward",
    )(normed, back, late, late, late)


def gradient_kernel(rights, summed, joined, order, left_ref, *refs):
    right_refs, refs = refs[:rights], refs[rights:]
    sums_ref = refs[0] if summed else None
    refs = refs[1:] if summed else refs
    if joined:
        both_ref, lefts, *held = refs
        mine_ref, other_ref = both_ref.at[:, 0], both_ref.at[:, 1]
    else:
        mine_ref, other_ref, lefts, *held = refs
    step = pl.program_id(0)
    features = lefts.shape[2]

    @pl.when(step == 0)
    def _():
        for r in range(lefts.shape[0]):
            lefts[r] = left_ref[:, r * features : (r + 1) * features]
        if held:
            width = held[0].shape[2]
            for c in range(held[0].shape[0]):
                held[0][c] = right_refs[0][:, c * width : (c + 1) * width]

    steps = pl.num_programs(0)
    column, row, core = order[step], order[steps + step] * 2, order[2 * steps]
    start = 0
    for right in right_refs:
        value = held[0][column] if held else right[...]
        width = value.shape[1]
        for target, r in ((mine_ref, row + core), (other_ref, row + 1 - core)):
            part = lax.dot_general(lefts[r], value, (((0,), (0,)), ((), ())), preferred_element_type=F32)
            target[0, :features, start : start + width] = part.astype(BF16)
        start += width
    if sums_ref is not None:
        for target, r in ((mine_ref, row + core), (other_ref, row + 1 - core)):
            target[0, features:, :] = sums_ref[r].astype(BF16)


def gradient_parts(order, left, *rights, sums=None, joined=False):
    tokens = left.shape[0]
    steps = (order.shape[0] - 1) // 2
    columns = steps // 2
    width = rights[0].shape[1] // columns
    features = left.shape[1] // 4
    aligned = width % 128 == 0
    if aligned:
        right_spec = pl.BlockSpec((tokens, width), lambda s, order: (0, order[s]))
    else:
        right_spec = pl.BlockSpec(rights[0].shape, lambda s, order: (0, 0))
    wide = width * len(rights)
    tall = features if sums is None else features + 16
    if joined:
        outs = [pl.BlockSpec((1, 2, tall, wide), lambda s, order: (s, 0, 0, 0))]
        shapes = [jax.ShapeDtypeStruct((steps, 2, tall, wide), BF16)]
    else:
        outs = [pl.BlockSpec((1, tall, wide), lambda s, order: (s, 0, 0))] * 2
        shapes = [jax.ShapeDtypeStruct((steps, tall, wide), BF16)] * 2
    held = [] if aligned else [pltpu.VMEM((columns, tokens, width), BF16)]
    more, more_specs = [], []
    if sums is not None:
        lines = -(-features // wide)
        more = [jnp.pad(sums.reshape(4, lines, -1), ((0, 0), (0, 16 - lines), (0, wide - features // lines)))]
        more_specs = [pl.BlockSpec((4, 16, wide), lambda s, order: (0, 0, 0))]
    return pl.pallas_call(
        functools.partial(gradient_kernel, len(rights), sums is not None, joined),
        grid_spec=pltpu.PrefetchScalarGridSpec(
            num_scalar_prefetch=1,
            grid=(steps,),
            in_specs=[
                pl.BlockSpec(left.shape, lambda s, order: (0, 0)),
                *(right_spec for _ in rights),
                *more_specs,
            ],
            out_specs=outs,
            scratch_shapes=[pltpu.VMEM((4, tokens, features), BF16), *held],
        ),
        out_shape=shapes,
        compiler_params=pltpu.CompilerParams(vmem_limit_bytes=56 * 2**20),
        cost_estimate=pl.CostEstimate(
            flops=2 * tokens * left.shape[1] * wide * columns, bytes_accessed=2 * left.shape[1] * wide * columns, transcendentals=0
        ),
        name="gradient_parts",
    )(order, left, *rights, *more)


ROW = ("high", "core")
ALL_ROW = ("high", "core", "col")
ALL_COL = ("col", "high", "core")
RING = ("high", "col")


def ring_steps(columns):
    path = [*range(columns), *reversed(range(columns, 2 * columns))]
    ahead = [(path[i], path[(i + 1) % len(path)]) for i in range(len(path))]
    return ahead, [(b, a) for a, b in ahead]


class RingScatter:
    def __init__(self, part, columns):
        self.part, (self.ahead, self.behind), self.count = part, ring_steps(columns), 2 * columns
        self.left = self.count // 2
        self.arrived = None
        self.ready = (part(self.left, 0).astype(BF16), part(self.left, 1).astype(BF16))

    def launch(self):
        out, back = self.ready
        self.arrived = (lax.ppermute(out, RING, self.ahead), lax.ppermute(back, RING, self.behind))
        self.ready = None
        self.left -= 1

    def prepare(self):
        out, back = self.part(self.left, None), self.part(self.count - self.left, None)
        front, rear = (v.astype(F32) for v in self.arrived)
        half = front.shape[0]
        if half == out.shape[0]:
            out, back = out + front, back + rear
        else:
            out = jnp.concatenate([out[:half] + front, out[half:]], axis=0)
            back = jnp.concatenate([back[:half], back[half:] + rear], axis=0)
        self.ready = (out.astype(BF16), back.astype(BF16))

    def finish(self):
        while self.left or self.ready:
            if self.ready is None:
                self.prepare()
            self.ready = lax.optimization_barrier(self.ready)
            self.launch()
        return self.part(0, None) + self.arrived[0].astype(F32) + self.arrived[1].astype(F32)


def depart(value, rings):
    for ring in rings:
        if ring.ready is None:
            ring.prepare()
    value, ready = lax.optimization_barrier((value, [ring.ready for ring in rings]))
    for ring, r in zip(rings, ready, strict=True):
        ring.ready = r
        ring.launch()
    return value


def halves(value, half):
    if half is None:
        return value
    middle = value.shape[0] // 2
    return value[middle:] if half else value[:middle]


def scatter(value, axes):
    return lax.psum_scatter(value, axes, scatter_dimension=0, tiled=True)


def gather(value, axes):
    return lax.all_gather(value, axes, axis=0, tiled=True)


def per_device(
    tokens,
    attention_gain,
    joint_weight,
    output_weight,
    feed_gain,
    gate_weight,
    up_weight,
    down_weight,
    cotangent,
    segment_lengths,
    parents,
):
    rows = lax.axis_size(ROW)
    columns = lax.axis_size("col")
    cores = lax.axis_size("core")
    own = tokens.shape[0] // rows
    held = own * cores
    groups = KV_HEADS // cores
    tables = tree_tables(segment_lengths, parents)
    row = lax.axis_index(ROW)
    column = lax.axis_index("col")
    high = lax.axis_index("high")
    core = lax.axis_index("core")
    index = column * tokens.shape[0] + row * own + jnp.arange(own, dtype=jnp.int32)
    cosines, sines = rotary_tables(index, tables)
    first = column * tokens.shape[0] + high * held

    spot = jnp.where(high == 0, column, 2 * columns - 1 - column)
    spots = lax.rem(spot + jnp.arange(2 * columns, dtype=jnp.int32), 2 * columns)
    far = spots >= columns
    ring_column = jnp.where(far, 2 * columns - 1 - spots, spots)
    ring_high = far.astype(jnp.int32)
    order = jnp.concatenate([ring_column, ring_high, jnp.reshape(core, (1,))]).astype(jnp.int32)
    key_first = ring_column * tokens.shape[0] + ring_high * held
    key_index = (key_first[:, None] + jnp.arange(held, dtype=jnp.int32)[None, :]).reshape(-1)

    block = 256 if held % 256 == 0 else 128
    lists, counts = block_lists(first, key_index, block, held, tables)
    key_hot = segment_hot(key_index, tables).astype(F32)
    marks = jnp.pad(key_hot, ((0, 0), (HEAD_DIM, HEAD_DIM - key_hot.shape[1]))).astype(BF16)
    own_hot = segment_hot(index, tables).astype(F32)
    reach = jnp.sum(own_hot[:, :, None] * tables[2][None], axis=1)
    bars = jnp.pad((reach - 1.0) * BIG, ((0, 0), (HEAD_DIM, HEAD_DIM - reach.shape[1]))).astype(BF16)

    def exchange(value, axes):
        return lax.all_to_all(value, axes, split_axis=0, concat_axis=0, tiled=True)

    def to_features(value):
        value = lax.all_to_all(value.reshape(own, rows, -1).transpose(1, 0, 2), ROW, split_axis=0, concat_axis=0)
        return value.reshape(rows * own, -1)

    joint_blocks = gather(joint_weight, ALL_COL).reshape(columns, D, -1)
    gains = jnp.broadcast_to(jnp.stack([attention_gain, feed_gain])[None], (rows, 2, attention_gain.shape[0]))
    extended = jnp.concatenate([tokens.reshape(rows, own, -1), jnp.pad(gains, ((0, 0), (0, 14), (0, 0)))], axis=1)
    extended = exchange(extended, ROW)

    x, normed_one, joint_full, packed, gains = project_in(extended, joint_blocks, cosines, sines, bars)
    packed = exchange(packed, "core").reshape(held, -1)
    wide = groups * REPEAT * 2 * HEAD_DIM
    pieces = []
    state = None
    ahead, behind = ring_steps(columns)
    value = packed[:, wide:]
    to_next, to_last = lax.ppermute(value, RING, ahead), lax.ppermute(value, RING, behind)
    fronts, backs = [], []

    def attend(state, places, some, ends):
        keys_here = jnp.concatenate([key_index[i * held // 2 : j * held // 2] for i, j in places])
        marks_here = jnp.concatenate([marks[i * held // 2 : j * held // 2] for i, j in places])
        lists_here, counts_here = block_lists(first, keys_here, block, held, tables)
        return tuple(attention_stage(lists_here, counts_here, packed, some, marks_here, state, ends))

    middle = held // 2
    for step in range(1, columns):
        fronts.append(to_next)
        backs.append(to_last)
        if step < columns - 1:
            further = (lax.ppermute(to_next, RING, ahead), lax.ppermute(to_last, RING, behind))
        else:
            further = (lax.ppermute(to_next[:middle], RING, ahead), lax.ppermute(to_last[middle:], RING, behind))
        far = 2 * (2 * columns - step)
        places, some = [(2 * step, 2 * step + 2), (far, far + 2)], [to_last, to_next]
        if step == 1:
            places, some = [(0, 2), *places], [value, *some]
        state = attend(state, places, some, False)
        state, further = lax.optimization_barrier((state, further))
        to_next, to_last = further
    pieces = [value, *backs, to_next, to_last, *reversed(fronts)]
    cotangent, to_next = lax.optimization_barrier((cotangent, to_next))
    state = attend(state, [(2 * columns, 2 * columns + 2)], [to_next, to_last], True)
    attended, lse = lax.cond(
        jnp.any(state[1] != state[1]),
        lambda: tuple(attention_forward(lists, counts, packed, pieces, marks)),
        lambda: tuple(state),
    )
    attended_rows = exchange(attended.reshape(cores, own, -1), "core")

    width = gate_weight.shape[1]
    part = feed_part(width)
    padding = jnp.zeros((output_weight.shape[1], -output_weight.shape[0] % part), BF16)
    late = jnp.concatenate([gate_weight, up_weight, down_weight.T, output_weight.T, padding], axis=1)
    late = gather(late, ALL_COL).reshape(columns, D, -1)
    upstream = exchange(cotangent.reshape(rows, own, -1), ROW).transpose(1, 0, 2).reshape(own, D)
    attended_rows, hidden, normed_two, output_full = project_out(attended_rows, late, x, gains, ATT // columns, late.shape[2] - 3 * width)
    mixed, gate_back, up_back, feed_out, normed_two_back = feed_forward(normed_two, upstream, late, width)
    layer_output = to_features((hidden + feed_out).astype(BF16))

    steps = jnp.arange(2 * columns, dtype=jnp.int32)
    plain = jnp.concatenate([steps // 2, steps % 2, jnp.zeros((1,), jnp.int32)])

    def scatter_gradient(left, *rights, sums=None):
        [parts] = gradient_parts(plain, left, *rights, sums=sums, joined=True)
        return scatter(parts.reshape(-1, parts.shape[3]), ALL_COL).astype(F32)

    def ring_gradient(left, *rights, sums=None):
        mine, other = gradient_parts(order, left, *rights, sums=sums)
        other = lax.ppermute(other, "core", [(0, 1), (1, 0)])

        def part(s, half):
            return halves(mine[s], half).astype(F32) + halves(other[s], half).astype(F32)

        return RingScatter(part, columns)

    down_gradient = scatter_gradient(upstream, mixed).T
    pair_gradient = scatter_gradient(normed_two, gate_back, up_back)
    hidden_back, hidden_low, heads_back, gain_two_part = output_back(normed_two_back, hidden, upstream, gains, output_full)
    output_summed = scatter_gradient(hidden_low, attended_rows, sums=gain_two_part[0])

    heads_back = exchange(heads_back, "core").reshape(held, -1)
    query_backs, pair_rings = [], []
    for g in range(groups):
        heads_back = depart(heads_back, pair_rings)
        query_back, pair_back = attention_backward(g, lists, counts, packed, heads_back, attended, pieces, marks, lse)
        pair_back = pair_back.reshape(2 * columns, held, -1)
        query_backs.append(query_back)
        pair_rings.append(RingScatter(lambda s, half, v=pair_back: halves(v[s], half).astype(F32), columns))
    held_pairs = jnp.concatenate([ring.finish().astype(BF16) for ring in pair_rings], axis=1)
    back = jnp.concatenate([*query_backs, held_pairs], axis=1).reshape(cores, own, -1)
    back = exchange(back, "core")
    joint_low, input_part, gain_one_part = joint_back(back, cosines, sines, joint_full, x, gains, hidden_back, rows)
    joint_ring = ring_gradient(normed_one, joint_low, sums=gain_one_part[0])
    input_gradient = exchange(input_part, ROW).reshape(rows * own, -1).astype(F32)
    joint_summed = joint_ring.finish()
    features = D // rows

    def carried(summed):
        lines = -(-features // summed.shape[1])
        return summed[features : features + lines, : features // lines].reshape(-1)

    return (
        layer_output,
        input_gradient,
        carried(joint_summed),
        joint_summed[:features],
        output_summed[:features].T,
        carried(output_summed),
        pair_gradient[:, :width],
        pair_gradient[:, width:],
        down_gradient,
    )


def solution(mesh):
    leaves, rows, columns = (mesh.shape[name] for name in ("leaf", "row", "col"))
    split = Mesh(mesh.devices.reshape(leaves, rows // 2, 2, columns), ("leaf", "high", "core", "col"))
    return jax.shard_map(
        per_device,
        mesh=split,
        in_specs=(
            P(("leaf", "col"), ROW),
            P(ROW),
            P(ROW, "col"),
            P("col", ROW),
            P(ROW),
            P(ROW, "col"),
            P(ROW, "col"),
            P("col", ROW),
            P(("leaf", "col"), ROW),
            P("leaf"),
            P("leaf"),
        ),
        out_specs=(
            P(("leaf", "col"), ROW),
            P(("leaf", "col"), ROW),
            P(("leaf", *ROW)),
            P(("leaf", *ROW), "col"),
            P(("leaf", "col"), ROW),
            P(("leaf", *ROW)),
            P(("leaf", *ROW), "col"),
            P(("leaf", *ROW), "col"),
            P(("leaf", "col"), ROW),
        ),
        check_vma=False,
    )
```

```python
import functools

import jax
import jax.numpy as jnp
from jax import lax
from jax.experimental import pallas as pl
from jax.experimental.pallas import tpu as pltpu
from jax.sharding import Mesh
from jax.sharding import PartitionSpec as P

D = 1152
HEADS = 18
KV_HEADS = 6
HEAD_DIM = 64
REPEAT = HEADS // KV_HEADS
ATT = HEADS * HEAD_DIM
KEYS = KV_HEADS * HEAD_DIM

EPSILON = 1e-05
THETA = 10000.0
BIG = 2.0**30
LOG2E = 1.4426950408889634
UNROLL = 8
BF16 = jnp.bfloat16
F32 = jnp.float32
NT = (((1,), (1,)), ((), ()))
NN = (((1,), (0,)), ((), ()))


def dg(a, b, dims):
    return lax.dot_general(a, b, dims, preferred_element_type=F32)


def tree_tables(segment_lengths, parents):
    count = segment_lengths.shape[0]
    labels = jnp.arange(count, dtype=jnp.int32)
    ends = jnp.sum(jnp.where(labels[None, :] <= labels[:, None], segment_lengths[None, :], 0), axis=1)
    starts = ends - segment_lengths
    parent_hot = parents[:, None] == labels[None, :]
    grand = jnp.sum(jnp.where(parent_hot, parents[None, :], 0), axis=1)
    self_mark = labels[:, None] == labels[None, :]
    grand_mark = grand[:, None] == labels[None, :]
    ancestry = (self_mark | parent_hot | grand_mark).astype(F32)
    strict = (parent_hot | grand_mark) & jnp.logical_not(self_mark)
    offsets = jnp.sum(jnp.where(strict, segment_lengths[None, :], 0), axis=1)
    return (ends, starts, ancestry, offsets)


def segment_hot(index, tables):
    ends, starts, _, _ = tables
    return (index[:, None] >= starts[None, :]) & (index[:, None] < ends[None, :])


def rotary_tables(index, tables):
    hot = segment_hot(index, tables)
    depth = index + jnp.sum(jnp.where(hot, (tables[3] - tables[1])[None, :], 0), axis=1)
    half = HEAD_DIM // 2
    rates = THETA ** (-jnp.arange(half, dtype=F32) / half)
    angles = depth.astype(F32)[:, None] * rates[None, :]
    cosines, sines = jnp.cos(angles), jnp.sin(angles)
    return (jnp.concatenate([cosines] * 4, axis=1), jnp.concatenate([-sines, sines] * 2, axis=1))


def block_lists(first, key_index, block, held, tables):
    ends, starts, ancestry, _ = tables
    blocks = held // block
    key_low = key_index[::block]
    labels = jnp.arange(key_low.shape[0], dtype=jnp.int32)
    low = first + jnp.arange(blocks, dtype=jnp.int32) * block
    high = low + block
    query_has = ((starts[None, :] < high[:, None]) & (ends[None, :] > low[:, None])).astype(F32)
    key_has = ((starts[None, :] < key_low[:, None] + block) & (ends[None, :] > key_low[:, None])).astype(F32)
    reach = jnp.sum(query_has[:, :, None] * ancestry[None], axis=1)
    seen = jnp.sum(reach[:, None, :] * key_has[None], axis=2) > 0.5
    seen = seen & (key_low[None, :] < low[:, None])
    before = labels[None, :] < labels[:, None]
    rank = jnp.sum((seen[:, None, :] & before[None]).astype(jnp.int32), axis=2)
    place = seen[:, None, :] & (rank[:, None, :] == labels[None, :, None])
    lists = jnp.sum(jnp.where(place, labels[None, None, :], 0), axis=2)
    counts = jnp.sum(seen.astype(jnp.int32), axis=1)
    own = jnp.sum(jnp.where(key_low[None, :] == low[:, None], labels[None, :], 0), axis=1)
    lists = jnp.where(labels[None, :] == counts[:, None], own[:, None], lists)
    return (lists.reshape(-1).astype(jnp.int32), counts.astype(jnp.int32))


def cascade(count, unroll, steps):
    def body(i, c):
        steps(i * unroll, unroll)
        return c

    whole = count // unroll
    lax.fori_loop(0, whole, body, 0)
    start = whole * unroll
    size = unroll // 2
    while size:
        some = ((count - start) // size) > 0
        pl.when(some)(functools.partial(steps, start, size))
        start = start + jnp.where(some, size, 0)
        size //= 2


def causal(scores, heads):
    rows = lax.broadcasted_iota(jnp.int32, scores.shape, 0)
    columns = lax.rem(lax.broadcasted_iota(jnp.int32, scores.shape, 1), scores.shape[1] // heads)
    return jnp.where(rows <= columns, scores, -BIG)


def stacked(ref):
    value, wide = ref[...], 2 * HEAD_DIM
    return jnp.concatenate([value[:, h * wide : (h + 1) * wide] for h in range(value.shape[1] // wide)], axis=0)


def beside(value, heads):
    rows = value.shape[0] // heads
    return jnp.concatenate([value[h * rows : (h + 1) * rows] for h in range(heads)], axis=1)


def left_half(shape):
    return lax.broadcasted_iota(jnp.int32, shape, 1) < HEAD_DIM


def fetch(pieces, group, kv_ref, sems):
    copies, start = [], 0
    for i, piece in enumerate(pieces):
        lanes = pl.ds(pl.multiple_of(group * 2 * HEAD_DIM, 2 * HEAD_DIM), 2 * HEAD_DIM)
        target = kv_ref.at[pl.ds(start, piece.shape[0])]
        copies.append(pltpu.make_async_copy(piece.at[:, lanes], target, sems.at[i]))
        start += piece.shape[0]
    for copy in copies:
        copy.start()
    for copy in copies:
        copy.wait()


def forward_kernel(lists, counts, q_ref, mark_ref, *refs):
    *pieces, o_ref, lse_ref, top_ref, sum_ref, kv_ref, vt_ref, sems = refs
    block = pl.program_id(1)
    heads, rows = q_ref.shape[1] // (2 * HEAD_DIM), q_ref.shape[0]
    total = kv_ref.shape[0]
    stride = total // rows
    count = counts[block]

    @pl.when(block == 0)
    def _():
        fetch(pieces, pl.program_id(0), kv_ref, sems)

        def flip(i, c):
            k0 = pl.multiple_of(i * rows, rows)
            turned = kv_ref[pl.ds(k0, rows), :].T
            vt_ref[:HEAD_DIM, pl.ds(k0, rows)] = turned[HEAD_DIM:]
            return c

        lax.fori_loop(0, stride, flip, 0)
        tail = (vt_ref.shape[0] - HEAD_DIM, total)
        vt_ref[HEAD_DIM:] = jnp.where(lax.broadcasted_iota(jnp.int32, tail, 0) == 0, 1.0, 0.0).astype(BF16)

    def queries():
        return stacked(q_ref)

    def blocks(start, n):
        offs = [pl.multiple_of(lists[block * stride + start + u] * rows, rows) for u in range(n)]
        kv = jnp.concatenate([kv_ref[pl.ds(k0, rows), :] for k0 in offs], axis=0)
        mark = jnp.concatenate([mark_ref[pl.ds(k0, rows), :] for k0 in offs], axis=0)
        vt = jnp.concatenate([vt_ref[:, pl.ds(k0, rows)] for k0 in offs], axis=1)
        return jnp.where(left_half(kv.shape), kv, mark), vt

    def begin():
        k, vt = blocks(count, 1)
        scores = causal(dg(k, queries(), NT), heads)
        top = jnp.max(scores, axis=0, keepdims=True)
        top_ref[...] = top
        sum_ref[...] = dg(vt, jnp.exp2(scores - top).astype(BF16), NN)

    def steps(start, n):
        k, vt = blocks(start, n)
        weights = jnp.exp2(dg(k, queries(), NT) - top_ref[...]).astype(BF16)
        sum_ref[...] += dg(vt, weights, NN)

    begin()
    cascade(count, UNROLL, steps)

    @pl.when(jnp.logical_not(jnp.max(sum_ref[HEAD_DIM : HEAD_DIM + 1, :]) < 2.0**100))
    def _():
        begin()

        def online(n, c):
            k, vt = blocks(n, 1)
            scores = dg(k, queries(), NT)
            old = top_ref[...]
            new = jnp.maximum(old, jnp.max(scores, axis=0, keepdims=True))
            top_ref[...] = new
            sum_ref[...] = sum_ref[...] * jnp.exp2(old - new) + dg(vt, jnp.exp2(scores - new).astype(BF16), NN)
            return c

        lax.fori_loop(0, count, online, 0)

    total_row = sum_ref[HEAD_DIM : HEAD_DIM + 1, :]
    spread = jnp.concatenate([jnp.zeros((HEAD_DIM, heads * rows), F32), sum_ref[:HEAD_DIM, :] / total_row], axis=0)
    o_ref[...] = beside(spread.T.astype(BF16), heads)
    lse_ref[0, 0] = top_ref[...] + jnp.log2(total_row)


def attention_forward(lists, counts, q, pieces, marks):
    tokens, wide, heads = q.shape[0], 2 * HEAD_DIM, REPEAT
    groups = q.shape[1] // (wide * heads)
    total = marks.shape[0]
    blocks = counts.shape[0]
    rows = tokens // blocks
    tall = HEAD_DIM + 16
    return pl.pallas_call(
        forward_kernel,
        grid_spec=pltpu.PrefetchScalarGridSpec(
            num_scalar_prefetch=2,
            grid=(groups, blocks),
            in_specs=[
                pl.BlockSpec((rows, heads * wide), lambda g, b, *_: (b, g)),
                pl.BlockSpec((total, wide), lambda g, b, *_: (0, 0)),
                *(pl.BlockSpec(memory_space=pl.ANY) for _ in pieces),
            ],
            out_specs=[
                pl.BlockSpec((rows, heads * wide), lambda g, b, *_: (b, g)),
                pl.BlockSpec((1, 1, 1, heads * rows), lambda g, b, *_: (g, b, 0, 0)),
            ],
            scratch_shapes=[
                pltpu.VMEM((1, heads * rows), F32),
                pltpu.VMEM((tall, heads * rows), F32),
                pltpu.VMEM((total, wide), BF16),
                pltpu.VMEM((tall, total), BF16),
                pltpu.SemaphoreType.DMA((len(pieces),)),
            ],
        ),
        out_shape=[
            jax.ShapeDtypeStruct((tokens, groups * heads * wide), BF16),
            jax.ShapeDtypeStruct((groups, blocks, 1, heads * rows), F32),
        ],
        compiler_params=pltpu.CompilerParams(vmem_limit_bytes=48 * 2**20),
        cost_estimate=pl.CostEstimate(
            flops=groups * heads * tokens * total * 256, bytes_accessed=groups * total * 512, transcendentals=0
        ),
        name="attention_forward",
    )(lists, counts, q, marks, *pieces)


def stage_kernel(begins, ends, lists, counts, q_ref, mark_ref, *refs):
    refs = list(refs)
    sums_in, tops_in = ([refs.pop(0), refs.pop(0)] if not begins else (None, None))
    *pieces, first_ref, second_ref, top_ref, sum_ref, kv_ref, vt_ref, sems = refs
    block = pl.program_id(1)
    heads, rows = q_ref.shape[1] // (2 * HEAD_DIM), q_ref.shape[0]
    total = kv_ref.shape[0]
    stride = total // rows
    count = counts[block]

    @pl.when(block == 0)
    def _():
        fetch(pieces, pl.program_id(0), kv_ref, sems)

        def flip(i, c):
            k0 = pl.multiple_of(i * rows, rows)
            turned = kv_ref[pl.ds(k0, rows), :].T
            vt_ref[:HEAD_DIM, pl.ds(k0, rows)] = turned[HEAD_DIM:]
            return c

        lax.fori_loop(0, stride, flip, 0)
        tail = (vt_ref.shape[0] - HEAD_DIM, total)
        vt_ref[HEAD_DIM:] = jnp.where(lax.broadcasted_iota(jnp.int32, tail, 0) == 0, 1.0, 0.0).astype(BF16)

    def queries():
        return stacked(q_ref)

    def blocks(start, n):
        offs = [pl.multiple_of(lists[block * stride + start + u] * rows, rows) for u in range(n)]
        kv = jnp.concatenate([kv_ref[pl.ds(k0, rows), :] for k0 in offs], axis=0)
        mark = jnp.concatenate([mark_ref[pl.ds(k0, rows), :] for k0 in offs], axis=0)
        vt = jnp.concatenate([vt_ref[:, pl.ds(k0, rows)] for k0 in offs], axis=1)
        return jnp.where(left_half(kv.shape), kv, mark), vt

    if begins:
        k, vt = blocks(count, 1)
        scores = causal(dg(k, queries(), NT), heads)
        top = jnp.max(scores, axis=0, keepdims=True)
        top_ref[...] = top
        sum_ref[...] = dg(vt, jnp.exp2(scores - top).astype(BF16), NN)
    else:
        top_ref[...] = tops_in[0, 0]
        sum_ref[...] = sums_in[0, 0]

    def steps(start, n):
        k, vt = blocks(start, n)
        weights = jnp.exp2(dg(k, queries(), NT) - top_ref[...]).astype(BF16)
        sum_ref[...] += dg(vt, weights, NN)

    cascade(count, UNROLL, steps)
    if ends:
        total_row = sum_ref[HEAD_DIM : HEAD_DIM + 1, :]
        spread = jnp.concatenate([jnp.zeros((HEAD_DIM, heads * rows), F32), sum_ref[:HEAD_DIM, :] / total_row], axis=0)
        first_ref[...] = beside(spread.T.astype(BF16), heads)
        second_ref[0, 0] = jnp.where(total_row < 2.0**100, top_ref[...] + jnp.log2(total_row), jnp.nan)
    else:
        first_ref[0, 0] = sum_ref[...]
        second_ref[0, 0] = top_ref[...]


def attention_stage(lists, counts, q, pieces, marks, state, ends):
    tokens, wide, heads = q.shape[0], 2 * HEAD_DIM, REPEAT
    groups = q.shape[1] // (wide * heads)
    total = marks.shape[0]
    blocks = counts.shape[0]
    rows = tokens // blocks
    tall = HEAD_DIM + 16
    lanes = heads * rows
    held_specs = [
        pl.BlockSpec((1, 1, tall, lanes), lambda g, b, *_: (g, b, 0, 0)),
        pl.BlockSpec((1, 1, 1, lanes), lambda g, b, *_: (g, b, 0, 0)),
    ]
    tops = jax.ShapeDtypeStruct((groups, blocks, 1, lanes), F32)
    if ends:
        out_specs = [pl.BlockSpec((rows, heads * wide), lambda g, b, *_: (b, g)), held_specs[1]]
        out_shape = [jax.ShapeDtypeStruct((tokens, groups * heads * wide), BF16), tops]
    else:
        out_specs = held_specs
        out_shape = [jax.ShapeDtypeStruct((groups, blocks, tall, lanes), F32), tops]
    return pl.pallas_call(
        functools.partial(stage_kernel, state is None, ends),
        grid_spec=pltpu.PrefetchScalarGridSpec(
            num_scalar_prefetch=2,
            grid=(groups, blocks),
            in_specs=[
                pl.BlockSpec((rows, heads * wide), lambda g, b, *_: (b, g)),
                pl.BlockSpec((total, wide), lambda g, b, *_: (0, 0)),
                *([] if state is None else held_specs),
                *(pl.BlockSpec(memory_space=pl.ANY) for _ in pieces),
            ],
            out_specs=out_specs,
            scratch_shapes=[
                pltpu.VMEM((1, lanes), F32),
                pltpu.VMEM((tall, lanes), F32),
                pltpu.VMEM((total, wide), BF16),
                pltpu.VMEM((tall, total), BF16),
                pltpu.SemaphoreType.DMA((len(pieces),)),
            ],
        ),
        out_shape=out_shape,
        compiler_params=pltpu.CompilerParams(vmem_limit_bytes=40 * 2**20),
        cost_estimate=pl.CostEstimate(
            flops=groups * heads * tokens * total * 256, bytes_accessed=groups * total * 512, transcendentals=0
        ),
        name="attention_stage",
    )(lists, counts, q, marks, *(() if state is None else state), *pieces)


def backward_kernel(group, lists, counts, q_ref, do_ref, o_ref, mark_ref, lse_ref, *refs):
    *pieces, dq_ref, dkv_ref, dq_sum, dkv_sum, kv_ref, kt_ref, delta_ref, sems = refs
    block = pl.program_id(0)
    heads, rows = q_ref.shape[1] // (2 * HEAD_DIM), q_ref.shape[0]
    total = kv_ref.shape[0]
    stride = total // rows
    count = counts[block]

    @pl.when(block == 0)
    def _():
        dkv_sum[...] = jnp.zeros(dkv_sum.shape, F32)
        fetch(pieces, group, kv_ref, sems)

        def flip(i, c):
            k0 = pl.multiple_of(i * rows, rows)
            turned = kv_ref[pl.ds(k0, rows), :].T
            kt_ref[:, pl.ds(k0, rows)] = turned[:HEAD_DIM]
            return c

        lax.fori_loop(0, stride, flip, 0)

    dq_sum[...] = jnp.zeros(dq_sum.shape, F32)
    products = stacked(do_ref).astype(F32) * stacked(o_ref).astype(F32)
    delta_ref[...] = jnp.sum(products.T, axis=0, keepdims=True)

    def steps(start, n, masked):
        q, do = stacked(q_ref), stacked(do_ref)
        offs = [pl.multiple_of(lists[block * stride + start + u] * rows, rows) for u in range(n)]
        kv = jnp.concatenate([kv_ref[pl.ds(k0, rows), :] for k0 in offs], axis=0)
        mark = jnp.concatenate([mark_ref[pl.ds(k0, rows), :] for k0 in offs], axis=0)
        kt = jnp.concatenate([kt_ref[:, pl.ds(k0, rows)] for k0 in offs], axis=1)
        scores = dg(jnp.where(left_half(kv.shape), kv, mark), q, NT) - lse_ref[0, 0]
        if masked:
            scores = causal(scores, heads)
        chances = jnp.exp2(scores)
        back = dg(kv, do, NT) - delta_ref[...]
        score_back = (chances * back).astype(BF16)
        only_q = jnp.where(left_half(q.shape), q, jnp.zeros_like(q))
        update = dg(score_back, only_q, NN) + dg(chances.astype(BF16), do, NN)
        dq_sum[...] += dg(kt, score_back, NN)
        for u in range(n):
            dkv_sum[pl.ds(offs[u], rows), :] += update[u * rows : (u + 1) * rows]

    steps(count, 1, True)
    cascade(count, UNROLL, lambda start, n: steps(start, n, False))
    spread = jnp.concatenate([dq_sum[...] * HEAD_DIM**-0.5, jnp.zeros(dq_sum.shape, F32)], axis=0)
    dq_ref[...] = beside(spread.T.astype(BF16), heads)

    @pl.when(block == pl.num_programs(0) - 1)
    def _():
        summed = dkv_sum[...]
        dkv_ref[...] = jnp.where(left_half(summed.shape), summed * (1.0 / LOG2E), summed).astype(BF16)


def attention_backward(group, lists, counts, q, do, o, pieces, marks, lse):
    tokens, wide, heads = q.shape[0], 2 * HEAD_DIM, REPEAT
    total = marks.shape[0]
    blocks = counts.shape[0]
    rows = tokens // blocks
    block = pl.BlockSpec((rows, heads * wide), lambda b, *_: (b, group))
    return pl.pallas_call(
        functools.partial(backward_kernel, group),
        grid_spec=pltpu.PrefetchScalarGridSpec(
            num_scalar_prefetch=2,
            grid=(blocks,),
            in_specs=[
                block,
                block,
                block,
                pl.BlockSpec((total, wide), lambda b, *_: (0, 0)),
                pl.BlockSpec((1, 1, 1, heads * rows), lambda b, *_: (group, b, 0, 0)),
                *(pl.BlockSpec(memory_space=pl.ANY) for _ in pieces),
            ],
            out_specs=[
                pl.BlockSpec((rows, heads * wide), lambda b, *_: (b, 0)),
                pl.BlockSpec((total, wide), lambda b, *_: (0, 0)),
            ],
            scratch_shapes=[
                pltpu.VMEM((HEAD_DIM, heads * rows), F32),
                pltpu.VMEM((total, wide), F32),
                pltpu.VMEM((total, wide), BF16),
                pltpu.VMEM((HEAD_DIM, total), BF16),
                pltpu.VMEM((1, heads * rows), F32),
                pltpu.SemaphoreType.DMA((len(pieces),)),
            ],
        ),
        out_shape=[
            jax.ShapeDtypeStruct((tokens, heads * wide), BF16),
            jax.ShapeDtypeStruct((total, wide), BF16),
        ],
        compiler_params=pltpu.CompilerParams(vmem_limit_bytes=60 * 2**20),
        cost_estimate=pl.CostEstimate(flops=heads * tokens * total * 640, bytes_accessed=total * 1024, transcendentals=0),
        name="attention_backward",
    )(lists, counts, q, do, o, marks, lse, *pieces)


def roll_half(value):
    return pltpu.roll(value, HEAD_DIM, 1)


def swap_quarters(value):
    quarter = HEAD_DIM // 2
    lane = lax.broadcasted_iota(jnp.int32, value.shape, 1)
    first = lax.rem(lane, HEAD_DIM) < quarter
    return jnp.where(first, pltpu.roll(value, value.shape[1] - quarter, 1), pltpu.roll(value, quarter, 1))


def root_mean(value):
    return lax.rsqrt(jnp.sum(value * value, axis=1, keepdims=True) / D + EPSILON)


def project_kernel(x4_ref, w_ref, cos_ref, sin_ref, bars_ref, x_ref, xa_ref, full_ref, query_ref, pair_ref, gains_ref, joint_ref):
    own = x_ref.shape[0]
    wide = 2 * HEAD_DIM
    x = jnp.concatenate([x4_ref[r, :own, :] for r in range(x4_ref.shape[0])], axis=1)
    gains = jnp.concatenate([x4_ref[r, own : own + 16, :] for r in range(x4_ref.shape[0])], axis=1).astype(F32)
    x_ref[...] = x
    gains_ref[...] = gains[:8]
    value = x.astype(F32)
    xa_ref[...] = (value * root_mean(value) * gains[0:1]).astype(BF16)
    full_ref[...] = jnp.concatenate([w_ref[c] for c in range(w_ref.shape[0])], axis=1)
    joint_ref[...] = dg(xa_ref[...], full_ref[...], NN).astype(BF16)
    left = left_half((own, wide))
    bars = bars_ref[...].astype(F32)
    heads, pairs = HEADS // 2, KV_HEADS // 2

    def part(i):
        return joint_ref[:, i * wide : (i + 1) * wide].astype(F32)

    def turned(i):
        value = part(i)
        return value * cos_ref[...] + swap_quarters(value) * sin_ref[...]

    for i in range(HEADS // 2):
        value = turned(i) * (LOG2E * HEAD_DIM**-0.5)
        for j, head in ((2 * i, value), (2 * i + 1, roll_half(value))):
            start = (j % heads) * wide
            query_ref[j // heads, :, start : start + wide] = jnp.where(left, head, bars).astype(BF16)
    for i in range(KV_HEADS // 2):
        key = turned(HEADS // 2 + i)
        value = part(HEADS // 2 + KV_HEADS // 2 + i)
        for j, both in (
            (2 * i, jnp.where(left, key, roll_half(value))),
            (2 * i + 1, jnp.where(left, roll_half(key), value)),
        ):
            start = (j % pairs) * wide
            pair_ref[j // pairs, :, start : start + wide] = both.astype(BF16)


def project_in(x4, weight, cosines, sines, bars):
    own = cosines.shape[0]
    shapes = [
        jax.ShapeDtypeStruct((own, D), BF16),
        jax.ShapeDtypeStruct((own, D), BF16),
        jax.ShapeDtypeStruct((D, ATT + 2 * KEYS), BF16),
        jax.ShapeDtypeStruct((2, own, ATT), BF16),
        jax.ShapeDtypeStruct((2, own, KEYS), BF16),
        jax.ShapeDtypeStruct((8, D), F32),
    ]
    return pl.pallas_call(
        project_kernel,
        out_shape=shapes,
        scratch_shapes=[pltpu.VMEM((own, ATT + 2 * KEYS), BF16)],
        compiler_params=pltpu.CompilerParams(vmem_limit_bytes=56 * 2**20),
        cost_estimate=pl.CostEstimate(flops=2 * own * D * (ATT + 2 * KEYS), bytes_accessed=2**24, transcendentals=0),
        name="project_in",
    )(x4, weight, cosines, sines, bars)


def output_kernel(width, o_ref, w_ref, x_ref, gains_ref, rows_ref, hidden_ref, normed_ref, full_ref):
    wide = 2 * HEAD_DIM
    heads = HEADS // 2
    left = left_half((x_ref.shape[0], wide))
    for i in range(HEADS // 2):
        first, second = (
            o_ref[j // heads, :, (j % heads) * wide : (j % heads + 1) * wide] for j in (2 * i, 2 * i + 1)
        )
        first = roll_half(first.astype(F32))
        rows_ref[:, i * wide : (i + 1) * wide] = jnp.where(left, first, second.astype(F32)).astype(BF16)
    full_ref[...] = jnp.concatenate([w_ref[c, :, :width] for c in range(w_ref.shape[0])], axis=1)
    hidden = x_ref[...].astype(F32) + dg(rows_ref[...], full_ref[...], NT)
    hidden_ref[...] = hidden
    normed_ref[...] = (hidden * root_mean(hidden) * gains_ref[1:2]).astype(BF16)


def project_out(o, late, x, gains, width, padded):
    own = x.shape[0]
    place = late.shape[2] // padded - 1
    return pl.pallas_call(
        functools.partial(output_kernel, width),
        grid=(1,),
        in_specs=[
            pl.BlockSpec(o.shape, lambda i: (0, 0, 0)),
            pl.BlockSpec((late.shape[0], D, padded), lambda i: (0, 0, place)),
            pl.BlockSpec(x.shape, lambda i: (0, 0)),
            pl.BlockSpec(gains.shape, lambda i: (0, 0)),
        ],
        out_specs=[pl.BlockSpec((own, D), lambda i: (0, 0))] * 3 + [pl.BlockSpec((D, ATT), lambda i: (0, 0))],
        out_shape=[
            jax.ShapeDtypeStruct((own, ATT), BF16),
            jax.ShapeDtypeStruct((own, D), F32),
            jax.ShapeDtypeStruct((own, D), BF16),
            jax.ShapeDtypeStruct((D, ATT), BF16),
        ],
        compiler_params=pltpu.CompilerParams(vmem_limit_bytes=56 * 2**20),
        cost_estimate=pl.CostEstimate(flops=2 * own * D * ATT, bytes_accessed=2**24, transcendentals=0),
        name="project_out",
    )(o, late, x, gains)


def norm_back(upstream, value, gain):
    scale = root_mean(value)
    weighted = upstream * gain
    inner = jnp.sum(weighted * value, axis=1, keepdims=True)
    gain_back = jnp.sum(upstream * value * scale, axis=0, keepdims=True)
    return scale * weighted - value * (scale * scale * scale * inner / D), gain_back


def output_back_kernel(back_ref, hidden_ref, upstream_ref, gains_ref, full_ref, hidden_back_ref, low_ref, do_ref, sums_ref):
    wide = 2 * HEAD_DIM
    heads = HEADS // 2
    part, sums = norm_back(back_ref[...], hidden_ref[...], gains_ref[1:2])
    hidden_back = upstream_ref[...].astype(F32) + part
    hidden_back_ref[...] = hidden_back
    low_ref[...] = hidden_back.astype(BF16)
    sums_ref[...] = jnp.broadcast_to(sums, sums_ref.shape)
    attended_back = dg(low_ref[...], full_ref[...], NN)
    left = left_half((low_ref.shape[0], wide))
    for i in range(HEADS // 2):
        value = attended_back[:, i * wide : (i + 1) * wide]
        for j, head in ((2 * i, roll_half(value)), (2 * i + 1, value)):
            start = (j % heads) * wide
            do_ref[j // heads, :, start : start + wide] = jnp.where(left, 0.0, head).astype(BF16)


def output_back(back, hidden, upstream, gains, full):
    own = back.shape[0]
    return pl.pallas_call(
        output_back_kernel,
        out_shape=[
            jax.ShapeDtypeStruct((own, D), F32),
            jax.ShapeDtypeStruct((own, D), BF16),
            jax.ShapeDtypeStruct((2, own, ATT), BF16),
            jax.ShapeDtypeStruct((8, D), F32),
        ],
        compiler_params=pltpu.CompilerParams(vmem_limit_bytes=56 * 2**20),
        cost_estimate=pl.CostEstimate(flops=2 * own * D * ATT, bytes_accessed=2**24, transcendentals=0),
        name="output_back",
    )(back, hidden, upstream, gains, full)


def joint_back_kernel(query_ref, pair_ref, cos_ref, sin_ref, full_ref, x_ref, gains_ref, hidden_back_ref, joint_ref, out_ref, sums_ref):
    wide = 2 * HEAD_DIM
    heads, pairs = HEADS // 2, KV_HEADS // 2
    left = left_half((x_ref.shape[0], wide))

    def queries(j):
        return query_ref[j // heads, :, (j % heads) * wide : (j % heads + 1) * wide].astype(F32)

    def both(j):
        start = (j % pairs) * wide
        return pair_ref[j // pairs, :, start : start + wide].astype(F32)

    def store(i, value):
        joint_ref[:, i * wide : (i + 1) * wide] = value.astype(BF16)

    def back(value):
        return value * cos_ref[...] - swap_quarters(value) * sin_ref[...]

    for i in range(HEADS // 2):
        store(i, back(jnp.where(left, queries(2 * i), roll_half(queries(2 * i + 1)))))
    for i in range(KV_HEADS // 2):
        first, second = both(2 * i), both(2 * i + 1)
        store(HEADS // 2 + i, back(jnp.where(left, first, roll_half(second))))
        store(HEADS // 2 + KV_HEADS // 2 + i, jnp.where(left, roll_half(first), second))
    upstream = dg(joint_ref[...], full_ref[...], NT)
    part, sums = norm_back(upstream, x_ref[...].astype(F32), gains_ref[0:1])
    total = (hidden_back_ref[...] + part).astype(BF16)
    features = out_ref.shape[2]
    for r in range(out_ref.shape[0]):
        out_ref[r] = total[:, r * features : (r + 1) * features]
    sums_ref[...] = jnp.broadcast_to(sums, sums_ref.shape)


def joint_back(queries, pairs, cosines, sines, full, x, gains, hidden_back, rows):
    own = x.shape[0]
    return pl.pallas_call(
        joint_back_kernel,
        out_shape=[
            jax.ShapeDtypeStruct((own, ATT + 2 * KEYS), BF16),
            jax.ShapeDtypeStruct((rows, own, D // rows), BF16),
            jax.ShapeDtypeStruct((8, D), F32),
        ],
        compiler_params=pltpu.CompilerParams(vmem_limit_bytes=56 * 2**20),
        cost_estimate=pl.CostEstimate(flops=2 * own * D * (ATT + 2 * KEYS), bytes_accessed=2**24, transcendentals=0),
        name="joint_back",
    )(queries, pairs, cosines, sines, full, x, gains, hidden_back)


def feed_kernel(normed_ref, back_ref, gate_ref, up_ref, down_ref, mixed_ref, gate_back_ref, up_back_ref, out_ref, normed_back_ref):
    @pl.when(pl.program_id(0) == 0)
    def _():
        out_ref[...] = jnp.zeros(out_ref.shape, F32)
        normed_back_ref[...] = jnp.zeros(normed_back_ref.shape, F32)

    gate = dg(normed_ref[...], gate_ref[0], NN)
    up_value = dg(normed_ref[...], up_ref[0], NN)
    mixed_back = dg(back_ref[...], down_ref[0], NN)
    sigmoid = jax.nn.sigmoid(gate)
    silu = gate * sigmoid
    mixed = (silu * up_value).astype(BF16)
    gate_back = (mixed_back * up_value * (sigmoid * (1.0 + gate * (1.0 - sigmoid)))).astype(BF16)
    up_back = (mixed_back * silu).astype(BF16)
    mixed_ref[...] = mixed
    gate_back_ref[...] = gate_back
    up_back_ref[...] = up_back
    out_ref[...] += dg(mixed, down_ref[0], NT)
    normed_back_ref[...] += dg(gate_back, gate_ref[0], NT) + dg(up_back, up_ref[0], NT)


def feed_forward(normed, back, late, width):
    tokens = normed.shape[0]
    columns = late.shape[0]
    whole = pl.BlockSpec((tokens, D), lambda c: (0, 0))
    blocks = [pl.BlockSpec((1, D, width), lambda c, k=k: (c, 0, k)) for k in range(3)]
    out = pl.BlockSpec((tokens, width), lambda c: (0, c))
    return pl.pallas_call(
        feed_kernel,
        grid=(columns,),
        in_specs=[whole, whole, *blocks],
        out_specs=[out, out, out, whole, whole],
        out_shape=[jax.ShapeDtypeStruct((tokens, columns * width), BF16)] * 3 + [jax.ShapeDtypeStruct((tokens, D), F32)] * 2,
        compiler_params=pltpu.CompilerParams(vmem_limit_bytes=62 * 2**20),
        cost_estimate=pl.CostEstimate(
            flops=12 * tokens * D * columns * width, bytes_accessed=6 * D * columns * width, transcendentals=0
        ),
        name="feed_forward",
    )(normed, back, late, late, late)


def gradient_kernel(counts, blocked, summed, *refs):
    refs = list(refs)
    sets = [(refs.pop(0), [refs.pop(0) for _ in range(n)]) for n in counts]
    sums_ref = refs.pop(0) if summed else None
    out_ref, turned, held = refs[0], refs[1 : 1 + len(sets)], refs[1 + len(sets) :]
    step = pl.program_id(0)
    rows = out_ref.shape[1]
    features = sets[0][0].shape[1] // rows
    rights = [right for _, some in sets for right in some]
    whole = [right for right, flag in zip(rights, blocked, strict=True) if not flag]

    @pl.when(step == 0)
    def _():
        for (left, _), target in zip(sets, turned, strict=True):
            target[...] = left[...].T
        for right, block in zip(whole, held, strict=True):
            width = block.shape[2]
            for c in range(block.shape[0]):
                block[c] = right[:, c * width : (c + 1) * width]

    spare, flags, start = list(held), list(blocked), 0
    for (_, some), target in zip(sets, turned, strict=True):
        for right in some:
            value = right[...] if flags.pop(0) else spare.pop(0)[step]
            width = value.shape[1]
            part = dg(target[...], value, NN).astype(BF16)
            for r in range(rows):
                out_ref[0, r, :, start : start + width] = part[r * features : (r + 1) * features]
            start += width
    if summed:
        tail = (rows, features, out_ref.shape[3] - start)
        out_ref[0, :, :, start:] = jnp.broadcast_to(sums_ref[...], tail).astype(BF16)


def gradient_parts(columns, rows, sums, *sets):
    tokens = sets[0][0].shape[0]
    features = D // rows
    operands, specs, turned, held, blocked, wide = [], [], [], [], [], 0
    for left, rights in sets:
        operands.append(left)
        specs.append(pl.BlockSpec(left.shape, lambda c: (0, 0)))
        turned.append(pltpu.VMEM((left.shape[1], tokens), BF16))
        for right in rights:
            width = right.shape[1] // columns
            operands.append(right)
            wide += width
            if width % 128 == 0:
                specs.append(pl.BlockSpec((tokens, width), lambda c: (0, c)))
                blocked.append(True)
            else:
                specs.append(pl.BlockSpec(right.shape, lambda c: (0, 0)))
                held.append(pltpu.VMEM((columns, tokens, width), BF16))
                blocked.append(False)
    if sums is not None:
        wide = (wide // 128 + 1) * 128
        operands.append(sums.reshape(rows, features, 1))
        specs.append(pl.BlockSpec((rows, features, 1), lambda c: (0, 0, 0)))
    shape = (columns, rows, features, wide)
    return pl.pallas_call(
        functools.partial(gradient_kernel, [len(rights) for _, rights in sets], blocked, sums is not None),
        grid=(columns,),
        in_specs=specs,
        out_specs=pl.BlockSpec((1, *shape[1:]), lambda c: (c, 0, 0, 0)),
        out_shape=jax.ShapeDtypeStruct(shape, BF16),
        scratch_shapes=[*turned, *held],
        compiler_params=pltpu.CompilerParams(vmem_limit_bytes=60 * 2**20),
        cost_estimate=pl.CostEstimate(
            flops=2 * tokens * D * wide * columns, bytes_accessed=2 * D * wide * columns, transcendentals=0
        ),
        name="gradient_parts",
    )(*operands)


ROW = ("high", "core")
ALL_ROW = ("high", "core", "col")
ALL_COL = ("col", "high", "core")
RING = ("high", "col")


def ring_steps(columns):
    path = [*range(columns), *reversed(range(columns, 2 * columns))]
    ahead = [(path[i], path[(i + 1) % len(path)]) for i in range(len(path))]
    return ahead, [(b, a) for a, b in ahead]


class RingScatter:
    def __init__(self, part, columns):
        self.part, (self.ahead, self.behind), self.count = part, ring_steps(columns), 2 * columns
        self.left = self.count // 2
        self.arrived = None
        self.ready = (part(self.left, 0).astype(BF16), part(self.left, 1).astype(BF16))

    def launch(self):
        out, back = self.ready
        self.arrived = (lax.ppermute(out, RING, self.ahead), lax.ppermute(back, RING, self.behind))
        self.ready = None
        self.left -= 1

    def prepare(self):
        out, back = self.part(self.left, None), self.part(self.count - self.left, None)
        front, rear = (v.astype(F32) for v in self.arrived)
        half = front.shape[0]
        if half == out.shape[0]:
            out, back = out + front, back + rear
        else:
            out = jnp.concatenate([out[:half] + front, out[half:]], axis=0)
            back = jnp.concatenate([back[:half], back[half:] + rear], axis=0)
        self.ready = (out.astype(BF16), back.astype(BF16))

    def finish(self):
        while self.left or self.ready:
            if self.ready is None:
                self.prepare()
            self.ready = lax.optimization_barrier(self.ready)
            self.launch()
        return self.part(0, None) + self.arrived[0].astype(F32) + self.arrived[1].astype(F32)


def after(value, rings):
    value, arrived = lax.optimization_barrier((value, [ring.arrived for ring in rings]))
    for ring, a in zip(rings, arrived, strict=True):
        ring.arrived = a
    return value


def depart(value, rings):
    rings = [ring for ring in rings if ring.left]
    for ring in rings:
        if ring.ready is None:
            ring.prepare()
    value, ready = lax.optimization_barrier((value, [ring.ready for ring in rings]))
    for ring, r in zip(rings, ready, strict=True):
        ring.ready = r
        ring.launch()
    return value


def halves(value, half):
    if half is None:
        return value
    middle = value.shape[0] // 2
    return value[middle:] if half else value[:middle]


def scatter(value, axes):
    return lax.psum_scatter(value, axes, scatter_dimension=0, tiled=True)


def gather(value, axes):
    return lax.all_gather(value, axes, axis=0, tiled=True)


def per_device(
    tokens,
    attention_gain,
    joint_weight,
    output_weight,
    feed_gain,
    gate_weight,
    up_weight,
    down_weight,
    cotangent,
    segment_lengths,
    parents,
):
    rows = lax.axis_size(ROW)
    columns = lax.axis_size("col")
    cores = lax.axis_size("core")
    own = tokens.shape[0] // rows
    held = own * cores
    groups = KV_HEADS // cores
    tables = tree_tables(segment_lengths, parents)
    row = lax.axis_index(ROW)
    column = lax.axis_index("col")
    high = lax.axis_index("high")
    core = lax.axis_index("core")
    index = column * tokens.shape[0] + row * own + jnp.arange(own, dtype=jnp.int32)
    cosines, sines = rotary_tables(index, tables)
    first = column * tokens.shape[0] + high * held

    spot = jnp.where(high == 0, column, 2 * columns - 1 - column)
    spots = lax.rem(spot + jnp.arange(2 * columns, dtype=jnp.int32), 2 * columns)
    far = spots >= columns
    ring_column = jnp.where(far, 2 * columns - 1 - spots, spots)
    ring_high = far.astype(jnp.int32)
    key_first = ring_column * tokens.shape[0] + ring_high * held
    key_index = (key_first[:, None] + jnp.arange(held, dtype=jnp.int32)[None, :]).reshape(-1)

    block = 256 if held % 256 == 0 else 128
    lists, counts = block_lists(first, key_index, block, held, tables)
    key_hot = segment_hot(key_index, tables).astype(F32)
    marks = jnp.pad(key_hot, ((0, 0), (HEAD_DIM, HEAD_DIM - key_hot.shape[1]))).astype(BF16)
    own_hot = segment_hot(index, tables).astype(F32)
    reach = jnp.sum(own_hot[:, :, None] * tables[2][None], axis=1)
    bars = jnp.pad((reach - 1.0) * BIG, ((0, 0), (HEAD_DIM, HEAD_DIM - reach.shape[1]))).astype(BF16)

    def exchange(value, axes):
        return lax.all_to_all(value, axes, split_axis=0, concat_axis=0, tiled=True)

    joint_blocks = gather(joint_weight, ALL_COL).reshape(columns, D, -1)
    gains = jnp.broadcast_to(jnp.stack([attention_gain, feed_gain])[None], (rows, 2, attention_gain.shape[0]))
    extended = jnp.concatenate([tokens.reshape(rows, own, -1), jnp.pad(gains, ((0, 0), (0, 14), (0, 0)))], axis=1)
    extended = exchange(extended, ROW)

    def plan(*places):
        keys = jnp.concatenate([key_index[i * held : j * held] for i, j in places])
        return (jnp.concatenate([marks[i * held : j * held] for i, j in places]), *block_lists(first, keys, block, held, tables))

    chips = 2 * columns
    plans = [plan((0, 2), (chips - 1, chips))]
    plans += [plan((s, s + 1), (chips - s, chips - s + 1)) for s in range(2, columns)]
    plans += [plan((columns, columns + 1))]
    (marks, lists, counts, plans), extended = lax.optimization_barrier(((marks, lists, counts, plans), extended))
    x, normed_one, joint_full, packed, value, gains = project_in(extended, joint_blocks, cosines, sines, bars)
    value, packed = lax.optimization_barrier((exchange(value, "core").reshape(held, -1), packed))
    packed = exchange(packed, "core").reshape(held, -1)
    width = gate_weight.shape[1]
    unit = width // 2 if width % 256 == 0 else width
    padding = jnp.zeros((output_weight.shape[1], -output_weight.shape[0] % unit), BF16)
    late = jnp.concatenate([gate_weight, up_weight, down_weight.T, output_weight.T, padding], axis=1)
    late = gather(late, ALL_COL).reshape(columns, D, -1)
    pieces = []
    state = None
    ahead, behind = ring_steps(columns)
    to_next, to_last = lax.ppermute(value, RING, ahead), lax.ppermute(value, RING, behind)
    fronts, backs = [], []

    def attend(state, plan, some, ends):
        keys, lists_here, counts_here = plan
        return tuple(attention_stage(lists_here, counts_here, packed, some, keys, state, ends))

    middle = held // 2
    for step in range(1, columns):
        fronts.append(to_next)
        backs.append(to_last)
        if step < columns - 1:
            further = (lax.ppermute(to_next, RING, ahead), lax.ppermute(to_last, RING, behind))
        else:
            further = (lax.ppermute(to_next[:middle], RING, ahead), lax.ppermute(to_last[middle:], RING, behind))
        some = [value, to_last, to_next] if step == 1 else [to_last, to_next]
        if step == 1:
            cotangent, further = lax.optimization_barrier((cotangent, further))
            upstream = exchange(cotangent.reshape(rows, own, -1), ROW).transpose(1, 0, 2).reshape(own, D)
        state = attend(state, plans[step - 1], some, False)
        state, further = lax.optimization_barrier((state, further))
        to_next, to_last = further
    pieces = [value, *backs, to_next, to_last, *reversed(fronts)]
    upstream, state = lax.optimization_barrier((upstream, state))
    state = attend(state, plans[columns - 1], [to_next, to_last], True)
    attended, lse = lax.cond(
        jnp.any(state[1] != state[1]),
        lambda: tuple(attention_forward(lists, counts, packed, pieces, marks)),
        lambda: tuple(state),
    )
    attended_rows = exchange(attended.reshape(cores, own, -1), "core")

    attended_rows, hidden, normed_two, output_full = project_out(attended_rows, late, x, gains, ATT // columns, late.shape[2] - 3 * width)
    mixed, gate_back, up_back, feed_out, normed_two_back = feed_forward(normed_two, upstream, late, width)

    feed_parts = gradient_parts(columns, rows, None, (normed_two, [gate_back, up_back]), (upstream, [mixed]))
    feed_parts, normed_two_back = lax.optimization_barrier((feed_parts, normed_two_back))
    feed_summed = scatter(feed_parts.reshape(-1, feed_parts.shape[3]), ALL_COL)
    hidden_back, hidden_low, heads_back, gain_two_part = output_back(normed_two_back, hidden, upstream, gains, output_full)
    output_parts = gradient_parts(columns, rows, gain_two_part[0], (hidden_low, [attended_rows]))

    heads_back = exchange(heads_back, "core").reshape(held, -1)
    query_backs, pair_rings = [], []
    for g in range(groups):
        heads_back = depart(heads_back, pair_rings)
        query_back, pair_back = attention_backward(g, lists, counts, packed, heads_back, attended, pieces, marks, lse)
        pair_back = pair_back.reshape(2 * columns, held, -1)
        query_backs.append(query_back)
        pair_back = after(pair_back, pair_rings)
        pair_rings.append(RingScatter(lambda s, half, v=pair_back: halves(v[s], half).astype(F32), columns))
    pair_rings[-1].launch()
    query_backs, feed_out = after((query_backs, feed_out), pair_rings[-1:])
    query_back = exchange(jnp.concatenate(query_backs, axis=1).reshape(cores, own, -1), "core")
    layer_low = (hidden + feed_out).astype(BF16).reshape(own, rows, -1).transpose(1, 0, 2)
    held_pairs = jnp.concatenate([ring.finish().astype(BF16) for ring in pair_rings], axis=1)
    held_pairs, query_back, layer_low, feed_summed, output_parts = lax.optimization_barrier(
        (held_pairs, query_back, layer_low, feed_summed, output_parts)
    )
    feed_summed = feed_summed.astype(F32)
    output_summed = scatter(output_parts.reshape(-1, output_parts.shape[3]), ALL_COL).astype(F32)
    pair_back = exchange(held_pairs.reshape(cores, own, -1), "core")
    layer_output = exchange(layer_low, ROW).reshape(rows * own, -1)
    joint_low, input_part, gain_one_part = joint_back(
        query_back, pair_back, cosines, sines, joint_full, x, gains, hidden_back, rows
    )
    joint_low, layer_output = lax.optimization_barrier((joint_low, layer_output))
    joint_parts = gradient_parts(columns, rows, gain_one_part[0], (normed_one, [joint_low]))
    joint_parts = joint_parts.reshape(2 * columns, cores, *joint_parts.shape[2:])
    places = ring_column * 2 + ring_high
    swap = [(0, 1), (1, 0)]
    joint_first = lax.dynamic_slice(joint_parts, (places[columns], 1 - core, 0, 0), (1, 1, *joint_parts.shape[2:]))[0, 0]
    joint_first = lax.ppermute(joint_first, "core", swap)
    joint_other = lax.dynamic_index_in_dim(joint_parts, 1 - core, 1, keepdims=False)
    joint_other = lax.ppermute(joint_other, "core", swap)

    def joint_part(s, half):
        mine = lax.dynamic_slice(joint_parts, (places[s], core, 0, 0), (1, 1, *joint_parts.shape[2:]))[0, 0]
        other = joint_first if s == columns else lax.dynamic_index_in_dim(joint_other, places[s], 0, keepdims=False)
        return halves(mine, half).astype(F32) + halves(other, half).astype(F32)

    joint_ring = RingScatter(joint_part, columns)
    input_gradient = exchange(input_part, ROW).reshape(rows * own, -1).astype(F32)
    joint_summed = joint_ring.finish()
    narrow, joined = ATT // columns, joint_weight.shape[1]
    return (
        layer_output,
        input_gradient,
        joint_summed[:, joined],
        joint_summed[:, :joined],
        output_summed[:, :narrow].T,
        output_summed[:, narrow],
        feed_summed[:, :width],
        feed_summed[:, width : 2 * width],
        feed_summed[:, 2 * width :].T,
    )


def solution(mesh):
    leaves, rows, columns = (mesh.shape[name] for name in ("leaf", "row", "col"))
    split = Mesh(mesh.devices.reshape(leaves, rows // 2, 2, columns), ("leaf", "high", "core", "col"))
    return jax.shard_map(
        per_device,
        mesh=split,
        in_specs=(
            P(("leaf", "col"), ROW),
            P(ROW),
            P(ROW, "col"),
            P("col", ROW),
            P(ROW),
            P(ROW, "col"),
            P(ROW, "col"),
            P("col", ROW),
            P(("leaf", "col"), ROW),
            P("leaf"),
            P("leaf"),
        ),
        out_specs=(
            P(("leaf", "col"), ROW),
            P(("leaf", "col"), ROW),
            P(("leaf", *ROW)),
            P(("leaf", *ROW), "col"),
            P(("leaf", "col"), ROW),
            P(("leaf", *ROW)),
            P(("leaf", *ROW), "col"),
            P(("leaf", *ROW), "col"),
            P(("leaf", "col"), ROW),
        ),
        check_vma=False,
    )
```

```python
import functools

import jax
import jax.numpy as jnp
from jax import lax
from jax.experimental import pallas as pl
from jax.experimental.pallas import tpu as pltpu
from jax.sharding import Mesh
from jax.sharding import PartitionSpec as P

D = 1152
HEADS = 18
KV_HEADS = 6
HEAD_DIM = 64
REPEAT = HEADS // KV_HEADS
ATT = HEADS * HEAD_DIM
KEYS = KV_HEADS * HEAD_DIM

EPSILON = 1e-05
THETA = 10000.0
BIG = 2.0**30
LOG2E = 1.4426950408889634
UNROLL = 8
DOWN_STEPS = 2
BF16 = jnp.bfloat16
F32 = jnp.float32
NT = (((1,), (1,)), ((), ()))
NN = (((1,), (0,)), ((), ()))


def dg(a, b, dims):
    return lax.dot_general(a, b, dims, preferred_element_type=F32)


def tree_tables(segment_lengths, parents):
    count = segment_lengths.shape[0]
    labels = jnp.arange(count, dtype=jnp.int32)
    ends = jnp.sum(jnp.where(labels[None, :] <= labels[:, None], segment_lengths[None, :], 0), axis=1)
    starts = ends - segment_lengths
    parent_hot = parents[:, None] == labels[None, :]
    grand = jnp.sum(jnp.where(parent_hot, parents[None, :], 0), axis=1)
    self_mark = labels[:, None] == labels[None, :]
    grand_mark = grand[:, None] == labels[None, :]
    ancestry = (self_mark | parent_hot | grand_mark).astype(F32)
    strict = (parent_hot | grand_mark) & jnp.logical_not(self_mark)
    offsets = jnp.sum(jnp.where(strict, segment_lengths[None, :], 0), axis=1)
    return (ends, starts, ancestry, offsets)


def segment_hot(index, tables):
    ends, starts, _, _ = tables
    return (index[:, None] >= starts[None, :]) & (index[:, None] < ends[None, :])


def rotary_tables(index, tables):
    hot = segment_hot(index, tables)
    depth = index + jnp.sum(jnp.where(hot, (tables[3] - tables[1])[None, :], 0), axis=1)
    half = HEAD_DIM // 2
    rates = THETA ** (-jnp.arange(half, dtype=F32) / half)
    angles = depth.astype(F32)[:, None] * rates[None, :]
    cosines, sines = jnp.cos(angles), jnp.sin(angles)
    return (jnp.concatenate([cosines] * 4, axis=1), jnp.concatenate([-sines, sines] * 2, axis=1))


def block_lists(first, key_index, block, held, tables):
    ends, starts, ancestry, _ = tables
    blocks = held // block
    key_low = key_index[::block]
    labels = jnp.arange(key_low.shape[0], dtype=jnp.int32)
    low = first + jnp.arange(blocks, dtype=jnp.int32) * block
    high = low + block
    query_has = ((starts[None, :] < high[:, None]) & (ends[None, :] > low[:, None])).astype(F32)
    key_has = ((starts[None, :] < key_low[:, None] + block) & (ends[None, :] > key_low[:, None])).astype(F32)
    reach = jnp.sum(query_has[:, :, None] * ancestry[None], axis=1)
    seen = jnp.sum(reach[:, None, :] * key_has[None], axis=2) > 0.5
    seen = seen & (key_low[None, :] < low[:, None])
    before = labels[None, :] < labels[:, None]
    rank = jnp.sum((seen[:, None, :] & before[None]).astype(jnp.int32), axis=2)
    place = seen[:, None, :] & (rank[:, None, :] == labels[None, :, None])
    lists = jnp.sum(jnp.where(place, labels[None, None, :], 0), axis=2)
    counts = jnp.sum(seen.astype(jnp.int32), axis=1)
    own = jnp.sum(jnp.where(key_low[None, :] == low[:, None], labels[None, :], 0), axis=1)
    lists = jnp.where(labels[None, :] == counts[:, None], own[:, None], lists)
    return (lists.reshape(-1).astype(jnp.int32), counts.astype(jnp.int32))


def cascade(count, unroll, steps):
    def body(i, c):
        steps(i * unroll, unroll)
        return c

    whole = count // unroll
    lax.fori_loop(0, whole, body, 0)
    start = whole * unroll
    size = unroll // 2
    while size:
        some = ((count - start) // size) > 0
        pl.when(some)(functools.partial(steps, start, size))
        start = start + jnp.where(some, size, 0)
        size //= 2


def causal(scores, heads):
    rows = lax.broadcasted_iota(jnp.int32, scores.shape, 0)
    columns = lax.rem(lax.broadcasted_iota(jnp.int32, scores.shape, 1), scores.shape[1] // heads)
    return jnp.where(rows <= columns, scores, -BIG)


def stacked(ref):
    value, wide = ref[...], 2 * HEAD_DIM
    return jnp.concatenate([value[:, h * wide : (h + 1) * wide] for h in range(value.shape[1] // wide)], axis=0)


def beside(value, heads):
    rows = value.shape[0] // heads
    return jnp.concatenate([value[h * rows : (h + 1) * rows] for h in range(heads)], axis=1)


def left_half(shape):
    return lax.broadcasted_iota(jnp.int32, shape, 1) < HEAD_DIM


def fetch(pieces, group, kv_ref, sems):
    copies, start = [], 0
    for i, piece in enumerate(pieces):
        lanes = pl.ds(pl.multiple_of(group * 2 * HEAD_DIM, 2 * HEAD_DIM), 2 * HEAD_DIM)
        target = kv_ref.at[pl.ds(start, piece.shape[0])]
        copies.append(pltpu.make_async_copy(piece.at[:, lanes], target, sems.at[i]))
        start += piece.shape[0]
    for copy in copies:
        copy.start()
    for copy in copies:
        copy.wait()


def forward_kernel(lists, counts, q_ref, mark_ref, *refs):
    *pieces, o_ref, lse_ref, top_ref, sum_ref, kv_ref, vt_ref, sems = refs
    block = pl.program_id(1)
    heads, rows = q_ref.shape[1] // (2 * HEAD_DIM), q_ref.shape[0]
    total = kv_ref.shape[0]
    stride = total // rows
    count = counts[block]

    @pl.when(block == 0)
    def _():
        fetch(pieces, pl.program_id(0), kv_ref, sems)

        def flip(i, c):
            k0 = pl.multiple_of(i * rows, rows)
            turned = kv_ref[pl.ds(k0, rows), :].T
            vt_ref[:HEAD_DIM, pl.ds(k0, rows)] = turned[HEAD_DIM:]
            return c

        lax.fori_loop(0, stride, flip, 0)
        tail = (vt_ref.shape[0] - HEAD_DIM, total)
        vt_ref[HEAD_DIM:] = jnp.where(lax.broadcasted_iota(jnp.int32, tail, 0) == 0, 1.0, 0.0).astype(BF16)

    def queries():
        return stacked(q_ref)

    def blocks(start, n):
        offs = [pl.multiple_of(lists[block * stride + start + u] * rows, rows) for u in range(n)]
        kv = jnp.concatenate([kv_ref[pl.ds(k0, rows), :] for k0 in offs], axis=0)
        mark = jnp.concatenate([mark_ref[pl.ds(k0, rows), :] for k0 in offs], axis=0)
        vt = jnp.concatenate([vt_ref[:, pl.ds(k0, rows)] for k0 in offs], axis=1)
        return jnp.where(left_half(kv.shape), kv, mark), vt

    def begin():
        k, vt = blocks(count, 1)
        scores = causal(dg(k, queries(), NT), heads)
        top = jnp.max(scores, axis=0, keepdims=True)
        top_ref[...] = top
        sum_ref[...] = dg(vt, jnp.exp2(scores - top).astype(BF16), NN)

    def steps(start, n):
        k, vt = blocks(start, n)
        weights = jnp.exp2(dg(k, queries(), NT) - top_ref[...]).astype(BF16)
        sum_ref[...] += dg(vt, weights, NN)

    begin()
    cascade(count, UNROLL, steps)

    @pl.when(jnp.logical_not(jnp.max(sum_ref[HEAD_DIM : HEAD_DIM + 1, :]) < 2.0**100))
    def _():
        begin()

        def online(n, c):
            k, vt = blocks(n, 1)
            scores = dg(k, queries(), NT)
            old = top_ref[...]
            new = jnp.maximum(old, jnp.max(scores, axis=0, keepdims=True))
            top_ref[...] = new
            sum_ref[...] = sum_ref[...] * jnp.exp2(old - new) + dg(vt, jnp.exp2(scores - new).astype(BF16), NN)
            return c

        lax.fori_loop(0, count, online, 0)

    total_row = sum_ref[HEAD_DIM : HEAD_DIM + 1, :]
    spread = jnp.concatenate([jnp.zeros((HEAD_DIM, heads * rows), F32), sum_ref[:HEAD_DIM, :] / total_row], axis=0)
    o_ref[...] = beside(spread.T.astype(BF16), heads)
    lse_ref[0, 0] = top_ref[...] + jnp.log2(total_row)


def attention_forward(lists, counts, q, pieces, marks):
    tokens, wide, heads = q.shape[0], 2 * HEAD_DIM, REPEAT
    groups = q.shape[1] // (wide * heads)
    total = marks.shape[0]
    blocks = counts.shape[0]
    rows = tokens // blocks
    tall = HEAD_DIM + 16
    return pl.pallas_call(
        forward_kernel,
        grid_spec=pltpu.PrefetchScalarGridSpec(
            num_scalar_prefetch=2,
            grid=(groups, blocks),
            in_specs=[
                pl.BlockSpec((rows, heads * wide), lambda g, b, *_: (b, g)),
                pl.BlockSpec((total, wide), lambda g, b, *_: (0, 0)),
                *(pl.BlockSpec(memory_space=pl.ANY) for _ in pieces),
            ],
            out_specs=[
                pl.BlockSpec((rows, heads * wide), lambda g, b, *_: (b, g)),
                pl.BlockSpec((1, 1, 1, heads * rows), lambda g, b, *_: (g, b, 0, 0)),
            ],
            scratch_shapes=[
                pltpu.VMEM((1, heads * rows), F32),
                pltpu.VMEM((tall, heads * rows), F32),
                pltpu.VMEM((total, wide), BF16),
                pltpu.VMEM((tall, total), BF16),
                pltpu.SemaphoreType.DMA((len(pieces),)),
            ],
        ),
        out_shape=[
            jax.ShapeDtypeStruct((tokens, groups * heads * wide), BF16),
            jax.ShapeDtypeStruct((groups, blocks, 1, heads * rows), F32),
        ],
        compiler_params=pltpu.CompilerParams(vmem_limit_bytes=48 * 2**20),
        cost_estimate=pl.CostEstimate(
            flops=groups * heads * tokens * total * 256, bytes_accessed=groups * total * 512, transcendentals=0
        ),
        name="attention_forward",
    )(lists, counts, q, marks, *pieces)


def stage_kernel(begins, ends, lists, counts, q_ref, mark_ref, *refs):
    refs = list(refs)
    sums_in, tops_in = ([refs.pop(0), refs.pop(0)] if not begins else (None, None))
    *pieces, first_ref, second_ref, top_ref, sum_ref, kv_ref, vt_ref, sems = refs
    block = pl.program_id(1)
    heads, rows = q_ref.shape[1] // (2 * HEAD_DIM), q_ref.shape[0]
    total = kv_ref.shape[0]
    stride = total // rows
    count = counts[block]

    @pl.when(block == 0)
    def _():
        fetch(pieces, pl.program_id(0), kv_ref, sems)

        def flip(i, c):
            k0 = pl.multiple_of(i * rows, rows)
            turned = kv_ref[pl.ds(k0, rows), :].T
            vt_ref[:HEAD_DIM, pl.ds(k0, rows)] = turned[HEAD_DIM:]
            return c

        lax.fori_loop(0, stride, flip, 0)
        tail = (vt_ref.shape[0] - HEAD_DIM, total)
        vt_ref[HEAD_DIM:] = jnp.where(lax.broadcasted_iota(jnp.int32, tail, 0) == 0, 1.0, 0.0).astype(BF16)

    def queries():
        return stacked(q_ref)

    def blocks(start, n):
        offs = [pl.multiple_of(lists[block * stride + start + u] * rows, rows) for u in range(n)]
        kv = jnp.concatenate([kv_ref[pl.ds(k0, rows), :] for k0 in offs], axis=0)
        mark = jnp.concatenate([mark_ref[pl.ds(k0, rows), :] for k0 in offs], axis=0)
        vt = jnp.concatenate([vt_ref[:, pl.ds(k0, rows)] for k0 in offs], axis=1)
        return jnp.where(left_half(kv.shape), kv, mark), vt

    if begins:
        k, vt = blocks(count, 1)
        scores = causal(dg(k, queries(), NT), heads)
        top = jnp.max(scores, axis=0, keepdims=True)
        top_ref[...] = top
        sum_ref[...] = dg(vt, jnp.exp2(scores - top).astype(BF16), NN)
    else:
        top_ref[...] = tops_in[0, 0]
        sum_ref[...] = sums_in[0, 0]

    def steps(start, n):
        k, vt = blocks(start, n)
        weights = jnp.exp2(dg(k, queries(), NT) - top_ref[...]).astype(BF16)
        sum_ref[...] += dg(vt, weights, NN)

    cascade(count, UNROLL, steps)
    if ends:
        total_row = sum_ref[HEAD_DIM : HEAD_DIM + 1, :]
        spread = jnp.concatenate([jnp.zeros((HEAD_DIM, heads * rows), F32), sum_ref[:HEAD_DIM, :] / total_row], axis=0)
        first_ref[...] = beside(spread.T.astype(BF16), heads)
        second_ref[0, 0] = jnp.where(total_row < 2.0**100, top_ref[...] + jnp.log2(total_row), jnp.nan)
    else:
        first_ref[0, 0] = sum_ref[...]
        second_ref[0, 0] = top_ref[...]


def attention_stage(lists, counts, q, pieces, marks, state, ends):
    tokens, wide, heads = q.shape[0], 2 * HEAD_DIM, REPEAT
    groups = q.shape[1] // (wide * heads)
    total = marks.shape[0]
    blocks = counts.shape[0]
    rows = tokens // blocks
    tall = HEAD_DIM + 16
    lanes = heads * rows
    held_specs = [
        pl.BlockSpec((1, 1, tall, lanes), lambda g, b, *_: (g, b, 0, 0)),
        pl.BlockSpec((1, 1, 1, lanes), lambda g, b, *_: (g, b, 0, 0)),
    ]
    tops = jax.ShapeDtypeStruct((groups, blocks, 1, lanes), F32)
    if ends:
        out_specs = [pl.BlockSpec((rows, heads * wide), lambda g, b, *_: (b, g)), held_specs[1]]
        out_shape = [jax.ShapeDtypeStruct((tokens, groups * heads * wide), BF16), tops]
    else:
        out_specs = held_specs
        out_shape = [jax.ShapeDtypeStruct((groups, blocks, tall, lanes), F32), tops]
    return pl.pallas_call(
        functools.partial(stage_kernel, state is None, ends),
        grid_spec=pltpu.PrefetchScalarGridSpec(
            num_scalar_prefetch=2,
            grid=(groups, blocks),
            in_specs=[
                pl.BlockSpec((rows, heads * wide), lambda g, b, *_: (b, g)),
                pl.BlockSpec((total, wide), lambda g, b, *_: (0, 0)),
                *([] if state is None else held_specs),
                *(pl.BlockSpec(memory_space=pl.ANY) for _ in pieces),
            ],
            out_specs=out_specs,
            scratch_shapes=[
                pltpu.VMEM((1, lanes), F32),
                pltpu.VMEM((tall, lanes), F32),
                pltpu.VMEM((total, wide), BF16),
                pltpu.VMEM((tall, total), BF16),
                pltpu.SemaphoreType.DMA((len(pieces),)),
            ],
        ),
        out_shape=out_shape,
        compiler_params=pltpu.CompilerParams(vmem_limit_bytes=40 * 2**20),
        cost_estimate=pl.CostEstimate(
            flops=groups * heads * tokens * total * 256, bytes_accessed=groups * total * 512, transcendentals=0
        ),
        name="attention_stage",
    )(lists, counts, q, marks, *(() if state is None else state), *pieces)


def backward_kernel(group, lists, counts, q_ref, do_ref, o_ref, mark_ref, lse_ref, *refs):
    *pieces, dq_ref, dkv_ref, dq_sum, dkv_sum, kv_ref, kt_ref, delta_ref, sems = refs
    block = pl.program_id(0)
    heads, rows = q_ref.shape[1] // (2 * HEAD_DIM), q_ref.shape[0]
    total = kv_ref.shape[0]
    stride = total // rows
    count = counts[block]

    @pl.when(block == 0)
    def _():
        dkv_sum[...] = jnp.zeros(dkv_sum.shape, F32)
        fetch(pieces, group, kv_ref, sems)

        def flip(i, c):
            k0 = pl.multiple_of(i * rows, rows)
            turned = kv_ref[pl.ds(k0, rows), :].T
            kt_ref[:, pl.ds(k0, rows)] = turned[:HEAD_DIM]
            return c

        lax.fori_loop(0, stride, flip, 0)

    dq_sum[...] = jnp.zeros(dq_sum.shape, F32)
    products = stacked(do_ref).astype(F32) * stacked(o_ref).astype(F32)
    delta_ref[...] = jnp.sum(products.T, axis=0, keepdims=True)

    def steps(start, n, masked):
        q, do = stacked(q_ref), stacked(do_ref)
        offs = [pl.multiple_of(lists[block * stride + start + u] * rows, rows) for u in range(n)]
        kv = jnp.concatenate([kv_ref[pl.ds(k0, rows), :] for k0 in offs], axis=0)
        mark = jnp.concatenate([mark_ref[pl.ds(k0, rows), :] for k0 in offs], axis=0)
        kt = jnp.concatenate([kt_ref[:, pl.ds(k0, rows)] for k0 in offs], axis=1)
        scores = dg(jnp.where(left_half(kv.shape), kv, mark), q, NT) - lse_ref[0, 0]
        if masked:
            scores = causal(scores, heads)
        chances = jnp.exp2(scores)
        back = dg(kv, do, NT) - delta_ref[...]
        score_back = (chances * back).astype(BF16)
        only_q = jnp.where(left_half(q.shape), q, jnp.zeros_like(q))
        update = dg(score_back, only_q, NN) + dg(chances.astype(BF16), do, NN)
        dq_sum[...] += dg(kt, score_back, NN)
        for u in range(n):
            dkv_sum[pl.ds(offs[u], rows), :] += update[u * rows : (u + 1) * rows]

    steps(count, 1, True)
    cascade(count, UNROLL, lambda start, n: steps(start, n, False))
    spread = jnp.concatenate([dq_sum[...] * HEAD_DIM**-0.5, jnp.zeros(dq_sum.shape, F32)], axis=0)
    dq_ref[...] = beside(spread.T.astype(BF16), heads)

    @pl.when(block == pl.num_programs(0) - 1)
    def _():
        summed = dkv_sum[...]
        dkv_ref[...] = jnp.where(left_half(summed.shape), summed * (1.0 / LOG2E), summed).astype(BF16)


def attention_backward(group, lists, counts, q, do, o, pieces, marks, lse):
    tokens, wide, heads = q.shape[0], 2 * HEAD_DIM, REPEAT
    total = marks.shape[0]
    blocks = counts.shape[0]
    rows = tokens // blocks
    block = pl.BlockSpec((rows, heads * wide), lambda b, *_: (b, group))
    return pl.pallas_call(
        functools.partial(backward_kernel, group),
        grid_spec=pltpu.PrefetchScalarGridSpec(
            num_scalar_prefetch=2,
            grid=(blocks,),
            in_specs=[
                block,
                block,
                block,
                pl.BlockSpec((total, wide), lambda b, *_: (0, 0)),
                pl.BlockSpec((1, 1, 1, heads * rows), lambda b, *_: (group, b, 0, 0)),
                *(pl.BlockSpec(memory_space=pl.ANY) for _ in pieces),
            ],
            out_specs=[
                pl.BlockSpec((rows, heads * wide), lambda b, *_: (b, 0)),
                pl.BlockSpec((total, wide), lambda b, *_: (0, 0)),
            ],
            scratch_shapes=[
                pltpu.VMEM((HEAD_DIM, heads * rows), F32),
                pltpu.VMEM((total, wide), F32),
                pltpu.VMEM((total, wide), BF16),
                pltpu.VMEM((HEAD_DIM, total), BF16),
                pltpu.VMEM((1, heads * rows), F32),
                pltpu.SemaphoreType.DMA((len(pieces),)),
            ],
        ),
        out_shape=[
            jax.ShapeDtypeStruct((tokens, heads * wide), BF16),
            jax.ShapeDtypeStruct((total, wide), BF16),
        ],
        compiler_params=pltpu.CompilerParams(vmem_limit_bytes=60 * 2**20),
        cost_estimate=pl.CostEstimate(flops=heads * tokens * total * 640, bytes_accessed=total * 1024, transcendentals=0),
        name="attention_backward",
    )(lists, counts, q, do, o, marks, lse, *pieces)


def roll_half(value):
    return pltpu.roll(value, HEAD_DIM, 1)


def swap_quarters(value):
    quarter = HEAD_DIM // 2
    lane = lax.broadcasted_iota(jnp.int32, value.shape, 1)
    first = lax.rem(lane, HEAD_DIM) < quarter
    return jnp.where(first, pltpu.roll(value, value.shape[1] - quarter, 1), pltpu.roll(value, quarter, 1))


def root_mean(value):
    return lax.rsqrt(jnp.sum(value * value, axis=1, keepdims=True) / D + EPSILON)


def project_kernel(x4_ref, w_ref, cos_ref, sin_ref, bars_ref, x_ref, xa_ref, full_ref, query_ref, pair_ref, gains_ref, joint_ref):
    own = x_ref.shape[0]
    wide = 2 * HEAD_DIM
    x = jnp.concatenate([x4_ref[r, :own, :] for r in range(x4_ref.shape[0])], axis=1)
    gains = jnp.concatenate([x4_ref[r, own : own + 16, :] for r in range(x4_ref.shape[0])], axis=1).astype(F32)
    x_ref[...] = x
    gains_ref[...] = gains[:8]
    value = x.astype(F32)
    xa_ref[...] = (value * root_mean(value) * gains[0:1]).astype(BF16)
    full_ref[...] = jnp.concatenate([w_ref[c] for c in range(w_ref.shape[0])], axis=1)
    joint_ref[...] = dg(xa_ref[...], full_ref[...], NN).astype(BF16)
    left = left_half((own, wide))
    bars = bars_ref[...].astype(F32)
    heads, pairs = HEADS // 2, KV_HEADS // 2

    def part(i):
        return joint_ref[:, i * wide : (i + 1) * wide].astype(F32)

    def turned(i):
        value = part(i)
        return value * cos_ref[...] + swap_quarters(value) * sin_ref[...]

    for i in range(HEADS // 2):
        value = turned(i) * (LOG2E * HEAD_DIM**-0.5)
        for j, head in ((2 * i, value), (2 * i + 1, roll_half(value))):
            start = (j % heads) * wide
            query_ref[j // heads, :, start : start + wide] = jnp.where(left, head, bars).astype(BF16)
    for i in range(KV_HEADS // 2):
        key = turned(HEADS // 2 + i)
        value = part(HEADS // 2 + KV_HEADS // 2 + i)
        for j, both in (
            (2 * i, jnp.where(left, key, roll_half(value))),
            (2 * i + 1, jnp.where(left, roll_half(key), value)),
        ):
            start = (j % pairs) * wide
            pair_ref[j // pairs, :, start : start + wide] = both.astype(BF16)


def project_in(x4, weight, cosines, sines, bars):
    own = cosines.shape[0]
    shapes = [
        jax.ShapeDtypeStruct((own, D), BF16),
        jax.ShapeDtypeStruct((own, D), BF16),
        jax.ShapeDtypeStruct((D, ATT + 2 * KEYS), BF16),
        jax.ShapeDtypeStruct((2, own, ATT), BF16),
        jax.ShapeDtypeStruct((2, own, KEYS), BF16),
        jax.ShapeDtypeStruct((8, D), F32),
    ]
    return pl.pallas_call(
        project_kernel,
        out_shape=shapes,
        scratch_shapes=[pltpu.VMEM((own, ATT + 2 * KEYS), BF16)],
        compiler_params=pltpu.CompilerParams(vmem_limit_bytes=56 * 2**20),
        cost_estimate=pl.CostEstimate(flops=2 * own * D * (ATT + 2 * KEYS), bytes_accessed=2**24, transcendentals=0),
        name="project_in",
    )(x4, weight, cosines, sines, bars)


def output_kernel(width, o_ref, w_ref, x_ref, gains_ref, rows_ref, hidden_ref, normed_ref, full_ref):
    wide = 2 * HEAD_DIM
    heads = HEADS // 2
    left = left_half((x_ref.shape[0], wide))
    for i in range(HEADS // 2):
        first, second = (
            o_ref[j // heads, :, (j % heads) * wide : (j % heads + 1) * wide] for j in (2 * i, 2 * i + 1)
        )
        first = roll_half(first.astype(F32))
        rows_ref[:, i * wide : (i + 1) * wide] = jnp.where(left, first, second.astype(F32)).astype(BF16)
    full_ref[...] = jnp.concatenate([w_ref[c, :, :width] for c in range(w_ref.shape[0])], axis=1)
    hidden = x_ref[...].astype(F32) + dg(rows_ref[...], full_ref[...], NT)
    hidden_ref[...] = hidden
    normed_ref[...] = (hidden * root_mean(hidden) * gains_ref[1:2]).astype(BF16)


def project_out(o, late, x, gains, width, padded):
    own = x.shape[0]
    place = late.shape[2] // padded - 1
    return pl.pallas_call(
        functools.partial(output_kernel, width),
        grid=(1,),
        in_specs=[
            pl.BlockSpec(o.shape, lambda i: (0, 0, 0)),
            pl.BlockSpec((late.shape[0], D, padded), lambda i: (0, 0, place)),
            pl.BlockSpec(x.shape, lambda i: (0, 0)),
            pl.BlockSpec(gains.shape, lambda i: (0, 0)),
        ],
        out_specs=[pl.BlockSpec((own, D), lambda i: (0, 0))] * 3 + [pl.BlockSpec((D, ATT), lambda i: (0, 0))],
        out_shape=[
            jax.ShapeDtypeStruct((own, ATT), BF16),
            jax.ShapeDtypeStruct((own, D), F32),
            jax.ShapeDtypeStruct((own, D), BF16),
            jax.ShapeDtypeStruct((D, ATT), BF16),
        ],
        compiler_params=pltpu.CompilerParams(vmem_limit_bytes=56 * 2**20),
        cost_estimate=pl.CostEstimate(flops=2 * own * D * ATT, bytes_accessed=2**24, transcendentals=0),
        name="project_out",
    )(o, late, x, gains)


def norm_back(upstream, value, gain):
    scale = root_mean(value)
    weighted = upstream * gain
    inner = jnp.sum(weighted * value, axis=1, keepdims=True)
    gain_back = jnp.sum(upstream * value * scale, axis=0, keepdims=True)
    return scale * weighted - value * (scale * scale * scale * inner / D), gain_back


def output_back_kernel(back_ref, hidden_ref, upstream_ref, gains_ref, full_ref, hidden_back_ref, low_ref, do_ref, sums_ref):
    wide = 2 * HEAD_DIM
    heads = HEADS // 2
    part, sums = norm_back(back_ref[...], hidden_ref[...], gains_ref[1:2])
    hidden_back = upstream_ref[...].astype(F32) + part
    hidden_back_ref[...] = hidden_back
    low_ref[...] = hidden_back.astype(BF16)
    sums_ref[...] = jnp.broadcast_to(sums, sums_ref.shape)
    attended_back = dg(low_ref[...], full_ref[...], NN)
    left = left_half((low_ref.shape[0], wide))
    for i in range(HEADS // 2):
        value = attended_back[:, i * wide : (i + 1) * wide]
        for j, head in ((2 * i, roll_half(value)), (2 * i + 1, value)):
            start = (j % heads) * wide
            do_ref[j // heads, :, start : start + wide] = jnp.where(left, 0.0, head).astype(BF16)


def output_back(back, hidden, upstream, gains, full):
    own = back.shape[0]
    return pl.pallas_call(
        output_back_kernel,
        out_shape=[
            jax.ShapeDtypeStruct((own, D), F32),
            jax.ShapeDtypeStruct((own, D), BF16),
            jax.ShapeDtypeStruct((2, own, ATT), BF16),
            jax.ShapeDtypeStruct((8, D), F32),
        ],
        compiler_params=pltpu.CompilerParams(vmem_limit_bytes=56 * 2**20),
        cost_estimate=pl.CostEstimate(flops=2 * own * D * ATT, bytes_accessed=2**24, transcendentals=0),
        name="output_back",
    )(back, hidden, upstream, gains, full)


def joint_back_kernel(query_ref, pair_ref, cos_ref, sin_ref, full_ref, x_ref, gains_ref, hidden_back_ref, joint_ref, out_ref, sums_ref):
    wide = 2 * HEAD_DIM
    heads, pairs = HEADS // 2, KV_HEADS // 2
    left = left_half((x_ref.shape[0], wide))

    def queries(j):
        return query_ref[j // heads, :, (j % heads) * wide : (j % heads + 1) * wide].astype(F32)

    def both(j):
        start = (j % pairs) * wide
        return pair_ref[j // pairs, :, start : start + wide].astype(F32)

    def store(i, value):
        joint_ref[:, i * wide : (i + 1) * wide] = value.astype(BF16)

    def back(value):
        return value * cos_ref[...] - swap_quarters(value) * sin_ref[...]

    for i in range(HEADS // 2):
        store(i, back(jnp.where(left, queries(2 * i), roll_half(queries(2 * i + 1)))))
    for i in range(KV_HEADS // 2):
        first, second = both(2 * i), both(2 * i + 1)
        store(HEADS // 2 + i, back(jnp.where(left, first, roll_half(second))))
        store(HEADS // 2 + KV_HEADS // 2 + i, jnp.where(left, roll_half(first), second))
    upstream = dg(joint_ref[...], full_ref[...], NT)
    part, sums = norm_back(upstream, x_ref[...].astype(F32), gains_ref[0:1])
    total = (hidden_back_ref[...] + part).astype(BF16)
    features = out_ref.shape[2]
    for r in range(out_ref.shape[0]):
        out_ref[r] = total[:, r * features : (r + 1) * features]
    sums_ref[...] = jnp.broadcast_to(sums, sums_ref.shape)


def joint_back(queries, pairs, cosines, sines, full, x, gains, hidden_back, rows):
    own = x.shape[0]
    return pl.pallas_call(
        joint_back_kernel,
        out_shape=[
            jax.ShapeDtypeStruct((own, ATT + 2 * KEYS), BF16),
            jax.ShapeDtypeStruct((rows, own, D // rows), BF16),
            jax.ShapeDtypeStruct((8, D), F32),
        ],
        compiler_params=pltpu.CompilerParams(vmem_limit_bytes=56 * 2**20),
        cost_estimate=pl.CostEstimate(flops=2 * own * D * (ATT + 2 * KEYS), bytes_accessed=2**24, transcendentals=0),
        name="joint_back",
    )(queries, pairs, cosines, sines, full, x, gains, hidden_back)


def feed_kernel(
    places, normed_ref, back_ref, gate_ref, up_ref, *refs
):
    mine, others = refs[:2], refs[2:4]
    mixed_ref, gate_back_ref, up_back_ref, out_ref, normed_back_ref, down_ref = refs[4:]
    core = places[places.shape[0] - 1]
    features = mine[0].shape[1]
    for high in range(2):
        for block, row in ((mine[high], 2 * high + core), (others[high], 2 * high + 1 - core)):
            down_ref[pl.ds(pl.multiple_of(row * features, 32), features), :] = block[0]

    @pl.when(pl.program_id(0) == 0)
    def _():
        out_ref[...] = jnp.zeros(out_ref.shape, F32)
        normed_back_ref[...] = jnp.zeros(normed_back_ref.shape, F32)

    gate = dg(normed_ref[...], gate_ref[0], NN)
    up_value = dg(normed_ref[...], up_ref[0], NN)
    mixed_back = dg(back_ref[...], down_ref[...], NN)
    sigmoid = jax.nn.sigmoid(gate)
    silu = gate * sigmoid
    mixed = (silu * up_value).astype(BF16)
    gate_back = (mixed_back * up_value * (sigmoid * (1.0 + gate * (1.0 - sigmoid)))).astype(BF16)
    up_back = (mixed_back * silu).astype(BF16)
    mixed_ref[...] = mixed
    gate_back_ref[...] = gate_back
    up_back_ref[...] = up_back
    out_ref[...] += dg(mixed, down_ref[...], NT)
    normed_back_ref[...] += dg(gate_back, gate_ref[0], NT) + dg(up_back, up_ref[0], NT)


def feed_forward(places, normed, back, late, mine, others):
    tokens = normed.shape[0]
    columns, (_, features, width) = late.shape[0], mine.shape
    whole = pl.BlockSpec((tokens, D), lambda c, places: (0, 0))
    blocks = [pl.BlockSpec((1, D, width), lambda c, places, k=k: (c, 0, k)) for k in range(2)]
    downs = [pl.BlockSpec((1, features, width), lambda c, places, h=h: (places[2 * c + h], 0, 0)) for h in range(2)]
    out = pl.BlockSpec((tokens, width), lambda c, places: (0, c))
    return pl.pallas_call(
        feed_kernel,
        grid_spec=pltpu.PrefetchScalarGridSpec(
            num_scalar_prefetch=1,
            grid=(columns,),
            in_specs=[whole, whole, *blocks, *downs, *downs],
            out_specs=[out, out, out, whole, whole],
            scratch_shapes=[pltpu.VMEM((D, width), BF16)],
        ),
        out_shape=[jax.ShapeDtypeStruct((tokens, columns * width), BF16)] * 3 + [jax.ShapeDtypeStruct((tokens, D), F32)] * 2,
        compiler_params=pltpu.CompilerParams(vmem_limit_bytes=62 * 2**20),
        cost_estimate=pl.CostEstimate(
            flops=12 * tokens * D * columns * width, bytes_accessed=6 * D * columns * width, transcendentals=0
        ),
        name="feed_forward",
    )(places, normed, back, late, late, mine, mine, others, others)


def gradient_kernel(counts, blocked, summed, *refs):
    refs = list(refs)
    sets = [(refs.pop(0), [refs.pop(0) for _ in range(n)]) for n in counts]
    sums_ref = refs.pop(0) if summed else None
    out_ref, turned, held = refs[0], refs[1 : 1 + len(sets)], refs[1 + len(sets) :]
    step = pl.program_id(0)
    rows = out_ref.shape[1]
    features = sets[0][0].shape[1] // rows
    rights = [right for _, some in sets for right in some]
    whole = [right for right, flag in zip(rights, blocked, strict=True) if not flag]

    @pl.when(step == 0)
    def _():
        for (left, _), target in zip(sets, turned, strict=True):
            target[...] = left[...].T
        for right, block in zip(whole, held, strict=True):
            width = block.shape[2]
            for c in range(block.shape[0]):
                block[c] = right[:, c * width : (c + 1) * width]

    spare, flags, start = list(held), list(blocked), 0
    for (_, some), target in zip(sets, turned, strict=True):
        for right in some:
            value = right[...] if flags.pop(0) else spare.pop(0)[step]
            width = value.shape[1]
            part = dg(target[...], value, NN).astype(BF16)
            for r in range(rows):
                out_ref[0, r, :, start : start + width] = part[r * features : (r + 1) * features]
            start += width
    if summed:
        tail = (rows, features, out_ref.shape[3] - start)
        out_ref[0, :, :, start:] = jnp.broadcast_to(sums_ref[...], tail).astype(BF16)


def gradient_parts(columns, rows, sums, *sets):
    tokens = sets[0][0].shape[0]
    features = D // rows
    operands, specs, turned, held, blocked, wide = [], [], [], [], [], 0
    for left, rights in sets:
        operands.append(left)
        specs.append(pl.BlockSpec(left.shape, lambda c: (0, 0)))
        turned.append(pltpu.VMEM((left.shape[1], tokens), BF16))
        for right in rights:
            width = right.shape[1] // columns
            operands.append(right)
            wide += width
            if width % 128 == 0:
                specs.append(pl.BlockSpec((tokens, width), lambda c: (0, c)))
                blocked.append(True)
            else:
                specs.append(pl.BlockSpec(right.shape, lambda c: (0, 0)))
                held.append(pltpu.VMEM((columns, tokens, width), BF16))
                blocked.append(False)
    if sums is not None:
        wide = (wide // 128 + 1) * 128
        operands.append(sums.reshape(rows, features, 1))
        specs.append(pl.BlockSpec((rows, features, 1), lambda c: (0, 0, 0)))
    shape = (columns, rows, features, wide)
    return pl.pallas_call(
        functools.partial(gradient_kernel, [len(rights) for _, rights in sets], blocked, sums is not None),
        grid=(columns,),
        in_specs=specs,
        out_specs=pl.BlockSpec((1, *shape[1:]), lambda c: (c, 0, 0, 0)),
        out_shape=jax.ShapeDtypeStruct(shape, BF16),
        scratch_shapes=[*turned, *held],
        compiler_params=pltpu.CompilerParams(vmem_limit_bytes=60 * 2**20),
        cost_estimate=pl.CostEstimate(
            flops=2 * tokens * D * wide * columns, bytes_accessed=2 * D * wide * columns, transcendentals=0
        ),
        name="gradient_parts",
    )(*operands)


ROW = ("high", "core")
ALL_ROW = ("high", "core", "col")
ALL_COL = ("col", "high", "core")
RING = ("high", "col")


def ring_steps(columns):
    path = [*range(columns), *reversed(range(columns, 2 * columns))]
    ahead = [(path[i], path[(i + 1) % len(path)]) for i in range(len(path))]
    return ahead, [(b, a) for a, b in ahead]


class RingScatter:
    def __init__(self, part, columns):
        self.part, (self.ahead, self.behind), self.count = part, ring_steps(columns), 2 * columns
        self.left = self.count // 2
        self.arrived = None
        self.ready = (part(self.left, 0).astype(BF16), part(self.left, 1).astype(BF16))

    def launch(self):
        out, back = self.ready
        self.arrived = (lax.ppermute(out, RING, self.ahead), lax.ppermute(back, RING, self.behind))
        self.ready = None
        self.left -= 1

    def prepare(self):
        out, back = self.part(self.left, None), self.part(self.count - self.left, None)
        front, rear = (v.astype(F32) for v in self.arrived)
        half = front.shape[0]
        if half == out.shape[0]:
            out, back = out + front, back + rear
        else:
            out = jnp.concatenate([out[:half] + front, out[half:]], axis=0)
            back = jnp.concatenate([back[:half], back[half:] + rear], axis=0)
        self.ready = (out.astype(BF16), back.astype(BF16))

    def finish(self):
        while self.left or self.ready:
            if self.ready is None:
                self.prepare()
            self.ready = lax.optimization_barrier(self.ready)
            self.launch()
        return self.part(0, None) + self.arrived[0].astype(F32) + self.arrived[1].astype(F32)


def after(value, rings):
    value, arrived = lax.optimization_barrier((value, [ring.arrived for ring in rings]))
    for ring, a in zip(rings, arrived, strict=True):
        ring.arrived = a
    return value


def depart(value, rings):
    rings = [ring for ring in rings if ring.left]
    for ring in rings:
        if ring.ready is None:
            ring.prepare()
    value, ready = lax.optimization_barrier((value, [ring.ready for ring in rings]))
    for ring, r in zip(rings, ready, strict=True):
        ring.ready = r
        ring.launch()
    return value


def halves(value, half):
    if half is None:
        return value
    middle = value.shape[0] // 2
    return value[middle:] if half else value[:middle]


def scatter(value, axes):
    return lax.psum_scatter(value, axes, scatter_dimension=0, tiled=True)


def gather(value, axes):
    return lax.all_gather(value, axes, axis=0, tiled=True)


def per_device(
    tokens,
    attention_gain,
    joint_weight,
    output_weight,
    feed_gain,
    gate_weight,
    up_weight,
    down_weight,
    cotangent,
    segment_lengths,
    parents,
):
    rows = lax.axis_size(ROW)
    columns = lax.axis_size("col")
    cores = lax.axis_size("core")
    own = tokens.shape[0] // rows
    held = own * cores
    groups = KV_HEADS // cores
    tables = tree_tables(segment_lengths, parents)
    row = lax.axis_index(ROW)
    column = lax.axis_index("col")
    high = lax.axis_index("high")
    core = lax.axis_index("core")
    index = column * tokens.shape[0] + row * own + jnp.arange(own, dtype=jnp.int32)
    cosines, sines = rotary_tables(index, tables)
    first = column * tokens.shape[0] + high * held

    spot = jnp.where(high == 0, column, 2 * columns - 1 - column)
    spots = lax.rem(spot + jnp.arange(2 * columns, dtype=jnp.int32), 2 * columns)
    far = spots >= columns
    ring_column = jnp.where(far, 2 * columns - 1 - spots, spots)
    ring_high = far.astype(jnp.int32)
    key_first = ring_column * tokens.shape[0] + ring_high * held
    key_index = (key_first[:, None] + jnp.arange(held, dtype=jnp.int32)[None, :]).reshape(-1)

    block = 256 if held % 256 == 0 else 128
    lists, counts = block_lists(first, key_index, block, held, tables)
    key_hot = segment_hot(key_index, tables).astype(F32)
    marks = jnp.pad(key_hot, ((0, 0), (HEAD_DIM, HEAD_DIM - key_hot.shape[1]))).astype(BF16)
    own_hot = segment_hot(index, tables).astype(F32)
    reach = jnp.sum(own_hot[:, :, None] * tables[2][None], axis=1)
    bars = jnp.pad((reach - 1.0) * BIG, ((0, 0), (HEAD_DIM, HEAD_DIM - reach.shape[1]))).astype(BF16)

    def exchange(value, axes):
        return lax.all_to_all(value, axes, split_axis=0, concat_axis=0, tiled=True)

    joint_blocks = gather(joint_weight, ALL_COL).reshape(columns, D, -1)
    gains = jnp.broadcast_to(jnp.stack([attention_gain, feed_gain])[None], (rows, 2, attention_gain.shape[0]))
    extended = jnp.concatenate([tokens.reshape(rows, own, -1), jnp.pad(gains, ((0, 0), (0, 14), (0, 0)))], axis=1)
    extended = exchange(extended, ROW)

    def plan(*places):
        keys = jnp.concatenate([key_index[i * held : j * held] for i, j in places])
        return (jnp.concatenate([marks[i * held : j * held] for i, j in places]), *block_lists(first, keys, block, held, tables))

    chips = 2 * columns
    plans = [plan((0, 2), (chips - 1, chips))]
    plans += [plan((s, s + 1), (chips - s, chips - s + 1)) for s in range(2, columns)]
    plans += [plan((columns, columns + 1))]
    (marks, lists, counts, plans), extended = lax.optimization_barrier(((marks, lists, counts, plans), extended))
    ahead, behind = ring_steps(columns)
    down_own = down_weight.T
    down_next, down_last = lax.ppermute(down_own, RING, ahead), lax.ppermute(down_own, RING, behind)
    down_fronts, down_backs = [], []

    def down_step(beside):
        nonlocal down_next, down_last
        beside, down_next, down_last = lax.optimization_barrier((beside, down_next, down_last))
        down_fronts.append(down_next)
        down_backs.append(down_last)
        if len(down_fronts) < columns - 1:
            down_next, down_last = lax.ppermute(down_next, RING, ahead), lax.ppermute(down_last, RING, behind)
        else:
            half = down_own.shape[0] // 2
            down_next = lax.ppermute(down_next[:half], RING, ahead)
            down_last = lax.ppermute(down_last[half:], RING, behind)
        return beside

    while len(down_fronts) < DOWN_STEPS:
        extended = down_step(extended)
    x, normed_one, joint_full, packed, value, gains = project_in(extended, joint_blocks, cosines, sines, bars)
    value, packed = lax.optimization_barrier((exchange(value, "core").reshape(held, -1), packed))
    packed = exchange(packed, "core").reshape(held, -1)
    width = gate_weight.shape[1]
    unit = width // 2 if width % 256 == 0 else width
    padding = jnp.zeros((output_weight.shape[1], -output_weight.shape[0] % unit), BF16)
    late = jnp.concatenate([gate_weight, up_weight, output_weight.T, padding], axis=1)
    late = gather(late, ALL_COL).reshape(columns, D, -1)
    pieces = []
    state = None
    to_next, to_last = lax.ppermute(value, RING, ahead), lax.ppermute(value, RING, behind)
    fronts, backs = [], []

    def attend(state, plan, some, ends):
        keys, lists_here, counts_here = plan
        return tuple(attention_stage(lists_here, counts_here, packed, some, keys, state, ends))

    middle = held // 2
    for step in range(1, columns):
        fronts.append(to_next)
        backs.append(to_last)
        if step < columns - 1:
            further = (lax.ppermute(to_next, RING, ahead), lax.ppermute(to_last, RING, behind))
        else:
            further = (lax.ppermute(to_next[:middle], RING, ahead), lax.ppermute(to_last[middle:], RING, behind))
        some = [value, to_last, to_next] if step == 1 else [to_last, to_next]
        if step == 1:
            while len(down_fronts) < columns - 1:
                to_next = down_step(to_next)
            cotangent, further = lax.optimization_barrier((cotangent, further))
            upstream = exchange(cotangent.reshape(rows, own, -1), ROW).transpose(1, 0, 2).reshape(own, D)
        state = attend(state, plans[step - 1], some, False)
        state, further = lax.optimization_barrier((state, further))
        if step == 1:
            down_mine = jnp.concatenate([down_own, *down_backs, down_next, down_last, *reversed(down_fronts)])
            down_mine, further = lax.optimization_barrier((down_mine.reshape(chips, *down_own.shape), further))
            down_others = lax.ppermute(down_mine, "core", [(0, 1), (1, 0)])
        to_next, to_last = further
    pieces = [value, *backs, to_next, to_last, *reversed(fronts)]
    upstream, state = lax.optimization_barrier((upstream, state))
    state = attend(state, plans[columns - 1], [to_next, to_last], True)
    attended, lse = lax.cond(
        jnp.any(state[1] != state[1]),
        lambda: tuple(attention_forward(lists, counts, packed, pieces, marks)),
        lambda: tuple(state),
    )
    attended_rows = exchange(attended.reshape(cores, own, -1), "core")

    steps = jnp.arange(chips, dtype=jnp.int32)
    away = jnp.where(steps % 2 == 0, steps // 2, chips - 1 - steps // 2) - spot
    down_places = jnp.concatenate([lax.rem(away + chips, chips), jnp.reshape(core, (1,))]).astype(jnp.int32)
    attended_rows, hidden, normed_two, output_full = project_out(attended_rows, late, x, gains, ATT // columns, late.shape[2] - 2 * width)
    mixed, gate_back, up_back, feed_out, normed_two_back = feed_forward(down_places, normed_two, upstream, late, down_mine, down_others)

    hidden_back, hidden_low, heads_back, gain_two_part = output_back(normed_two_back, hidden, upstream, gains, output_full)
    heads_back, mixed = lax.optimization_barrier((heads_back, mixed))
    heads_back = exchange(heads_back, "core").reshape(held, -1)
    feed_parts = gradient_parts(columns, rows, None, (normed_two, [gate_back, up_back]), (upstream, [mixed]))
    feed_parts, heads_back = lax.optimization_barrier((feed_parts, heads_back))
    feed_summed = scatter(feed_parts.reshape(-1, feed_parts.shape[3]), ALL_COL)
    output_parts = gradient_parts(columns, rows, gain_two_part[0], (hidden_low, [attended_rows]))

    query_backs, pair_rings = [], []
    for g in range(groups):
        heads_back = depart(heads_back, pair_rings)
        query_back, pair_back = attention_backward(g, lists, counts, packed, heads_back, attended, pieces, marks, lse)
        pair_back = pair_back.reshape(2 * columns, held, -1)
        query_backs.append(query_back)
        pair_back = after(pair_back, pair_rings)
        pair_rings.append(RingScatter(lambda s, half, v=pair_back: halves(v[s], half).astype(F32), columns))
    pair_rings[-1].launch()
    query_backs, feed_out = after((query_backs, feed_out), pair_rings[-1:])
    query_back = exchange(jnp.concatenate(query_backs, axis=1).reshape(cores, own, -1), "core")
    layer_low = (hidden + feed_out).astype(BF16).reshape(own, rows, -1).transpose(1, 0, 2)
    held_pairs = jnp.concatenate([ring.finish().astype(BF16) for ring in pair_rings], axis=1)
    held_pairs, query_back, layer_low, feed_summed, output_parts = lax.optimization_barrier(
        (held_pairs, query_back, layer_low, feed_summed, output_parts)
    )
    feed_summed = feed_summed.astype(F32)
    output_summed = scatter(output_parts.reshape(-1, output_parts.shape[3]), ALL_COL).astype(F32)
    pair_back = exchange(held_pairs.reshape(cores, own, -1), "core")
    layer_output = exchange(layer_low, ROW).reshape(rows * own, -1)
    joint_low, input_part, gain_one_part = joint_back(
        query_back, pair_back, cosines, sines, joint_full, x, gains, hidden_back, rows
    )
    joint_low, layer_output = lax.optimization_barrier((joint_low, layer_output))
    joint_parts = gradient_parts(columns, rows, gain_one_part[0], (normed_one, [joint_low]))
    joint_parts = joint_parts.reshape(2 * columns, cores, *joint_parts.shape[2:])
    places = ring_column * 2 + ring_high
    swap = [(0, 1), (1, 0)]
    joint_first = lax.dynamic_slice(joint_parts, (places[columns], 1 - core, 0, 0), (1, 1, *joint_parts.shape[2:]))[0, 0]
    joint_first = lax.ppermute(joint_first, "core", swap)
    joint_other = lax.dynamic_index_in_dim(joint_parts, 1 - core, 1, keepdims=False)
    joint_other = lax.ppermute(joint_other, "core", swap)

    def joint_part(s, half):
        mine = lax.dynamic_slice(joint_parts, (places[s], core, 0, 0), (1, 1, *joint_parts.shape[2:]))[0, 0]
        other = joint_first if s == columns else lax.dynamic_index_in_dim(joint_other, places[s], 0, keepdims=False)
        return halves(mine, half).astype(F32) + halves(other, half).astype(F32)

    joint_ring = RingScatter(joint_part, columns)
    input_gradient = exchange(input_part, ROW).reshape(rows * own, -1).astype(F32)
    joint_summed = joint_ring.finish()
    narrow, joined = ATT // columns, joint_weight.shape[1]
    return (
        layer_output,
        input_gradient,
        joint_summed[:, joined],
        joint_summed[:, :joined],
        output_summed[:, :narrow].T,
        output_summed[:, narrow],
        feed_summed[:, :width],
        feed_summed[:, width : 2 * width],
        feed_summed[:, 2 * width :].T,
    )


def solution(mesh):
    leaves, rows, columns = (mesh.shape[name] for name in ("leaf", "row", "col"))
    split = Mesh(mesh.devices.reshape(leaves, rows // 2, 2, columns), ("leaf", "high", "core", "col"))
    return jax.shard_map(
        per_device,
        mesh=split,
        in_specs=(
            P(("leaf", "col"), ROW),
            P(ROW),
            P(ROW, "col"),
            P("col", ROW),
            P(ROW),
            P(ROW, "col"),
            P(ROW, "col"),
            P("col", ROW),
            P(("leaf", "col"), ROW),
            P("leaf"),
            P("leaf"),
        ),
        out_specs=(
            P(("leaf", "col"), ROW),
            P(("leaf", "col"), ROW),
            P(("leaf", *ROW)),
            P(("leaf", *ROW), "col"),
            P(("leaf", "col"), ROW),
            P(("leaf", *ROW)),
            P(("leaf", *ROW), "col"),
            P(("leaf", *ROW), "col"),
            P(("leaf", "col"), ROW),
        ),
        check_vma=False,
    )
```

```python
import functools

import jax
import jax.numpy as jnp
from jax import lax
from jax.experimental import pallas as pl
from jax.experimental.pallas import tpu as pltpu
from jax.sharding import Mesh
from jax.sharding import PartitionSpec as P

D = 1152
HEADS = 18
KV_HEADS = 6
HEAD_DIM = 64
REPEAT = HEADS // KV_HEADS
ATT = HEADS * HEAD_DIM
KEYS = KV_HEADS * HEAD_DIM

EPSILON = 1e-05
THETA = 10000.0
BIG = 2.0**30
LOG2E = 1.4426950408889634
UNROLL = 8
BF16 = jnp.bfloat16
F32 = jnp.float32
NT = (((1,), (1,)), ((), ()))
NN = (((1,), (0,)), ((), ()))


def dg(a, b, dims):
    return lax.dot_general(a, b, dims, preferred_element_type=F32)


def tree_tables(segment_lengths, parents):
    count = segment_lengths.shape[0]
    labels = jnp.arange(count, dtype=jnp.int32)
    ends = jnp.sum(jnp.where(labels[None, :] <= labels[:, None], segment_lengths[None, :], 0), axis=1)
    starts = ends - segment_lengths
    parent_hot = parents[:, None] == labels[None, :]
    grand = jnp.sum(jnp.where(parent_hot, parents[None, :], 0), axis=1)
    self_mark = labels[:, None] == labels[None, :]
    grand_mark = grand[:, None] == labels[None, :]
    ancestry = (self_mark | parent_hot | grand_mark).astype(F32)
    strict = (parent_hot | grand_mark) & jnp.logical_not(self_mark)
    offsets = jnp.sum(jnp.where(strict, segment_lengths[None, :], 0), axis=1)
    return (ends, starts, ancestry, offsets)


def segment_hot(index, tables):
    ends, starts, _, _ = tables
    return (index[:, None] >= starts[None, :]) & (index[:, None] < ends[None, :])


def rotary_tables(index, tables):
    hot = segment_hot(index, tables)
    depth = index + jnp.sum(jnp.where(hot, (tables[3] - tables[1])[None, :], 0), axis=1)
    half = HEAD_DIM // 2
    rates = THETA ** (-jnp.arange(half, dtype=F32) / half)
    angles = depth.astype(F32)[:, None] * rates[None, :]
    cosines, sines = jnp.cos(angles), jnp.sin(angles)
    return (jnp.concatenate([cosines] * 4, axis=1), jnp.concatenate([-sines, sines] * 2, axis=1))


def block_lists(first, key_index, block, held, tables):
    ends, starts, ancestry, _ = tables
    blocks = held // block
    key_low = key_index[::block]
    labels = jnp.arange(key_low.shape[0], dtype=jnp.int32)
    low = first + jnp.arange(blocks, dtype=jnp.int32) * block
    high = low + block
    query_has = ((starts[None, :] < high[:, None]) & (ends[None, :] > low[:, None])).astype(F32)
    key_has = ((starts[None, :] < key_low[:, None] + block) & (ends[None, :] > key_low[:, None])).astype(F32)
    reach = jnp.sum(query_has[:, :, None] * ancestry[None], axis=1)
    seen = jnp.sum(reach[:, None, :] * key_has[None], axis=2) > 0.5
    seen = seen & (key_low[None, :] < low[:, None])
    before = labels[None, :] < labels[:, None]
    rank = jnp.sum((seen[:, None, :] & before[None]).astype(jnp.int32), axis=2)
    place = seen[:, None, :] & (rank[:, None, :] == labels[None, :, None])
    lists = jnp.sum(jnp.where(place, labels[None, None, :], 0), axis=2)
    counts = jnp.sum(seen.astype(jnp.int32), axis=1)
    own = jnp.sum(jnp.where(key_low[None, :] == low[:, None], labels[None, :], 0), axis=1)
    lists = jnp.where(labels[None, :] == counts[:, None], own[:, None], lists)
    return (lists.reshape(-1).astype(jnp.int32), counts.astype(jnp.int32))


def cascade(count, unroll, steps):
    def body(i, c):
        steps(i * unroll, unroll)
        return c

    whole = count // unroll
    lax.fori_loop(0, whole, body, 0)
    start = whole * unroll
    size = unroll // 2
    while size:
        some = ((count - start) // size) > 0
        pl.when(some)(functools.partial(steps, start, size))
        start = start + jnp.where(some, size, 0)
        size //= 2


def causal(scores, heads):
    rows = lax.broadcasted_iota(jnp.int32, scores.shape, 0)
    columns = lax.rem(lax.broadcasted_iota(jnp.int32, scores.shape, 1), scores.shape[1] // heads)
    return jnp.where(rows <= columns, scores, -BIG)


def stacked(ref):
    value, wide = ref[...], 2 * HEAD_DIM
    return jnp.concatenate([value[:, h * wide : (h + 1) * wide] for h in range(value.shape[1] // wide)], axis=0)


def beside(value, heads):
    rows = value.shape[0] // heads
    return jnp.concatenate([value[h * rows : (h + 1) * rows] for h in range(heads)], axis=1)


def left_half(shape):
    return lax.broadcasted_iota(jnp.int32, shape, 1) < HEAD_DIM


def fetch(pieces, group, kv_ref, sems):
    copies, start = [], 0
    for i, piece in enumerate(pieces):
        lanes = pl.ds(pl.multiple_of(group * 2 * HEAD_DIM, 2 * HEAD_DIM), 2 * HEAD_DIM)
        target = kv_ref.at[pl.ds(start, piece.shape[0])]
        copies.append(pltpu.make_async_copy(piece.at[:, lanes], target, sems.at[i]))
        start += piece.shape[0]
    for copy in copies:
        copy.start()
    for copy in copies:
        copy.wait()


def forward_kernel(lists, counts, q_ref, mark_ref, *refs):
    *pieces, o_ref, lse_ref, top_ref, sum_ref, kv_ref, vt_ref, sems = refs
    block = pl.program_id(1)
    heads, rows = q_ref.shape[1] // (2 * HEAD_DIM), q_ref.shape[0]
    total = kv_ref.shape[0]
    stride = total // rows
    count = counts[block]

    @pl.when(block == 0)
    def _():
        fetch(pieces, pl.program_id(0), kv_ref, sems)

        def flip(i, c):
            k0 = pl.multiple_of(i * rows, rows)
            turned = kv_ref[pl.ds(k0, rows), :].T
            vt_ref[:HEAD_DIM, pl.ds(k0, rows)] = turned[HEAD_DIM:]
            return c

        lax.fori_loop(0, stride, flip, 0)
        tail = (vt_ref.shape[0] - HEAD_DIM, total)
        vt_ref[HEAD_DIM:] = jnp.where(lax.broadcasted_iota(jnp.int32, tail, 0) == 0, 1.0, 0.0).astype(BF16)

    def queries():
        return stacked(q_ref)

    def blocks(start, n):
        offs = [pl.multiple_of(lists[block * stride + start + u] * rows, rows) for u in range(n)]
        kv = jnp.concatenate([kv_ref[pl.ds(k0, rows), :] for k0 in offs], axis=0)
        mark = jnp.concatenate([mark_ref[pl.ds(k0, rows), :] for k0 in offs], axis=0)
        vt = jnp.concatenate([vt_ref[:, pl.ds(k0, rows)] for k0 in offs], axis=1)
        return jnp.where(left_half(kv.shape), kv, mark), vt

    def begin():
        k, vt = blocks(count, 1)
        scores = causal(dg(k, queries(), NT), heads)
        top = jnp.max(scores, axis=0, keepdims=True)
        top_ref[...] = top
        sum_ref[...] = dg(vt, jnp.exp2(scores - top).astype(BF16), NN)

    def steps(start, n):
        k, vt = blocks(start, n)
        weights = jnp.exp2(dg(k, queries(), NT) - top_ref[...]).astype(BF16)
        sum_ref[...] += dg(vt, weights, NN)

    begin()
    cascade(count, UNROLL, steps)

    @pl.when(jnp.logical_not(jnp.max(sum_ref[HEAD_DIM : HEAD_DIM + 1, :]) < 2.0**100))
    def _():
        begin()

        def online(n, c):
            k, vt = blocks(n, 1)
            scores = dg(k, queries(), NT)
            old = top_ref[...]
            new = jnp.maximum(old, jnp.max(scores, axis=0, keepdims=True))
            top_ref[...] = new
            sum_ref[...] = sum_ref[...] * jnp.exp2(old - new) + dg(vt, jnp.exp2(scores - new).astype(BF16), NN)
            return c

        lax.fori_loop(0, count, online, 0)

    total_row = sum_ref[HEAD_DIM : HEAD_DIM + 1, :]
    spread = jnp.concatenate([jnp.zeros((HEAD_DIM, heads * rows), F32), sum_ref[:HEAD_DIM, :] / total_row], axis=0)
    o_ref[...] = beside(spread.T.astype(BF16), heads)
    lse_ref[0, 0] = top_ref[...] + jnp.log2(total_row)


def attention_forward(lists, counts, q, pieces, marks):
    tokens, wide, heads = q.shape[0], 2 * HEAD_DIM, REPEAT
    groups = q.shape[1] // (wide * heads)
    total = marks.shape[0]
    blocks = counts.shape[0]
    rows = tokens // blocks
    tall = HEAD_DIM + 16
    return pl.pallas_call(
        forward_kernel,
        grid_spec=pltpu.PrefetchScalarGridSpec(
            num_scalar_prefetch=2,
            grid=(groups, blocks),
            in_specs=[
                pl.BlockSpec((rows, heads * wide), lambda g, b, *_: (b, g)),
                pl.BlockSpec((total, wide), lambda g, b, *_: (0, 0)),
                *(pl.BlockSpec(memory_space=pl.ANY) for _ in pieces),
            ],
            out_specs=[
                pl.BlockSpec((rows, heads * wide), lambda g, b, *_: (b, g)),
                pl.BlockSpec((1, 1, 1, heads * rows), lambda g, b, *_: (g, b, 0, 0)),
            ],
            scratch_shapes=[
                pltpu.VMEM((1, heads * rows), F32),
                pltpu.VMEM((tall, heads * rows), F32),
                pltpu.VMEM((total, wide), BF16),
                pltpu.VMEM((tall, total), BF16),
                pltpu.SemaphoreType.DMA((len(pieces),)),
            ],
        ),
        out_shape=[
            jax.ShapeDtypeStruct((tokens, groups * heads * wide), BF16),
            jax.ShapeDtypeStruct((groups, blocks, 1, heads * rows), F32),
        ],
        compiler_params=pltpu.CompilerParams(vmem_limit_bytes=48 * 2**20),
        cost_estimate=pl.CostEstimate(
            flops=groups * heads * tokens * total * 256, bytes_accessed=groups * total * 512, transcendentals=0
        ),
        name="attention_forward",
    )(lists, counts, q, marks, *pieces)


def stage_kernel(begins, ends, lists, counts, q_ref, mark_ref, *refs):
    refs = list(refs)
    sums_in, tops_in = ([refs.pop(0), refs.pop(0)] if not begins else (None, None))
    *pieces, first_ref, second_ref, top_ref, sum_ref, kv_ref, vt_ref, sems = refs
    block = pl.program_id(1)
    heads, rows = q_ref.shape[1] // (2 * HEAD_DIM), q_ref.shape[0]
    total = kv_ref.shape[0]
    stride = total // rows
    count = counts[block]

    @pl.when(block == 0)
    def _():
        fetch(pieces, pl.program_id(0), kv_ref, sems)

        def flip(i, c):
            k0 = pl.multiple_of(i * rows, rows)
            turned = kv_ref[pl.ds(k0, rows), :].T
            vt_ref[:HEAD_DIM, pl.ds(k0, rows)] = turned[HEAD_DIM:]
            return c

        lax.fori_loop(0, stride, flip, 0)
        tail = (vt_ref.shape[0] - HEAD_DIM, total)
        vt_ref[HEAD_DIM:] = jnp.where(lax.broadcasted_iota(jnp.int32, tail, 0) == 0, 1.0, 0.0).astype(BF16)

    def queries():
        return stacked(q_ref)

    def blocks(start, n):
        offs = [pl.multiple_of(lists[block * stride + start + u] * rows, rows) for u in range(n)]
        kv = jnp.concatenate([kv_ref[pl.ds(k0, rows), :] for k0 in offs], axis=0)
        mark = jnp.concatenate([mark_ref[pl.ds(k0, rows), :] for k0 in offs], axis=0)
        vt = jnp.concatenate([vt_ref[:, pl.ds(k0, rows)] for k0 in offs], axis=1)
        return jnp.where(left_half(kv.shape), kv, mark), vt

    if begins:
        k, vt = blocks(count, 1)
        scores = causal(dg(k, queries(), NT), heads)
        top = jnp.max(scores, axis=0, keepdims=True)
        top_ref[...] = top
        sum_ref[...] = dg(vt, jnp.exp2(scores - top).astype(BF16), NN)
    else:
        top_ref[...] = tops_in[0, 0]
        sum_ref[...] = sums_in[0, 0]

    def steps(start, n):
        k, vt = blocks(start, n)
        weights = jnp.exp2(dg(k, queries(), NT) - top_ref[...]).astype(BF16)
        sum_ref[...] += dg(vt, weights, NN)

    cascade(count, UNROLL, steps)
    if ends:
        total_row = sum_ref[HEAD_DIM : HEAD_DIM + 1, :]
        spread = jnp.concatenate([jnp.zeros((HEAD_DIM, heads * rows), F32), sum_ref[:HEAD_DIM, :] / total_row], axis=0)
        first_ref[...] = beside(spread.T.astype(BF16), heads)
        second_ref[0, 0] = jnp.where(total_row < 2.0**100, top_ref[...] + jnp.log2(total_row), jnp.nan)
    else:
        first_ref[0, 0] = sum_ref[...]
        second_ref[0, 0] = top_ref[...]


def attention_stage(lists, counts, q, pieces, marks, state, ends):
    tokens, wide, heads = q.shape[0], 2 * HEAD_DIM, REPEAT
    groups = q.shape[1] // (wide * heads)
    total = marks.shape[0]
    blocks = counts.shape[0]
    rows = tokens // blocks
    tall = HEAD_DIM + 16
    lanes = heads * rows
    held_specs = [
        pl.BlockSpec((1, 1, tall, lanes), lambda g, b, *_: (g, b, 0, 0)),
        pl.BlockSpec((1, 1, 1, lanes), lambda g, b, *_: (g, b, 0, 0)),
    ]
    tops = jax.ShapeDtypeStruct((groups, blocks, 1, lanes), F32)
    if ends:
        out_specs = [pl.BlockSpec((rows, heads * wide), lambda g, b, *_: (b, g)), held_specs[1]]
        out_shape = [jax.ShapeDtypeStruct((tokens, groups * heads * wide), BF16), tops]
    else:
        out_specs = held_specs
        out_shape = [jax.ShapeDtypeStruct((groups, blocks, tall, lanes), F32), tops]
    return pl.pallas_call(
        functools.partial(stage_kernel, state is None, ends),
        grid_spec=pltpu.PrefetchScalarGridSpec(
            num_scalar_prefetch=2,
            grid=(groups, blocks),
            in_specs=[
                pl.BlockSpec((rows, heads * wide), lambda g, b, *_: (b, g)),
                pl.BlockSpec((total, wide), lambda g, b, *_: (0, 0)),
                *([] if state is None else held_specs),
                *(pl.BlockSpec(memory_space=pl.ANY) for _ in pieces),
            ],
            out_specs=out_specs,
            scratch_shapes=[
                pltpu.VMEM((1, lanes), F32),
                pltpu.VMEM((tall, lanes), F32),
                pltpu.VMEM((total, wide), BF16),
                pltpu.VMEM((tall, total), BF16),
                pltpu.SemaphoreType.DMA((len(pieces),)),
            ],
        ),
        out_shape=out_shape,
        compiler_params=pltpu.CompilerParams(vmem_limit_bytes=40 * 2**20),
        cost_estimate=pl.CostEstimate(
            flops=groups * heads * tokens * total * 256, bytes_accessed=groups * total * 512, transcendentals=0
        ),
        name="attention_stage",
    )(lists, counts, q, marks, *(() if state is None else state), *pieces)


def backward_kernel(group, lists, counts, q_ref, do_ref, o_ref, mark_ref, lse_ref, *refs):
    *pieces, dq_ref, dkv_ref, dq_sum, dkv_sum, kv_ref, kt_ref, delta_ref, sems = refs
    block = pl.program_id(0)
    heads, rows = q_ref.shape[1] // (2 * HEAD_DIM), q_ref.shape[0]
    total = kv_ref.shape[0]
    stride = total // rows
    count = counts[block]

    @pl.when(block == 0)
    def _():
        dkv_sum[...] = jnp.zeros(dkv_sum.shape, F32)
        fetch(pieces, group, kv_ref, sems)

        def flip(i, c):
            k0 = pl.multiple_of(i * rows, rows)
            turned = kv_ref[pl.ds(k0, rows), :].T
            kt_ref[:, pl.ds(k0, rows)] = turned[:HEAD_DIM]
            return c

        lax.fori_loop(0, stride, flip, 0)

    dq_sum[...] = jnp.zeros(dq_sum.shape, F32)
    products = stacked(do_ref).astype(F32) * stacked(o_ref).astype(F32)
    delta_ref[...] = jnp.sum(products.T, axis=0, keepdims=True)

    def steps(start, n, masked):
        q, do = stacked(q_ref), stacked(do_ref)
        offs = [pl.multiple_of(lists[block * stride + start + u] * rows, rows) for u in range(n)]
        kv = jnp.concatenate([kv_ref[pl.ds(k0, rows), :] for k0 in offs], axis=0)
        mark = jnp.concatenate([mark_ref[pl.ds(k0, rows), :] for k0 in offs], axis=0)
        kt = jnp.concatenate([kt_ref[:, pl.ds(k0, rows)] for k0 in offs], axis=1)
        scores = dg(jnp.where(left_half(kv.shape), kv, mark), q, NT) - lse_ref[0, 0]
        if masked:
            scores = causal(scores, heads)
        chances = jnp.exp2(scores)
        back = dg(kv, do, NT) - delta_ref[...]
        score_back = (chances * back).astype(BF16)
        only_q = jnp.where(left_half(q.shape), q, jnp.zeros_like(q))
        update = dg(score_back, only_q, NN) + dg(chances.astype(BF16), do, NN)
        dq_sum[...] += dg(kt, score_back, NN)
        for u in range(n):
            dkv_sum[pl.ds(offs[u], rows), :] += update[u * rows : (u + 1) * rows]

    steps(count, 1, True)
    cascade(count, UNROLL, lambda start, n: steps(start, n, False))
    spread = jnp.concatenate([dq_sum[...] * HEAD_DIM**-0.5, jnp.zeros(dq_sum.shape, F32)], axis=0)
    dq_ref[...] = beside(spread.T.astype(BF16), heads)

    @pl.when(block == pl.num_programs(0) - 1)
    def _():
        summed = dkv_sum[...]
        dkv_ref[...] = jnp.where(left_half(summed.shape), summed * (1.0 / LOG2E), summed).astype(BF16)


def attention_backward(group, lists, counts, q, do, o, pieces, marks, lse):
    tokens, wide, heads = q.shape[0], 2 * HEAD_DIM, REPEAT
    total = marks.shape[0]
    blocks = counts.shape[0]
    rows = tokens // blocks
    block = pl.BlockSpec((rows, heads * wide), lambda b, *_: (b, group))
    return pl.pallas_call(
        functools.partial(backward_kernel, group),
        grid_spec=pltpu.PrefetchScalarGridSpec(
            num_scalar_prefetch=2,
            grid=(blocks,),
            in_specs=[
                block,
                block,
                block,
                pl.BlockSpec((total, wide), lambda b, *_: (0, 0)),
                pl.BlockSpec((1, 1, 1, heads * rows), lambda b, *_: (group, b, 0, 0)),
                *(pl.BlockSpec(memory_space=pl.ANY) for _ in pieces),
            ],
            out_specs=[
                pl.BlockSpec((rows, heads * wide), lambda b, *_: (b, 0)),
                pl.BlockSpec((total, wide), lambda b, *_: (0, 0)),
            ],
            scratch_shapes=[
                pltpu.VMEM((HEAD_DIM, heads * rows), F32),
                pltpu.VMEM((total, wide), F32),
                pltpu.VMEM((total, wide), BF16),
                pltpu.VMEM((HEAD_DIM, total), BF16),
                pltpu.VMEM((1, heads * rows), F32),
                pltpu.SemaphoreType.DMA((len(pieces),)),
            ],
        ),
        out_shape=[
            jax.ShapeDtypeStruct((tokens, heads * wide), BF16),
            jax.ShapeDtypeStruct((total, wide), BF16),
        ],
        compiler_params=pltpu.CompilerParams(vmem_limit_bytes=60 * 2**20),
        cost_estimate=pl.CostEstimate(flops=heads * tokens * total * 640, bytes_accessed=total * 1024, transcendentals=0),
        name="attention_backward",
    )(lists, counts, q, do, o, marks, lse, *pieces)


def roll_half(value):
    return pltpu.roll(value, HEAD_DIM, 1)


def swap_quarters(value):
    quarter = HEAD_DIM // 2
    lane = lax.broadcasted_iota(jnp.int32, value.shape, 1)
    first = lax.rem(lane, HEAD_DIM) < quarter
    return jnp.where(first, pltpu.roll(value, value.shape[1] - quarter, 1), pltpu.roll(value, quarter, 1))


def root_mean(value):
    return lax.rsqrt(jnp.sum(value * value, axis=1, keepdims=True) / D + EPSILON)


def project_kernel(x4_ref, w_ref, cos_ref, sin_ref, bars_ref, x_ref, xa_ref, full_ref, query_ref, pair_ref, gains_ref, joint_ref):
    own = x_ref.shape[0]
    wide = 2 * HEAD_DIM
    x = jnp.concatenate([x4_ref[r, :own, :] for r in range(x4_ref.shape[0])], axis=1)
    gains = jnp.concatenate([x4_ref[r, own : own + 16, :] for r in range(x4_ref.shape[0])], axis=1).astype(F32)
    x_ref[...] = x
    gains_ref[...] = gains[:8]
    value = x.astype(F32)
    xa_ref[...] = (value * root_mean(value) * gains[0:1]).astype(BF16)
    full_ref[...] = jnp.concatenate([w_ref[c] for c in range(w_ref.shape[0])], axis=1)
    joint_ref[...] = dg(xa_ref[...], full_ref[...], NN).astype(BF16)
    left = left_half((own, wide))
    bars = bars_ref[...].astype(F32)
    heads, pairs = HEADS // 2, KV_HEADS // 2

    def part(i):
        return joint_ref[:, i * wide : (i + 1) * wide].astype(F32)

    def turned(i):
        value = part(i)
        return value * cos_ref[...] + swap_quarters(value) * sin_ref[...]

    for i in range(HEADS // 2):
        value = turned(i) * (LOG2E * HEAD_DIM**-0.5)
        for j, head in ((2 * i, value), (2 * i + 1, roll_half(value))):
            start = (j % heads) * wide
            query_ref[j // heads, :, start : start + wide] = jnp.where(left, head, bars).astype(BF16)
    for i in range(KV_HEADS // 2):
        key = turned(HEADS // 2 + i)
        value = part(HEADS // 2 + KV_HEADS // 2 + i)
        for j, both in (
            (2 * i, jnp.where(left, key, roll_half(value))),
            (2 * i + 1, jnp.where(left, roll_half(key), value)),
        ):
            start = (j % pairs) * wide
            pair_ref[j // pairs, :, start : start + wide] = both.astype(BF16)


def project_in(x4, weight, cosines, sines, bars):
    own = cosines.shape[0]
    shapes = [
        jax.ShapeDtypeStruct((own, D), BF16),
        jax.ShapeDtypeStruct((own, D), BF16),
        jax.ShapeDtypeStruct((D, ATT + 2 * KEYS), BF16),
        jax.ShapeDtypeStruct((2, own, ATT), BF16),
        jax.ShapeDtypeStruct((2, own, KEYS), BF16),
        jax.ShapeDtypeStruct((8, D), F32),
    ]
    return pl.pallas_call(
        project_kernel,
        out_shape=shapes,
        scratch_shapes=[pltpu.VMEM((own, ATT + 2 * KEYS), BF16)],
        compiler_params=pltpu.CompilerParams(vmem_limit_bytes=56 * 2**20),
        cost_estimate=pl.CostEstimate(flops=2 * own * D * (ATT + 2 * KEYS), bytes_accessed=2**24, transcendentals=0),
        name="project_in",
    )(x4, weight, cosines, sines, bars)


def output_kernel(width, o_ref, w_ref, x_ref, gains_ref, rows_ref, hidden_ref, normed_ref, full_ref):
    wide = 2 * HEAD_DIM
    heads = HEADS // 2
    left = left_half((x_ref.shape[0], wide))
    for i in range(HEADS // 2):
        first, second = (
            o_ref[j // heads, :, (j % heads) * wide : (j % heads + 1) * wide] for j in (2 * i, 2 * i + 1)
        )
        first = roll_half(first.astype(F32))
        rows_ref[:, i * wide : (i + 1) * wide] = jnp.where(left, first, second.astype(F32)).astype(BF16)
    full_ref[...] = jnp.concatenate([w_ref[c, :, :width] for c in range(w_ref.shape[0])], axis=1)
    hidden = x_ref[...].astype(F32) + dg(rows_ref[...], full_ref[...], NT)
    hidden_ref[...] = hidden
    normed_ref[...] = (hidden * root_mean(hidden) * gains_ref[1:2]).astype(BF16)


def project_out(o, late, x, gains, width, padded):
    own = x.shape[0]
    place = late.shape[2] // padded - 1
    return pl.pallas_call(
        functools.partial(output_kernel, width),
        grid=(1,),
        in_specs=[
            pl.BlockSpec(o.shape, lambda i: (0, 0, 0)),
            pl.BlockSpec((late.shape[0], D, padded), lambda i: (0, 0, place)),
            pl.BlockSpec(x.shape, lambda i: (0, 0)),
            pl.BlockSpec(gains.shape, lambda i: (0, 0)),
        ],
        out_specs=[pl.BlockSpec((own, D), lambda i: (0, 0))] * 3 + [pl.BlockSpec((D, ATT), lambda i: (0, 0))],
        out_shape=[
            jax.ShapeDtypeStruct((own, ATT), BF16),
            jax.ShapeDtypeStruct((own, D), F32),
            jax.ShapeDtypeStruct((own, D), BF16),
            jax.ShapeDtypeStruct((D, ATT), BF16),
        ],
        compiler_params=pltpu.CompilerParams(vmem_limit_bytes=56 * 2**20),
        cost_estimate=pl.CostEstimate(flops=2 * own * D * ATT, bytes_accessed=2**24, transcendentals=0),
        name="project_out",
    )(o, late, x, gains)


def norm_back(upstream, value, gain):
    scale = root_mean(value)
    weighted = upstream * gain
    inner = jnp.sum(weighted * value, axis=1, keepdims=True)
    gain_back = jnp.sum(upstream * value * scale, axis=0, keepdims=True)
    return scale * weighted - value * (scale * scale * scale * inner / D), gain_back


def output_back_kernel(back_ref, hidden_ref, upstream_ref, gains_ref, full_ref, hidden_back_ref, low_ref, do_ref, sums_ref):
    wide = 2 * HEAD_DIM
    heads = HEADS // 2
    part, sums = norm_back(back_ref[...], hidden_ref[...], gains_ref[1:2])
    hidden_back = upstream_ref[...].astype(F32) + part
    hidden_back_ref[...] = hidden_back
    low_ref[...] = hidden_back.astype(BF16)
    sums_ref[...] = jnp.broadcast_to(sums, sums_ref.shape)
    attended_back = dg(low_ref[...], full_ref[...], NN)
    left = left_half((low_ref.shape[0], wide))
    for i in range(HEADS // 2):
        value = attended_back[:, i * wide : (i + 1) * wide]
        for j, head in ((2 * i, roll_half(value)), (2 * i + 1, value)):
            start = (j % heads) * wide
            do_ref[j // heads, :, start : start + wide] = jnp.where(left, 0.0, head).astype(BF16)


def output_back(back, hidden, upstream, gains, full):
    own = back.shape[0]
    return pl.pallas_call(
        output_back_kernel,
        out_shape=[
            jax.ShapeDtypeStruct((own, D), F32),
            jax.ShapeDtypeStruct((own, D), BF16),
            jax.ShapeDtypeStruct((2, own, ATT), BF16),
            jax.ShapeDtypeStruct((8, D), F32),
        ],
        compiler_params=pltpu.CompilerParams(vmem_limit_bytes=56 * 2**20),
        cost_estimate=pl.CostEstimate(flops=2 * own * D * ATT, bytes_accessed=2**24, transcendentals=0),
        name="output_back",
    )(back, hidden, upstream, gains, full)


def joint_back_kernel(query_ref, pair_ref, cos_ref, sin_ref, full_ref, x_ref, gains_ref, hidden_back_ref, joint_ref, out_ref, sums_ref):
    wide = 2 * HEAD_DIM
    heads, pairs = HEADS // 2, KV_HEADS // 2
    left = left_half((x_ref.shape[0], wide))

    def queries(j):
        return query_ref[j // heads, :, (j % heads) * wide : (j % heads + 1) * wide].astype(F32)

    def both(j):
        start = (j % pairs) * wide
        return pair_ref[j // pairs, :, start : start + wide].astype(F32)

    def store(i, value):
        joint_ref[:, i * wide : (i + 1) * wide] = value.astype(BF16)

    def back(value):
        return value * cos_ref[...] - swap_quarters(value) * sin_ref[...]

    for i in range(HEADS // 2):
        store(i, back(jnp.where(left, queries(2 * i), roll_half(queries(2 * i + 1)))))
    for i in range(KV_HEADS // 2):
        first, second = both(2 * i), both(2 * i + 1)
        store(HEADS // 2 + i, back(jnp.where(left, first, roll_half(second))))
        store(HEADS // 2 + KV_HEADS // 2 + i, jnp.where(left, roll_half(first), second))
    upstream = dg(joint_ref[...], full_ref[...], NT)
    part, sums = norm_back(upstream, x_ref[...].astype(F32), gains_ref[0:1])
    total = (hidden_back_ref[...] + part).astype(BF16)
    features = out_ref.shape[2]
    for r in range(out_ref.shape[0]):
        out_ref[r] = total[:, r * features : (r + 1) * features]
    sums_ref[...] = jnp.broadcast_to(sums, sums_ref.shape)


def joint_back(queries, pairs, cosines, sines, full, x, gains, hidden_back, rows):
    own = x.shape[0]
    return pl.pallas_call(
        joint_back_kernel,
        out_shape=[
            jax.ShapeDtypeStruct((own, ATT + 2 * KEYS), BF16),
            jax.ShapeDtypeStruct((rows, own, D // rows), BF16),
            jax.ShapeDtypeStruct((8, D), F32),
        ],
        compiler_params=pltpu.CompilerParams(vmem_limit_bytes=56 * 2**20),
        cost_estimate=pl.CostEstimate(flops=2 * own * D * (ATT + 2 * KEYS), bytes_accessed=2**24, transcendentals=0),
        name="joint_back",
    )(queries, pairs, cosines, sines, full, x, gains, hidden_back)


def feed_kernel(normed_ref, back_ref, gate_ref, up_ref, down_ref, mixed_ref, gate_back_ref, up_back_ref, out_ref, normed_back_ref):
    @pl.when(pl.program_id(0) == 0)
    def _():
        out_ref[...] = jnp.zeros(out_ref.shape, F32)
        normed_back_ref[...] = jnp.zeros(normed_back_ref.shape, F32)

    gate = dg(normed_ref[...], gate_ref[0], NN)
    up_value = dg(normed_ref[...], up_ref[0], NN)
    mixed_back = dg(back_ref[...], down_ref[0], NN)
    sigmoid = jax.nn.sigmoid(gate)
    silu = gate * sigmoid
    mixed = (silu * up_value).astype(BF16)
    gate_back = (mixed_back * up_value * (sigmoid * (1.0 + gate * (1.0 - sigmoid)))).astype(BF16)
    up_back = (mixed_back * silu).astype(BF16)
    mixed_ref[...] = mixed
    gate_back_ref[...] = gate_back
    up_back_ref[...] = up_back
    out_ref[...] += dg(mixed, down_ref[0], NT)
    normed_back_ref[...] += dg(gate_back, gate_ref[0], NT) + dg(up_back, up_ref[0], NT)


def feed_forward(normed, back, late, width):
    tokens = normed.shape[0]
    columns = late.shape[0]
    whole = pl.BlockSpec((tokens, D), lambda c: (0, 0))
    blocks = [pl.BlockSpec((1, D, width), lambda c, k=k: (c, 0, k)) for k in range(3)]
    out = pl.BlockSpec((tokens, width), lambda c: (0, c))
    return pl.pallas_call(
        feed_kernel,
        grid=(columns,),
        in_specs=[whole, whole, *blocks],
        out_specs=[out, out, out, whole, whole],
        out_shape=[jax.ShapeDtypeStruct((tokens, columns * width), BF16)] * 3 + [jax.ShapeDtypeStruct((tokens, D), F32)] * 2,
        compiler_params=pltpu.CompilerParams(vmem_limit_bytes=62 * 2**20),
        cost_estimate=pl.CostEstimate(
            flops=12 * tokens * D * columns * width, bytes_accessed=6 * D * columns * width, transcendentals=0
        ),
        name="feed_forward",
    )(normed, back, late, late, late)


def gradient_kernel(counts, blocked, summed, *refs):
    refs = list(refs)
    sets = [(refs.pop(0), [refs.pop(0) for _ in range(n)]) for n in counts]
    sums_ref = refs.pop(0) if summed else None
    out_ref, turned, held = refs[0], refs[1 : 1 + len(sets)], refs[1 + len(sets) :]
    step = pl.program_id(0)
    rows = out_ref.shape[1]
    features = sets[0][0].shape[1] // rows
    rights = [right for _, some in sets for right in some]
    whole = [right for right, flag in zip(rights, blocked, strict=True) if not flag]

    @pl.when(step == 0)
    def _():
        for (left, _), target in zip(sets, turned, strict=True):
            target[...] = left[...].T
        for right, block in zip(whole, held, strict=True):
            width = block.shape[2]
            for c in range(block.shape[0]):
                block[c] = right[:, c * width : (c + 1) * width]

    spare, flags, start = list(held), list(blocked), 0
    for (_, some), target in zip(sets, turned, strict=True):
        for right in some:
            value = right[...] if flags.pop(0) else spare.pop(0)[step]
            width = value.shape[1]
            part = dg(target[...], value, NN).astype(BF16)
            for r in range(rows):
                out_ref[0, r, :, start : start + width] = part[r * features : (r + 1) * features]
            start += width
    if summed:
        tail = (rows, features, out_ref.shape[3] - start)
        out_ref[0, :, :, start:] = jnp.broadcast_to(sums_ref[...], tail).astype(BF16)


def gradient_parts(columns, rows, sums, *sets):
    tokens = sets[0][0].shape[0]
    features = D // rows
    operands, specs, turned, held, blocked, wide = [], [], [], [], [], 0
    for left, rights in sets:
        operands.append(left)
        specs.append(pl.BlockSpec(left.shape, lambda c: (0, 0)))
        turned.append(pltpu.VMEM((left.shape[1], tokens), BF16))
        for right in rights:
            width = right.shape[1] // columns
            operands.append(right)
            wide += width
            if width % 128 == 0:
                specs.append(pl.BlockSpec((tokens, width), lambda c: (0, c)))
                blocked.append(True)
            else:
                specs.append(pl.BlockSpec(right.shape, lambda c: (0, 0)))
                held.append(pltpu.VMEM((columns, tokens, width), BF16))
                blocked.append(False)
    if sums is not None:
        wide = (wide // 128 + 1) * 128
        operands.append(sums.reshape(rows, features, 1))
        specs.append(pl.BlockSpec((rows, features, 1), lambda c: (0, 0, 0)))
    shape = (columns, rows, features, wide)
    return pl.pallas_call(
        functools.partial(gradient_kernel, [len(rights) for _, rights in sets], blocked, sums is not None),
        grid=(columns,),
        in_specs=specs,
        out_specs=pl.BlockSpec((1, *shape[1:]), lambda c: (c, 0, 0, 0)),
        out_shape=jax.ShapeDtypeStruct(shape, BF16),
        scratch_shapes=[*turned, *held],
        compiler_params=pltpu.CompilerParams(vmem_limit_bytes=60 * 2**20),
        cost_estimate=pl.CostEstimate(
            flops=2 * tokens * D * wide * columns, bytes_accessed=2 * D * wide * columns, transcendentals=0
        ),
        name="gradient_parts",
    )(*operands)


ROW = ("high", "core")
ALL_ROW = ("high", "core", "col")
ALL_COL = ("col", "high", "core")
RING = ("high", "col")


def ring_steps(columns):
    path = [*range(columns), *reversed(range(columns, 2 * columns))]
    ahead = [(path[i], path[(i + 1) % len(path)]) for i in range(len(path))]
    return ahead, [(b, a) for a, b in ahead]


class RingScatter:
    def __init__(self, part, columns):
        self.part, (self.ahead, self.behind), self.count = part, ring_steps(columns), 2 * columns
        self.left = self.count // 2
        self.arrived = None
        self.ready = (part(self.left, 0).astype(BF16), part(self.left, 1).astype(BF16))

    def launch(self):
        out, back = self.ready
        self.arrived = (lax.ppermute(out, RING, self.ahead), lax.ppermute(back, RING, self.behind))
        self.ready = None
        self.left -= 1

    def prepare(self):
        out, back = self.part(self.left, None), self.part(self.count - self.left, None)
        front, rear = (v.astype(F32) for v in self.arrived)
        half = front.shape[0]
        if half == out.shape[0]:
            out, back = out + front, back + rear
        else:
            out = jnp.concatenate([out[:half] + front, out[half:]], axis=0)
            back = jnp.concatenate([back[:half], back[half:] + rear], axis=0)
        self.ready = (out.astype(BF16), back.astype(BF16))

    def finish(self):
        while self.left or self.ready:
            if self.ready is None:
                self.prepare()
            self.ready = lax.optimization_barrier(self.ready)
            self.launch()
        return self.part(0, None) + self.arrived[0].astype(F32) + self.arrived[1].astype(F32)


def after(value, rings):
    value, arrived = lax.optimization_barrier((value, [ring.arrived for ring in rings]))
    for ring, a in zip(rings, arrived, strict=True):
        ring.arrived = a
    return value


def depart(value, rings):
    rings = [ring for ring in rings if ring.left]
    for ring in rings:
        if ring.ready is None:
            ring.prepare()
    value, ready = lax.optimization_barrier((value, [ring.ready for ring in rings]))
    for ring, r in zip(rings, ready, strict=True):
        ring.ready = r
        ring.launch()
    return value


def halves(value, half):
    if half is None:
        return value
    middle = value.shape[0] // 2
    return value[middle:] if half else value[:middle]


def scatter(value, axes):
    return lax.psum_scatter(value, axes, scatter_dimension=0, tiled=True)


def gather(value, axes):
    return lax.all_gather(value, axes, axis=0, tiled=True)


def per_device(
    tokens,
    attention_gain,
    joint_weight,
    output_weight,
    feed_gain,
    gate_weight,
    up_weight,
    down_weight,
    cotangent,
    segment_lengths,
    parents,
):
    rows = lax.axis_size(ROW)
    columns = lax.axis_size("col")
    cores = lax.axis_size("core")
    own = tokens.shape[0] // rows
    held = own * cores
    groups = KV_HEADS // cores
    tables = tree_tables(segment_lengths, parents)
    row = lax.axis_index(ROW)
    column = lax.axis_index("col")
    high = lax.axis_index("high")
    core = lax.axis_index("core")
    index = column * tokens.shape[0] + row * own + jnp.arange(own, dtype=jnp.int32)
    cosines, sines = rotary_tables(index, tables)
    first = column * tokens.shape[0] + high * held

    spot = jnp.where(high == 0, column, 2 * columns - 1 - column)
    spots = lax.rem(spot + jnp.arange(2 * columns, dtype=jnp.int32), 2 * columns)
    far = spots >= columns
    ring_column = jnp.where(far, 2 * columns - 1 - spots, spots)
    ring_high = far.astype(jnp.int32)
    key_first = ring_column * tokens.shape[0] + ring_high * held
    key_index = (key_first[:, None] + jnp.arange(held, dtype=jnp.int32)[None, :]).reshape(-1)

    block = 256 if held % 256 == 0 else 128
    lists, counts = block_lists(first, key_index, block, held, tables)
    key_hot = segment_hot(key_index, tables).astype(F32)
    marks = jnp.pad(key_hot, ((0, 0), (HEAD_DIM, HEAD_DIM - key_hot.shape[1]))).astype(BF16)
    own_hot = segment_hot(index, tables).astype(F32)
    reach = jnp.sum(own_hot[:, :, None] * tables[2][None], axis=1)
    bars = jnp.pad((reach - 1.0) * BIG, ((0, 0), (HEAD_DIM, HEAD_DIM - reach.shape[1]))).astype(BF16)

    def exchange(value, axes):
        return lax.all_to_all(value, axes, split_axis=0, concat_axis=0, tiled=True)

    joint_blocks = gather(joint_weight, ALL_COL).reshape(columns, D, -1)
    gains = jnp.broadcast_to(jnp.stack([attention_gain, feed_gain])[None], (rows, 2, attention_gain.shape[0]))
    extended = jnp.concatenate([tokens.reshape(rows, own, -1), jnp.pad(gains, ((0, 0), (0, 14), (0, 0)))], axis=1)
    extended = exchange(extended, ROW)

    def plan(*places):
        keys = jnp.concatenate([key_index[i * held : j * held] for i, j in places])
        return (jnp.concatenate([marks[i * held : j * held] for i, j in places]), *block_lists(first, keys, block, held, tables))

    chips = 2 * columns
    plans = [plan((0, 2), (chips - 1, chips))]
    plans += [plan((s, s + 1), (chips - s, chips - s + 1)) for s in range(2, columns)]
    plans += [plan((columns, columns + 1))]
    (marks, lists, counts, plans), extended = lax.optimization_barrier(((marks, lists, counts, plans), extended))
    x, normed_one, joint_full, packed, value, gains = project_in(extended, joint_blocks, cosines, sines, bars)
    value, packed = lax.optimization_barrier((exchange(value, "core").reshape(held, -1), packed))
    packed = exchange(packed, "core").reshape(held, -1)
    width = gate_weight.shape[1]
    unit = width // 2 if width % 256 == 0 else width
    padding = jnp.zeros((output_weight.shape[1], -output_weight.shape[0] % unit), BF16)
    late = jnp.concatenate([gate_weight, up_weight, down_weight.T, output_weight.T, padding], axis=1)
    late = gather(late, ALL_COL).reshape(columns, D, -1)
    pieces = []
    state = None
    ahead, behind = ring_steps(columns)
    to_next, to_last = lax.ppermute(value, RING, ahead), lax.ppermute(value, RING, behind)
    fronts, backs = [], []

    def attend(state, plan, some, ends):
        keys, lists_here, counts_here = plan
        return tuple(attention_stage(lists_here, counts_here, packed, some, keys, state, ends))

    middle = held // 2
    for step in range(1, columns):
        fronts.append(to_next)
        backs.append(to_last)
        if step < columns - 1:
            further = (lax.ppermute(to_next, RING, ahead), lax.ppermute(to_last, RING, behind))
        else:
            further = (lax.ppermute(to_next[:middle], RING, ahead), lax.ppermute(to_last[middle:], RING, behind))
        some = [value, to_last, to_next] if step == 1 else [to_last, to_next]
        if step == 1:
            cotangent, further = lax.optimization_barrier((cotangent, further))
            upstream = exchange(cotangent.reshape(rows, own, -1), ROW).transpose(1, 0, 2).reshape(own, D)
        state = attend(state, plans[step - 1], some, False)
        state, further = lax.optimization_barrier((state, further))
        to_next, to_last = further
    pieces = [value, *backs, to_next, to_last, *reversed(fronts)]
    upstream, state = lax.optimization_barrier((upstream, state))
    state = attend(state, plans[columns - 1], [to_next, to_last], True)
    attended, lse = lax.cond(
        jnp.any(state[1] != state[1]),
        lambda: tuple(attention_forward(lists, counts, packed, pieces, marks)),
        lambda: tuple(state),
    )
    attended_rows = exchange(attended.reshape(cores, own, -1), "core")

    attended_rows, hidden, normed_two, output_full = project_out(attended_rows, late, x, gains, ATT // columns, late.shape[2] - 3 * width)
    mixed, gate_back, up_back, feed_out, normed_two_back = feed_forward(normed_two, upstream, late, width)

    hidden_back, hidden_low, heads_back, gain_two_part = output_back(normed_two_back, hidden, upstream, gains, output_full)
    heads_back, mixed = lax.optimization_barrier((heads_back, mixed))
    heads_back = exchange(heads_back, "core").reshape(held, -1)
    feed_parts = gradient_parts(columns, rows, None, (normed_two, [gate_back, up_back]), (upstream, [mixed]))
    feed_parts, heads_back = lax.optimization_barrier((feed_parts, heads_back))
    feed_summed = scatter(feed_parts.reshape(-1, feed_parts.shape[3]), ALL_COL)
    output_parts = gradient_parts(columns, rows, gain_two_part[0], (hidden_low, [attended_rows]))

    query_backs, pair_rings = [], []
    for g in range(groups):
        heads_back = depart(heads_back, pair_rings)
        query_back, pair_back = attention_backward(g, lists, counts, packed, heads_back, attended, pieces, marks, lse)
        pair_back = pair_back.reshape(2 * columns, held, -1)
        query_backs.append(query_back)
        pair_back = after(pair_back, pair_rings)
        pair_rings.append(RingScatter(lambda s, half, v=pair_back: halves(v[s], half).astype(F32), columns))
    pair_rings[-1].launch()
    query_backs, feed_out = after((query_backs, feed_out), pair_rings[-1:])
    query_back = exchange(jnp.concatenate(query_backs, axis=1).reshape(cores, own, -1), "core")
    layer_low = (hidden + feed_out).astype(BF16).reshape(own, rows, -1).transpose(1, 0, 2)
    held_pairs = jnp.concatenate([ring.finish().astype(BF16) for ring in pair_rings], axis=1)
    held_pairs, query_back, layer_low, feed_summed, output_parts = lax.optimization_barrier(
        (held_pairs, query_back, layer_low, feed_summed, output_parts)
    )
    feed_summed = feed_summed.astype(F32)
    output_summed = scatter(output_parts.reshape(-1, output_parts.shape[3]), ALL_COL).astype(F32)
    pair_back = exchange(held_pairs.reshape(cores, own, -1), "core")
    layer_output = exchange(layer_low, ROW).reshape(rows * own, -1)
    joint_low, input_part, gain_one_part = joint_back(
        query_back, pair_back, cosines, sines, joint_full, x, gains, hidden_back, rows
    )
    joint_low, layer_output = lax.optimization_barrier((joint_low, layer_output))
    joint_parts = gradient_parts(columns, rows, gain_one_part[0], (normed_one, [joint_low]))
    joint_parts = joint_parts.reshape(2 * columns, cores, *joint_parts.shape[2:])
    places = ring_column * 2 + ring_high
    swap = [(0, 1), (1, 0)]
    joint_first = lax.dynamic_slice(joint_parts, (places[columns], 1 - core, 0, 0), (1, 1, *joint_parts.shape[2:]))[0, 0]
    joint_first = lax.ppermute(joint_first, "core", swap)
    joint_other = lax.dynamic_index_in_dim(joint_parts, 1 - core, 1, keepdims=False)
    joint_other = lax.ppermute(joint_other, "core", swap)

    def joint_part(s, half):
        mine = lax.dynamic_slice(joint_parts, (places[s], core, 0, 0), (1, 1, *joint_parts.shape[2:]))[0, 0]
        other = joint_first if s == columns else lax.dynamic_index_in_dim(joint_other, places[s], 0, keepdims=False)
        return halves(mine, half).astype(F32) + halves(other, half).astype(F32)

    joint_ring = RingScatter(joint_part, columns)
    input_gradient = exchange(input_part, ROW).reshape(rows * own, -1).astype(F32)
    joint_summed = joint_ring.finish()
    narrow, joined = ATT // columns, joint_weight.shape[1]
    return (
        layer_output,
        input_gradient,
        joint_summed[:, joined],
        joint_summed[:, :joined],
        output_summed[:, :narrow].T,
        output_summed[:, narrow],
        feed_summed[:, :width],
        feed_summed[:, width : 2 * width],
        feed_summed[:, 2 * width :].T,
    )


def solution(mesh):
    leaves, rows, columns = (mesh.shape[name] for name in ("leaf", "row", "col"))
    split = Mesh(mesh.devices.reshape(leaves, rows // 2, 2, columns), ("leaf", "high", "core", "col"))
    return jax.shard_map(
        per_device,
        mesh=split,
        in_specs=(
            P(("leaf", "col"), ROW),
            P(ROW),
            P(ROW, "col"),
            P("col", ROW),
            P(ROW),
            P(ROW, "col"),
            P(ROW, "col"),
            P("col", ROW),
            P(("leaf", "col"), ROW),
            P("leaf"),
            P("leaf"),
        ),
        out_specs=(
            P(("leaf", "col"), ROW),
            P(("leaf", "col"), ROW),
            P(("leaf", *ROW)),
            P(("leaf", *ROW), "col"),
            P(("leaf", "col"), ROW),
            P(("leaf", *ROW)),
            P(("leaf", *ROW), "col"),
            P(("leaf", *ROW), "col"),
            P(("leaf", "col"), ROW),
        ),
        check_vma=False,
    )
```

```python
import functools

import jax
import jax.numpy as jnp
from jax import lax
from jax.experimental import pallas as pl
from jax.experimental.pallas import tpu as pltpu
from jax.sharding import Mesh
from jax.sharding import PartitionSpec as P

D = 1152
HEADS = 18
KV_HEADS = 6
HEAD_DIM = 64
REPEAT = HEADS // KV_HEADS
ATT = HEADS * HEAD_DIM
KEYS = KV_HEADS * HEAD_DIM

EPSILON = 1e-05
THETA = 10000.0
BIG = 2.0**30
LOG2E = 1.4426950408889634
UNROLL = 8
BF16 = jnp.bfloat16
F32 = jnp.float32
NT = (((1,), (1,)), ((), ()))
NN = (((1,), (0,)), ((), ()))


def dg(a, b, dims):
    return lax.dot_general(a, b, dims, preferred_element_type=F32)


def tree_tables(segment_lengths, parents):
    count = segment_lengths.shape[0]
    labels = jnp.arange(count, dtype=jnp.int32)
    ends = jnp.sum(jnp.where(labels[None, :] <= labels[:, None], segment_lengths[None, :], 0), axis=1)
    starts = ends - segment_lengths
    parent_hot = parents[:, None] == labels[None, :]
    grand = jnp.sum(jnp.where(parent_hot, parents[None, :], 0), axis=1)
    self_mark = labels[:, None] == labels[None, :]
    grand_mark = grand[:, None] == labels[None, :]
    ancestry = (self_mark | parent_hot | grand_mark).astype(F32)
    strict = (parent_hot | grand_mark) & jnp.logical_not(self_mark)
    offsets = jnp.sum(jnp.where(strict, segment_lengths[None, :], 0), axis=1)
    return (ends, starts, ancestry, offsets)


def segment_hot(index, tables):
    ends, starts, _, _ = tables
    return (index[:, None] >= starts[None, :]) & (index[:, None] < ends[None, :])


def rotary_tables(index, tables):
    hot = segment_hot(index, tables)
    depth = index + jnp.sum(jnp.where(hot, (tables[3] - tables[1])[None, :], 0), axis=1)
    half = HEAD_DIM // 2
    rates = THETA ** (-jnp.arange(half, dtype=F32) / half)
    angles = depth.astype(F32)[:, None] * rates[None, :]
    cosines, sines = jnp.cos(angles), jnp.sin(angles)
    return (jnp.concatenate([cosines] * 4, axis=1), jnp.concatenate([-sines, sines] * 2, axis=1))


def block_lists(first, key_index, block, held, tables):
    ends, starts, ancestry, _ = tables
    blocks = held // block
    key_low = key_index[::block]
    labels = jnp.arange(key_low.shape[0], dtype=jnp.int32)
    low = first + jnp.arange(blocks, dtype=jnp.int32) * block
    high = low + block
    query_has = ((starts[None, :] < high[:, None]) & (ends[None, :] > low[:, None])).astype(F32)
    key_has = ((starts[None, :] < key_low[:, None] + block) & (ends[None, :] > key_low[:, None])).astype(F32)
    reach = jnp.sum(query_has[:, :, None] * ancestry[None], axis=1)
    seen = jnp.sum(reach[:, None, :] * key_has[None], axis=2) > 0.5
    seen = seen & (key_low[None, :] < low[:, None])
    before = labels[None, :] < labels[:, None]
    rank = jnp.sum((seen[:, None, :] & before[None]).astype(jnp.int32), axis=2)
    place = seen[:, None, :] & (rank[:, None, :] == labels[None, :, None])
    lists = jnp.sum(jnp.where(place, labels[None, None, :], 0), axis=2)
    counts = jnp.sum(seen.astype(jnp.int32), axis=1)
    own = jnp.sum(jnp.where(key_low[None, :] == low[:, None], labels[None, :], 0), axis=1)
    lists = jnp.where(labels[None, :] == counts[:, None], own[:, None], lists)
    return (lists.reshape(-1).astype(jnp.int32), counts.astype(jnp.int32))


def cascade(count, unroll, steps):
    def body(i, c):
        steps(i * unroll, unroll)
        return c

    whole = count // unroll
    lax.fori_loop(0, whole, body, 0)
    start = whole * unroll
    size = unroll // 2
    while size:
        some = ((count - start) // size) > 0
        pl.when(some)(functools.partial(steps, start, size))
        start = start + jnp.where(some, size, 0)
        size //= 2


def causal(scores, heads):
    rows = lax.broadcasted_iota(jnp.int32, scores.shape, 0)
    columns = lax.rem(lax.broadcasted_iota(jnp.int32, scores.shape, 1), scores.shape[1] // heads)
    return jnp.where(rows <= columns, scores, -BIG)


def stacked(ref):
    value, wide = ref[...], 2 * HEAD_DIM
    return jnp.concatenate([value[:, h * wide : (h + 1) * wide] for h in range(value.shape[1] // wide)], axis=0)


def beside(value, heads):
    rows = value.shape[0] // heads
    return jnp.concatenate([value[h * rows : (h + 1) * rows] for h in range(heads)], axis=1)


def left_half(shape):
    return lax.broadcasted_iota(jnp.int32, shape, 1) < HEAD_DIM


def fetch(pieces, group, kv_ref, sems):
    copies, start = [], 0
    for i, piece in enumerate(pieces):
        lanes = pl.ds(pl.multiple_of(group * 2 * HEAD_DIM, 2 * HEAD_DIM), 2 * HEAD_DIM)
        target = kv_ref.at[pl.ds(start, piece.shape[0])]
        copies.append(pltpu.make_async_copy(piece.at[:, lanes], target, sems.at[i]))
        start += piece.shape[0]
    for copy in copies:
        copy.start()
    for copy in copies:
        copy.wait()


def forward_kernel(lists, counts, q_ref, mark_ref, *refs):
    *pieces, o_ref, lse_ref, top_ref, sum_ref, kv_ref, vt_ref, sems = refs
    block = pl.program_id(1)
    heads, rows = q_ref.shape[1] // (2 * HEAD_DIM), q_ref.shape[0]
    total = kv_ref.shape[0]
    stride = total // rows
    count = counts[block]

    @pl.when(block == 0)
    def _():
        fetch(pieces, pl.program_id(0), kv_ref, sems)

        def flip(i, c):
            k0 = pl.multiple_of(i * rows, rows)
            turned = kv_ref[pl.ds(k0, rows), :].T
            vt_ref[:HEAD_DIM, pl.ds(k0, rows)] = turned[HEAD_DIM:]
            return c

        lax.fori_loop(0, stride, flip, 0)
        tail = (vt_ref.shape[0] - HEAD_DIM, total)
        vt_ref[HEAD_DIM:] = jnp.where(lax.broadcasted_iota(jnp.int32, tail, 0) == 0, 1.0, 0.0).astype(BF16)

    def queries():
        return stacked(q_ref)

    def blocks(start, n):
        offs = [pl.multiple_of(lists[block * stride + start + u] * rows, rows) for u in range(n)]
        kv = jnp.concatenate([kv_ref[pl.ds(k0, rows), :] for k0 in offs], axis=0)
        mark = jnp.concatenate([mark_ref[pl.ds(k0, rows), :] for k0 in offs], axis=0)
        vt = jnp.concatenate([vt_ref[:, pl.ds(k0, rows)] for k0 in offs], axis=1)
        return jnp.where(left_half(kv.shape), kv, mark), vt

    def begin():
        k, vt = blocks(count, 1)
        scores = causal(dg(k, queries(), NT), heads)
        top = jnp.max(scores, axis=0, keepdims=True)
        top_ref[...] = top
        sum_ref[...] = dg(vt, jnp.exp2(scores - top).astype(BF16), NN)

    def steps(start, n):
        k, vt = blocks(start, n)
        weights = jnp.exp2(dg(k, queries(), NT) - top_ref[...]).astype(BF16)
        sum_ref[...] += dg(vt, weights, NN)

    begin()
    cascade(count, UNROLL, steps)

    @pl.when(jnp.logical_not(jnp.max(sum_ref[HEAD_DIM : HEAD_DIM + 1, :]) < 2.0**100))
    def _():
        begin()

        def online(n, c):
            k, vt = blocks(n, 1)
            scores = dg(k, queries(), NT)
            old = top_ref[...]
            new = jnp.maximum(old, jnp.max(scores, axis=0, keepdims=True))
            top_ref[...] = new
            sum_ref[...] = sum_ref[...] * jnp.exp2(old - new) + dg(vt, jnp.exp2(scores - new).astype(BF16), NN)
            return c

        lax.fori_loop(0, count, online, 0)

    total_row = sum_ref[HEAD_DIM : HEAD_DIM + 1, :]
    spread = jnp.concatenate([jnp.zeros((HEAD_DIM, heads * rows), F32), sum_ref[:HEAD_DIM, :] / total_row], axis=0)
    o_ref[...] = beside(spread.T.astype(BF16), heads)
    lse_ref[0, 0] = top_ref[...] + jnp.log2(total_row)


def attention_forward(lists, counts, q, pieces, marks):
    tokens, wide, heads = q.shape[0], 2 * HEAD_DIM, REPEAT
    groups = q.shape[1] // (wide * heads)
    total = marks.shape[0]
    blocks = counts.shape[0]
    rows = tokens // blocks
    tall = HEAD_DIM + 16
    return pl.pallas_call(
        forward_kernel,
        grid_spec=pltpu.PrefetchScalarGridSpec(
            num_scalar_prefetch=2,
            grid=(groups, blocks),
            in_specs=[
                pl.BlockSpec((rows, heads * wide), lambda g, b, *_: (b, g)),
                pl.BlockSpec((total, wide), lambda g, b, *_: (0, 0)),
                *(pl.BlockSpec(memory_space=pl.ANY) for _ in pieces),
            ],
            out_specs=[
                pl.BlockSpec((rows, heads * wide), lambda g, b, *_: (b, g)),
                pl.BlockSpec((1, 1, 1, heads * rows), lambda g, b, *_: (g, b, 0, 0)),
            ],
            scratch_shapes=[
                pltpu.VMEM((1, heads * rows), F32),
                pltpu.VMEM((tall, heads * rows), F32),
                pltpu.VMEM((total, wide), BF16),
                pltpu.VMEM((tall, total), BF16),
                pltpu.SemaphoreType.DMA((len(pieces),)),
            ],
        ),
        out_shape=[
            jax.ShapeDtypeStruct((tokens, groups * heads * wide), BF16),
            jax.ShapeDtypeStruct((groups, blocks, 1, heads * rows), F32),
        ],
        compiler_params=pltpu.CompilerParams(vmem_limit_bytes=48 * 2**20),
        cost_estimate=pl.CostEstimate(
            flops=groups * heads * tokens * total * 256, bytes_accessed=groups * total * 512, transcendentals=0
        ),
        name="attention_forward",
    )(lists, counts, q, marks, *pieces)


def stage_kernel(begins, ends, lists, counts, q_ref, mark_ref, *refs):
    refs = list(refs)
    sums_in, tops_in = ([refs.pop(0), refs.pop(0)] if not begins else (None, None))
    *pieces, first_ref, second_ref, top_ref, sum_ref, kv_ref, vt_ref, sems = refs
    block = pl.program_id(1)
    heads, rows = q_ref.shape[1] // (2 * HEAD_DIM), q_ref.shape[0]
    total = kv_ref.shape[0]
    stride = total // rows
    count = counts[block]

    @pl.when(block == 0)
    def _():
        fetch(pieces, pl.program_id(0), kv_ref, sems)

        def flip(i, c):
            k0 = pl.multiple_of(i * rows, rows)
            turned = kv_ref[pl.ds(k0, rows), :].T
            vt_ref[:HEAD_DIM, pl.ds(k0, rows)] = turned[HEAD_DIM:]
            return c

        lax.fori_loop(0, stride, flip, 0)
        tail = (vt_ref.shape[0] - HEAD_DIM, total)
        vt_ref[HEAD_DIM:] = jnp.where(lax.broadcasted_iota(jnp.int32, tail, 0) == 0, 1.0, 0.0).astype(BF16)

    def queries():
        return stacked(q_ref)

    def blocks(start, n):
        offs = [pl.multiple_of(lists[block * stride + start + u] * rows, rows) for u in range(n)]
        kv = jnp.concatenate([kv_ref[pl.ds(k0, rows), :] for k0 in offs], axis=0)
        mark = jnp.concatenate([mark_ref[pl.ds(k0, rows), :] for k0 in offs], axis=0)
        vt = jnp.concatenate([vt_ref[:, pl.ds(k0, rows)] for k0 in offs], axis=1)
        return jnp.where(left_half(kv.shape), kv, mark), vt

    if begins:
        k, vt = blocks(count, 1)
        scores = causal(dg(k, queries(), NT), heads)
        top = jnp.max(scores, axis=0, keepdims=True)
        top_ref[...] = top
        sum_ref[...] = dg(vt, jnp.exp2(scores - top).astype(BF16), NN)
    else:
        top_ref[...] = tops_in[0, 0]
        sum_ref[...] = sums_in[0, 0]

    def steps(start, n):
        k, vt = blocks(start, n)
        weights = jnp.exp2(dg(k, queries(), NT) - top_ref[...]).astype(BF16)
        sum_ref[...] += dg(vt, weights, NN)

    cascade(count, UNROLL, steps)
    if ends:
        total_row = sum_ref[HEAD_DIM : HEAD_DIM + 1, :]
        spread = jnp.concatenate([jnp.zeros((HEAD_DIM, heads * rows), F32), sum_ref[:HEAD_DIM, :] / total_row], axis=0)
        first_ref[...] = beside(spread.T.astype(BF16), heads)
        second_ref[0, 0] = jnp.where(total_row < 2.0**100, top_ref[...] + jnp.log2(total_row), jnp.nan)
    else:
        first_ref[0, 0] = sum_ref[...]
        second_ref[0, 0] = top_ref[...]


def attention_stage(lists, counts, q, pieces, marks, state, ends):
    tokens, wide, heads = q.shape[0], 2 * HEAD_DIM, REPEAT
    groups = q.shape[1] // (wide * heads)
    total = marks.shape[0]
    blocks = counts.shape[0]
    rows = tokens // blocks
    tall = HEAD_DIM + 16
    lanes = heads * rows
    held_specs = [
        pl.BlockSpec((1, 1, tall, lanes), lambda g, b, *_: (g, b, 0, 0)),
        pl.BlockSpec((1, 1, 1, lanes), lambda g, b, *_: (g, b, 0, 0)),
    ]
    tops = jax.ShapeDtypeStruct((groups, blocks, 1, lanes), F32)
    if ends:
        out_specs = [pl.BlockSpec((rows, heads * wide), lambda g, b, *_: (b, g)), held_specs[1]]
        out_shape = [jax.ShapeDtypeStruct((tokens, groups * heads * wide), BF16), tops]
    else:
        out_specs = held_specs
        out_shape = [jax.ShapeDtypeStruct((groups, blocks, tall, lanes), F32), tops]
    return pl.pallas_call(
        functools.partial(stage_kernel, state is None, ends),
        grid_spec=pltpu.PrefetchScalarGridSpec(
            num_scalar_prefetch=2,
            grid=(groups, blocks),
            in_specs=[
                pl.BlockSpec((rows, heads * wide), lambda g, b, *_: (b, g)),
                pl.BlockSpec((total, wide), lambda g, b, *_: (0, 0)),
                *([] if state is None else held_specs),
                *(pl.BlockSpec(memory_space=pl.ANY) for _ in pieces),
            ],
            out_specs=out_specs,
            scratch_shapes=[
                pltpu.VMEM((1, lanes), F32),
                pltpu.VMEM((tall, lanes), F32),
                pltpu.VMEM((total, wide), BF16),
                pltpu.VMEM((tall, total), BF16),
                pltpu.SemaphoreType.DMA((len(pieces),)),
            ],
        ),
        out_shape=out_shape,
        compiler_params=pltpu.CompilerParams(vmem_limit_bytes=40 * 2**20),
        cost_estimate=pl.CostEstimate(
            flops=groups * heads * tokens * total * 256, bytes_accessed=groups * total * 512, transcendentals=0
        ),
        name="attention_stage",
    )(lists, counts, q, marks, *(() if state is None else state), *pieces)


def backward_kernel(group, lists, counts, q_ref, do_ref, o_ref, mark_ref, lse_ref, *refs):
    *pieces, dq_ref, dkv_ref, dq_sum, dkv_sum, kv_ref, kt_ref, delta_ref, sems = refs
    block = pl.program_id(0)
    heads, rows = q_ref.shape[1] // (2 * HEAD_DIM), q_ref.shape[0]
    total = kv_ref.shape[0]
    stride = total // rows
    count = counts[block]

    @pl.when(block == 0)
    def _():
        dkv_sum[...] = jnp.zeros(dkv_sum.shape, F32)
        fetch(pieces, group, kv_ref, sems)

        def flip(i, c):
            k0 = pl.multiple_of(i * rows, rows)
            turned = kv_ref[pl.ds(k0, rows), :].T
            kt_ref[:, pl.ds(k0, rows)] = turned[:HEAD_DIM]
            return c

        lax.fori_loop(0, stride, flip, 0)

    dq_sum[...] = jnp.zeros(dq_sum.shape, F32)
    products = stacked(do_ref).astype(F32) * stacked(o_ref).astype(F32)
    delta_ref[...] = jnp.sum(products.T, axis=0, keepdims=True)

    def steps(start, n, masked):
        q, do = stacked(q_ref), stacked(do_ref)
        offs = [pl.multiple_of(lists[block * stride + start + u] * rows, rows) for u in range(n)]
        kv = jnp.concatenate([kv_ref[pl.ds(k0, rows), :] for k0 in offs], axis=0)
        mark = jnp.concatenate([mark_ref[pl.ds(k0, rows), :] for k0 in offs], axis=0)
        kt = jnp.concatenate([kt_ref[:, pl.ds(k0, rows)] for k0 in offs], axis=1)
        scores = dg(jnp.where(left_half(kv.shape), kv, mark), q, NT) - lse_ref[0, 0]
        if masked:
            scores = causal(scores, heads)
        chances = jnp.exp2(scores)
        back = dg(kv, do, NT) - delta_ref[...]
        score_back = (chances * back).astype(BF16)
        only_q = jnp.where(left_half(q.shape), q, jnp.zeros_like(q))
        update = dg(score_back, only_q, NN) + dg(chances.astype(BF16), do, NN)
        dq_sum[...] += dg(kt, score_back, NN)
        for u in range(n):
            dkv_sum[pl.ds(offs[u], rows), :] += update[u * rows : (u + 1) * rows]

    steps(count, 1, True)
    cascade(count, UNROLL, lambda start, n: steps(start, n, False))
    spread = jnp.concatenate([dq_sum[...] * HEAD_DIM**-0.5, jnp.zeros(dq_sum.shape, F32)], axis=0)
    dq_ref[...] = beside(spread.T.astype(BF16), heads)

    @pl.when(block == pl.num_programs(0) - 1)
    def _():
        summed = dkv_sum[...]
        dkv_ref[...] = jnp.where(left_half(summed.shape), summed * (1.0 / LOG2E), summed).astype(BF16)


def attention_backward(group, lists, counts, q, do, o, pieces, marks, lse):
    tokens, wide, heads = q.shape[0], 2 * HEAD_DIM, REPEAT
    total = marks.shape[0]
    blocks = counts.shape[0]
    rows = tokens // blocks
    block = pl.BlockSpec((rows, heads * wide), lambda b, *_: (b, group))
    return pl.pallas_call(
        functools.partial(backward_kernel, group),
        grid_spec=pltpu.PrefetchScalarGridSpec(
            num_scalar_prefetch=2,
            grid=(blocks,),
            in_specs=[
                block,
                block,
                block,
                pl.BlockSpec((total, wide), lambda b, *_: (0, 0)),
                pl.BlockSpec((1, 1, 1, heads * rows), lambda b, *_: (group, b, 0, 0)),
                *(pl.BlockSpec(memory_space=pl.ANY) for _ in pieces),
            ],
            out_specs=[
                pl.BlockSpec((rows, heads * wide), lambda b, *_: (b, 0)),
                pl.BlockSpec((total, wide), lambda b, *_: (0, 0)),
            ],
            scratch_shapes=[
                pltpu.VMEM((HEAD_DIM, heads * rows), F32),
                pltpu.VMEM((total, wide), F32),
                pltpu.VMEM((total, wide), BF16),
                pltpu.VMEM((HEAD_DIM, total), BF16),
                pltpu.VMEM((1, heads * rows), F32),
                pltpu.SemaphoreType.DMA((len(pieces),)),
            ],
        ),
        out_shape=[
            jax.ShapeDtypeStruct((tokens, heads * wide), BF16),
            jax.ShapeDtypeStruct((total, wide), BF16),
        ],
        compiler_params=pltpu.CompilerParams(vmem_limit_bytes=60 * 2**20),
        cost_estimate=pl.CostEstimate(flops=heads * tokens * total * 640, bytes_accessed=total * 1024, transcendentals=0),
        name="attention_backward",
    )(lists, counts, q, do, o, marks, lse, *pieces)


def roll_half(value):
    return pltpu.roll(value, HEAD_DIM, 1)


def swap_quarters(value):
    quarter = HEAD_DIM // 2
    lane = lax.broadcasted_iota(jnp.int32, value.shape, 1)
    first = lax.rem(lane, HEAD_DIM) < quarter
    return jnp.where(first, pltpu.roll(value, value.shape[1] - quarter, 1), pltpu.roll(value, quarter, 1))


def root_mean(value):
    return lax.rsqrt(jnp.sum(value * value, axis=1, keepdims=True) / D + EPSILON)


def project_kernel(x4_ref, w_ref, cos_ref, sin_ref, bars_ref, x_ref, xa_ref, full_ref, query_ref, pair_ref, gains_ref, joint_ref):
    own = x_ref.shape[0]
    wide = 2 * HEAD_DIM
    x = jnp.concatenate([x4_ref[r, :own, :] for r in range(x4_ref.shape[0])], axis=1)
    gains = jnp.concatenate([x4_ref[r, own : own + 16, :] for r in range(x4_ref.shape[0])], axis=1).astype(F32)
    x_ref[...] = x
    gains_ref[...] = gains[:8]
    value = x.astype(F32)
    xa_ref[...] = (value * root_mean(value) * gains[0:1]).astype(BF16)
    full_ref[...] = jnp.concatenate([w_ref[c] for c in range(w_ref.shape[0])], axis=1)
    joint_ref[...] = dg(xa_ref[...], full_ref[...], NN).astype(BF16)
    left = left_half((own, wide))
    bars = bars_ref[...].astype(F32)
    heads, pairs = HEADS // 2, KV_HEADS // 2

    def part(i):
        return joint_ref[:, i * wide : (i + 1) * wide].astype(F32)

    def turned(i):
        value = part(i)
        return value * cos_ref[...] + swap_quarters(value) * sin_ref[...]

    for i in range(HEADS // 2):
        value = turned(i) * (LOG2E * HEAD_DIM**-0.5)
        for j, head in ((2 * i, value), (2 * i + 1, roll_half(value))):
            start = (j % heads) * wide
            query_ref[j // heads, :, start : start + wide] = jnp.where(left, head, bars).astype(BF16)
    for i in range(KV_HEADS // 2):
        key = turned(HEADS // 2 + i)
        value = part(HEADS // 2 + KV_HEADS // 2 + i)
        for j, both in (
            (2 * i, jnp.where(left, key, roll_half(value))),
            (2 * i + 1, jnp.where(left, roll_half(key), value)),
        ):
            start = (j % pairs) * wide
            pair_ref[j // pairs, :, start : start + wide] = both.astype(BF16)


def project_in(x4, weight, cosines, sines, bars):
    own = cosines.shape[0]
    shapes = [
        jax.ShapeDtypeStruct((own, D), BF16),
        jax.ShapeDtypeStruct((own, D), BF16),
        jax.ShapeDtypeStruct((D, ATT + 2 * KEYS), BF16),
        jax.ShapeDtypeStruct((2, own, ATT), BF16),
        jax.ShapeDtypeStruct((2, own, KEYS), BF16),
        jax.ShapeDtypeStruct((8, D), F32),
    ]
    return pl.pallas_call(
        project_kernel,
        out_shape=shapes,
        scratch_shapes=[pltpu.VMEM((own, ATT + 2 * KEYS), BF16)],
        compiler_params=pltpu.CompilerParams(vmem_limit_bytes=56 * 2**20),
        cost_estimate=pl.CostEstimate(flops=2 * own * D * (ATT + 2 * KEYS), bytes_accessed=2**24, transcendentals=0),
        name="project_in",
    )(x4, weight, cosines, sines, bars)


def output_kernel(width, o_ref, w_ref, x_ref, gains_ref, rows_ref, hidden_ref, normed_ref, full_ref):
    wide = 2 * HEAD_DIM
    heads = HEADS // 2
    left = left_half((x_ref.shape[0], wide))
    for i in range(HEADS // 2):
        first, second = (
            o_ref[j // heads, :, (j % heads) * wide : (j % heads + 1) * wide] for j in (2 * i, 2 * i + 1)
        )
        first = roll_half(first.astype(F32))
        rows_ref[:, i * wide : (i + 1) * wide] = jnp.where(left, first, second.astype(F32)).astype(BF16)
    full_ref[...] = jnp.concatenate([w_ref[c, :, :width] for c in range(w_ref.shape[0])], axis=1)
    hidden = x_ref[...].astype(F32) + dg(rows_ref[...], full_ref[...], NT)
    hidden_ref[...] = hidden
    normed_ref[...] = (hidden * root_mean(hidden) * gains_ref[1:2]).astype(BF16)


def project_out(o, late, x, gains, width, padded):
    own = x.shape[0]
    place = late.shape[2] // padded - 1
    return pl.pallas_call(
        functools.partial(output_kernel, width),
        grid=(1,),
        in_specs=[
            pl.BlockSpec(o.shape, lambda i: (0, 0, 0)),
            pl.BlockSpec((late.shape[0], D, padded), lambda i: (0, 0, place)),
            pl.BlockSpec(x.shape, lambda i: (0, 0)),
            pl.BlockSpec(gains.shape, lambda i: (0, 0)),
        ],
        out_specs=[pl.BlockSpec((own, D), lambda i: (0, 0))] * 3 + [pl.BlockSpec((D, ATT), lambda i: (0, 0))],
        out_shape=[
            jax.ShapeDtypeStruct((own, ATT), BF16),
            jax.ShapeDtypeStruct((own, D), F32),
            jax.ShapeDtypeStruct((own, D), BF16),
            jax.ShapeDtypeStruct((D, ATT), BF16),
        ],
        compiler_params=pltpu.CompilerParams(vmem_limit_bytes=56 * 2**20),
        cost_estimate=pl.CostEstimate(flops=2 * own * D * ATT, bytes_accessed=2**24, transcendentals=0),
        name="project_out",
    )(o, late, x, gains)


def norm_back(upstream, value, gain):
    scale = root_mean(value)
    weighted = upstream * gain
    inner = jnp.sum(weighted * value, axis=1, keepdims=True)
    gain_back = jnp.sum(upstream * value * scale, axis=0, keepdims=True)
    return scale * weighted - value * (scale * scale * scale * inner / D), gain_back


def output_back_kernel(back_ref, hidden_ref, upstream_ref, gains_ref, full_ref, hidden_back_ref, low_ref, do_ref, sums_ref):
    wide = 2 * HEAD_DIM
    heads = HEADS // 2
    part, sums = norm_back(back_ref[...], hidden_ref[...], gains_ref[1:2])
    hidden_back = upstream_ref[...].astype(F32) + part
    hidden_back_ref[...] = hidden_back
    low_ref[...] = hidden_back.astype(BF16)
    sums_ref[...] = jnp.broadcast_to(sums, sums_ref.shape)
    attended_back = dg(low_ref[...], full_ref[...], NN)
    left = left_half((low_ref.shape[0], wide))
    for i in range(HEADS // 2):
        value = attended_back[:, i * wide : (i + 1) * wide]
        for j, head in ((2 * i, roll_half(value)), (2 * i + 1, value)):
            start = (j % heads) * wide
            do_ref[j // heads, :, start : start + wide] = jnp.where(left, 0.0, head).astype(BF16)


def output_back(back, hidden, upstream, gains, full):
    own = back.shape[0]
    return pl.pallas_call(
        output_back_kernel,
        out_shape=[
            jax.ShapeDtypeStruct((own, D), F32),
            jax.ShapeDtypeStruct((own, D), BF16),
            jax.ShapeDtypeStruct((2, own, ATT), BF16),
            jax.ShapeDtypeStruct((8, D), F32),
        ],
        compiler_params=pltpu.CompilerParams(vmem_limit_bytes=56 * 2**20),
        cost_estimate=pl.CostEstimate(flops=2 * own * D * ATT, bytes_accessed=2**24, transcendentals=0),
        name="output_back",
    )(back, hidden, upstream, gains, full)


def joint_back_kernel(query_ref, pair_ref, cos_ref, sin_ref, full_ref, x_ref, gains_ref, hidden_back_ref, joint_ref, out_ref, sums_ref):
    wide = 2 * HEAD_DIM
    heads, pairs = HEADS // 2, KV_HEADS // 2
    left = left_half((x_ref.shape[0], wide))

    def queries(j):
        return query_ref[j // heads, :, (j % heads) * wide : (j % heads + 1) * wide].astype(F32)

    def both(j):
        start = (j % pairs) * wide
        return pair_ref[j // pairs, :, start : start + wide].astype(F32)

    def store(i, value):
        joint_ref[:, i * wide : (i + 1) * wide] = value.astype(BF16)

    def back(value):
        return value * cos_ref[...] - swap_quarters(value) * sin_ref[...]

    for i in range(HEADS // 2):
        store(i, back(jnp.where(left, queries(2 * i), roll_half(queries(2 * i + 1)))))
    for i in range(KV_HEADS // 2):
        first, second = both(2 * i), both(2 * i + 1)
        store(HEADS // 2 + i, back(jnp.where(left, first, roll_half(second))))
        store(HEADS // 2 + KV_HEADS // 2 + i, jnp.where(left, roll_half(first), second))
    upstream = dg(joint_ref[...], full_ref[...], NT)
    part, sums = norm_back(upstream, x_ref[...].astype(F32), gains_ref[0:1])
    total = (hidden_back_ref[...] + part).astype(BF16)
    features = out_ref.shape[2]
    for r in range(out_ref.shape[0]):
        out_ref[r] = total[:, r * features : (r + 1) * features]
    sums_ref[...] = jnp.broadcast_to(sums, sums_ref.shape)


def joint_back(queries, pairs, cosines, sines, full, x, gains, hidden_back, rows):
    own = x.shape[0]
    return pl.pallas_call(
        joint_back_kernel,
        out_shape=[
            jax.ShapeDtypeStruct((own, ATT + 2 * KEYS), BF16),
            jax.ShapeDtypeStruct((rows, own, D // rows), BF16),
            jax.ShapeDtypeStruct((8, D), F32),
        ],
        compiler_params=pltpu.CompilerParams(vmem_limit_bytes=56 * 2**20),
        cost_estimate=pl.CostEstimate(flops=2 * own * D * (ATT + 2 * KEYS), bytes_accessed=2**24, transcendentals=0),
        name="joint_back",
    )(queries, pairs, cosines, sines, full, x, gains, hidden_back)


def feed_kernel(normed_ref, back_ref, gate_ref, up_ref, down_ref, mixed_ref, gate_back_ref, up_back_ref, out_ref, normed_back_ref):
    @pl.when(pl.program_id(0) == 0)
    def _():
        out_ref[...] = jnp.zeros(out_ref.shape, F32)
        normed_back_ref[...] = jnp.zeros(normed_back_ref.shape, F32)

    gate = dg(normed_ref[...], gate_ref[0], NN)
    up_value = dg(normed_ref[...], up_ref[0], NN)
    mixed_back = dg(back_ref[...], down_ref[0], NN)
    sigmoid = jax.nn.sigmoid(gate)
    silu = gate * sigmoid
    mixed = (silu * up_value).astype(BF16)
    gate_back = (mixed_back * up_value * (sigmoid * (1.0 + gate * (1.0 - sigmoid)))).astype(BF16)
    up_back = (mixed_back * silu).astype(BF16)
    mixed_ref[...] = mixed
    gate_back_ref[...] = gate_back
    up_back_ref[...] = up_back
    out_ref[...] += dg(mixed, down_ref[0], NT)
    normed_back_ref[...] += dg(gate_back, gate_ref[0], NT) + dg(up_back, up_ref[0], NT)


def feed_forward(normed, back, late, width):
    tokens = normed.shape[0]
    columns = late.shape[0]
    whole = pl.BlockSpec((tokens, D), lambda c: (0, 0))
    blocks = [pl.BlockSpec((1, D, width), lambda c, k=k: (c, 0, k)) for k in range(3)]
    out = pl.BlockSpec((tokens, width), lambda c: (0, c))
    return pl.pallas_call(
        feed_kernel,
        grid=(columns,),
        in_specs=[whole, whole, *blocks],
        out_specs=[out, out, out, whole, whole],
        out_shape=[jax.ShapeDtypeStruct((tokens, columns * width), BF16)] * 3 + [jax.ShapeDtypeStruct((tokens, D), F32)] * 2,
        compiler_params=pltpu.CompilerParams(vmem_limit_bytes=62 * 2**20),
        cost_estimate=pl.CostEstimate(
            flops=12 * tokens * D * columns * width, bytes_accessed=6 * D * columns * width, transcendentals=0
        ),
        name="feed_forward",
    )(normed, back, late, late, late)


def gradient_kernel(counts, blocked, summed, *refs):
    refs = list(refs)
    sets = [(refs.pop(0), [refs.pop(0) for _ in range(n)]) for n in counts]
    sums_ref = refs.pop(0) if summed else None
    out_ref, turned, held = refs[0], refs[1 : 1 + len(sets)], refs[1 + len(sets) :]
    step = pl.program_id(0)
    rows = out_ref.shape[1]
    features = sets[0][0].shape[1] // rows
    rights = [right for _, some in sets for right in some]
    whole = [right for right, flag in zip(rights, blocked, strict=True) if not flag]

    @pl.when(step == 0)
    def _():
        for (left, _), target in zip(sets, turned, strict=True):
            target[...] = left[...].T
        for right, block in zip(whole, held, strict=True):
            width = block.shape[2]
            for c in range(block.shape[0]):
                block[c] = right[:, c * width : (c + 1) * width]

    spare, flags, start = list(held), list(blocked), 0
    for (_, some), target in zip(sets, turned, strict=True):
        for right in some:
            value = right[...] if flags.pop(0) else spare.pop(0)[step]
            width = value.shape[1]
            part = dg(target[...], value, NN).astype(BF16)
            for r in range(rows):
                out_ref[0, r, :, start : start + width] = part[r * features : (r + 1) * features]
            start += width
    if summed:
        tail = (rows, features, out_ref.shape[3] - start)
        out_ref[0, :, :, start:] = jnp.broadcast_to(sums_ref[...], tail).astype(BF16)


def gradient_parts(columns, rows, sums, *sets):
    tokens = sets[0][0].shape[0]
    features = D // rows
    operands, specs, turned, held, blocked, wide = [], [], [], [], [], 0
    for left, rights in sets:
        operands.append(left)
        specs.append(pl.BlockSpec(left.shape, lambda c: (0, 0)))
        turned.append(pltpu.VMEM((left.shape[1], tokens), BF16))
        for right in rights:
            width = right.shape[1] // columns
            operands.append(right)
            wide += width
            if width % 128 == 0:
                specs.append(pl.BlockSpec((tokens, width), lambda c: (0, c)))
                blocked.append(True)
            else:
                specs.append(pl.BlockSpec(right.shape, lambda c: (0, 0)))
                held.append(pltpu.VMEM((columns, tokens, width), BF16))
                blocked.append(False)
    if sums is not None:
        wide = (wide // 128 + 1) * 128
        operands.append(sums.reshape(rows, features, 1))
        specs.append(pl.BlockSpec((rows, features, 1), lambda c: (0, 0, 0)))
    shape = (columns, rows, features, wide)
    return pl.pallas_call(
        functools.partial(gradient_kernel, [len(rights) for _, rights in sets], blocked, sums is not None),
        grid=(columns,),
        in_specs=specs,
        out_specs=pl.BlockSpec((1, *shape[1:]), lambda c: (c, 0, 0, 0)),
        out_shape=jax.ShapeDtypeStruct(shape, BF16),
        scratch_shapes=[*turned, *held],
        compiler_params=pltpu.CompilerParams(vmem_limit_bytes=60 * 2**20),
        cost_estimate=pl.CostEstimate(
            flops=2 * tokens * D * wide * columns, bytes_accessed=2 * D * wide * columns, transcendentals=0
        ),
        name="gradient_parts",
    )(*operands)


ROW = ("high", "core")
ALL_ROW = ("high", "core", "col")
ALL_COL = ("col", "high", "core")
RING = ("high", "col")


def ring_steps(columns):
    path = [*range(columns), *reversed(range(columns, 2 * columns))]
    ahead = [(path[i], path[(i + 1) % len(path)]) for i in range(len(path))]
    return ahead, [(b, a) for a, b in ahead]


class RingScatter:
    def __init__(self, part, columns):
        self.part, (self.ahead, self.behind), self.count = part, ring_steps(columns), 2 * columns
        self.left = self.count // 2
        self.arrived = None
        self.ready = (part(self.left, 0).astype(BF16), part(self.left, 1).astype(BF16))

    def launch(self):
        out, back = self.ready
        self.arrived = (lax.ppermute(out, RING, self.ahead), lax.ppermute(back, RING, self.behind))
        self.ready = None
        self.left -= 1

    def prepare(self):
        out, back = self.part(self.left, None), self.part(self.count - self.left, None)
        front, rear = (v.astype(F32) for v in self.arrived)
        half = front.shape[0]
        if half == out.shape[0]:
            out, back = out + front, back + rear
        else:
            out = jnp.concatenate([out[:half] + front, out[half:]], axis=0)
            back = jnp.concatenate([back[:half], back[half:] + rear], axis=0)
        self.ready = (out.astype(BF16), back.astype(BF16))

    def finish(self):
        while self.left or self.ready:
            if self.ready is None:
                self.prepare()
            self.ready = lax.optimization_barrier(self.ready)
            self.launch()
        return self.part(0, None) + self.arrived[0].astype(F32) + self.arrived[1].astype(F32)


def after(value, rings):
    value, arrived = lax.optimization_barrier((value, [ring.arrived for ring in rings]))
    for ring, a in zip(rings, arrived, strict=True):
        ring.arrived = a
    return value


def depart(value, rings):
    rings = [ring for ring in rings if ring.left]
    for ring in rings:
        if ring.ready is None:
            ring.prepare()
    value, ready = lax.optimization_barrier((value, [ring.ready for ring in rings]))
    for ring, r in zip(rings, ready, strict=True):
        ring.ready = r
        ring.launch()
    return value


def halves(value, half):
    if half is None:
        return value
    middle = value.shape[0] // 2
    return value[middle:] if half else value[:middle]


def scatter(value, axes):
    return lax.psum_scatter(value, axes, scatter_dimension=0, tiled=True)


def gather(value, axes):
    return lax.all_gather(value, axes, axis=0, tiled=True)


def per_device(
    tokens,
    attention_gain,
    joint_weight,
    output_weight,
    feed_gain,
    gate_weight,
    up_weight,
    down_weight,
    cotangent,
    segment_lengths,
    parents,
):
    rows = lax.axis_size(ROW)
    columns = lax.axis_size("col")
    cores = lax.axis_size("core")
    own = tokens.shape[0] // rows
    held = own * cores
    groups = KV_HEADS // cores
    tables = tree_tables(segment_lengths, parents)
    row = lax.axis_index(ROW)
    column = lax.axis_index("col")
    high = lax.axis_index("high")
    core = lax.axis_index("core")
    index = column * tokens.shape[0] + row * own + jnp.arange(own, dtype=jnp.int32)
    cosines, sines = rotary_tables(index, tables)
    first = column * tokens.shape[0] + high * held

    spot = jnp.where(high == 0, column, 2 * columns - 1 - column)
    spots = lax.rem(spot + jnp.arange(2 * columns, dtype=jnp.int32), 2 * columns)
    far = spots >= columns
    ring_column = jnp.where(far, 2 * columns - 1 - spots, spots)
    ring_high = far.astype(jnp.int32)
    key_first = ring_column * tokens.shape[0] + ring_high * held
    key_index = (key_first[:, None] + jnp.arange(held, dtype=jnp.int32)[None, :]).reshape(-1)

    block = 256 if held % 256 == 0 else 128
    lists, counts = block_lists(first, key_index, block, held, tables)
    key_hot = segment_hot(key_index, tables).astype(F32)
    marks = jnp.pad(key_hot, ((0, 0), (HEAD_DIM, HEAD_DIM - key_hot.shape[1]))).astype(BF16)
    own_hot = segment_hot(index, tables).astype(F32)
    reach = jnp.sum(own_hot[:, :, None] * tables[2][None], axis=1)
    bars = jnp.pad((reach - 1.0) * BIG, ((0, 0), (HEAD_DIM, HEAD_DIM - reach.shape[1]))).astype(BF16)

    def exchange(value, axes):
        return lax.all_to_all(value, axes, split_axis=0, concat_axis=0, tiled=True)

    joint_blocks = gather(joint_weight, ALL_COL).reshape(columns, D, -1)
    gains = jnp.broadcast_to(jnp.stack([attention_gain, feed_gain])[None], (rows, 2, attention_gain.shape[0]))
    extended = jnp.concatenate([tokens.reshape(rows, own, -1), jnp.pad(gains, ((0, 0), (0, 14), (0, 0)))], axis=1)
    extended = exchange(extended, ROW)

    def plan(*places):
        keys = jnp.concatenate([key_index[i * held : j * held] for i, j in places])
        return (jnp.concatenate([marks[i * held : j * held] for i, j in places]), *block_lists(first, keys, block, held, tables))

    chips = 2 * columns
    plans = [plan((0, 2), (chips - 1, chips))]
    plans += [plan((s, s + 1), (chips - s, chips - s + 1)) for s in range(2, columns)]
    plans += [plan((columns, columns + 1))]
    (marks, lists, counts, plans), extended = lax.optimization_barrier(((marks, lists, counts, plans), extended))
    x, normed_one, joint_full, packed, value, gains = project_in(extended, joint_blocks, cosines, sines, bars)
    value, packed = lax.optimization_barrier((exchange(value, "core").reshape(held, -1), packed))
    packed = exchange(packed, "core").reshape(held, -1)
    width = gate_weight.shape[1]
    unit = width // 2 if width % 256 == 0 else width
    padding = jnp.zeros((output_weight.shape[1], -output_weight.shape[0] % unit), BF16)
    late = jnp.concatenate([gate_weight, up_weight, down_weight.T, output_weight.T, padding], axis=1)
    late = gather(late, ALL_COL).reshape(columns, D, -1)
    pieces = []
    state = None
    ahead, behind = ring_steps(columns)
    to_next, to_last = lax.ppermute(value, RING, ahead), lax.ppermute(value, RING, behind)
    fronts, backs = [], []

    def attend(state, plan, some, ends):
        keys, lists_here, counts_here = plan
        return tuple(attention_stage(lists_here, counts_here, packed, some, keys, state, ends))

    middle = held // 2
    for step in range(1, columns):
        fronts.append(to_next)
        backs.append(to_last)
        if step < columns - 1:
            further = (lax.ppermute(to_next, RING, ahead), lax.ppermute(to_last, RING, behind))
        else:
            further = (lax.ppermute(to_next[:middle], RING, ahead), lax.ppermute(to_last[middle:], RING, behind))
        some = [value, to_last, to_next] if step == 1 else [to_last, to_next]
        if step == 1:
            cotangent, further = lax.optimization_barrier((cotangent, further))
            upstream = exchange(cotangent.reshape(rows, own, -1), ROW).transpose(1, 0, 2).reshape(own, D)
        state = attend(state, plans[step - 1], some, False)
        state, further = lax.optimization_barrier((state, further))
        to_next, to_last = further
    pieces = [value, *backs, to_next, to_last, *reversed(fronts)]
    upstream, state = lax.optimization_barrier((upstream, state))
    state = attend(state, plans[columns - 1], [to_next, to_last], True)
    attended, lse = lax.cond(
        jnp.any(state[1] != state[1]),
        lambda: tuple(attention_forward(lists, counts, packed, pieces, marks)),
        lambda: tuple(state),
    )
    attended_rows = exchange(attended.reshape(cores, own, -1), "core")

    attended_rows, hidden, normed_two, output_full = project_out(attended_rows, late, x, gains, ATT // columns, late.shape[2] - 3 * width)
    mixed, gate_back, up_back, feed_out, normed_two_back = feed_forward(normed_two, upstream, late, width)

    hidden_back, hidden_low, heads_back, gain_two_part = output_back(normed_two_back, hidden, upstream, gains, output_full)
    heads_back, mixed = lax.optimization_barrier((heads_back, mixed))
    heads_back = exchange(heads_back, "core").reshape(held, -1)
    feed_parts = gradient_parts(columns, rows, None, (normed_two, [gate_back, up_back]), (upstream, [mixed]))
    feed_parts, heads_back = lax.optimization_barrier((feed_parts, heads_back))
    feed_summed = scatter(feed_parts.reshape(-1, feed_parts.shape[3]), ALL_COL)
    output_parts = gradient_parts(columns, rows, gain_two_part[0], (hidden_low, [attended_rows]))

    query_backs, pair_rings = [], []
    for g in range(groups):
        heads_back = depart(heads_back, pair_rings)
        query_back, pair_back = attention_backward(g, lists, counts, packed, heads_back, attended, pieces, marks, lse)
        pair_back = pair_back.reshape(2 * columns, held, -1)
        query_backs.append(query_back)
        pair_back = after(pair_back, pair_rings)
        pair_rings.append(RingScatter(lambda s, half, v=pair_back: halves(v[s], half).astype(F32), columns))
    pair_rings[-1].launch()
    query_backs, feed_out, feed_summed, output_parts = after(
        (query_backs, feed_out, feed_summed, output_parts), pair_rings[-1:]
    )
    output_summed = scatter(output_parts.reshape(-1, output_parts.shape[3]), ALL_COL).astype(F32)
    query_back = exchange(jnp.concatenate(query_backs, axis=1).reshape(cores, own, -1), "core")
    layer_low = (hidden + feed_out).astype(BF16).reshape(own, rows, -1).transpose(1, 0, 2)
    held_pairs = jnp.concatenate([ring.finish().astype(BF16) for ring in pair_rings], axis=1)
    held_pairs, query_back, layer_low = lax.optimization_barrier((held_pairs, query_back, layer_low))
    feed_summed = feed_summed.astype(F32)
    pair_back = exchange(held_pairs.reshape(cores, own, -1), "core")
    layer_output = exchange(layer_low, ROW).reshape(rows * own, -1)
    joint_low, input_part, gain_one_part = joint_back(
        query_back, pair_back, cosines, sines, joint_full, x, gains, hidden_back, rows
    )
    joint_low, layer_output = lax.optimization_barrier((joint_low, layer_output))
    joint_parts = gradient_parts(columns, rows, gain_one_part[0], (normed_one, [joint_low]))
    joint_parts = joint_parts.reshape(2 * columns, cores, *joint_parts.shape[2:])
    places = ring_column * 2 + ring_high
    swap = [(0, 1), (1, 0)]
    joint_first = lax.dynamic_slice(joint_parts, (places[columns], 1 - core, 0, 0), (1, 1, *joint_parts.shape[2:]))[0, 0]
    joint_first = lax.ppermute(joint_first, "core", swap)
    joint_other = lax.dynamic_index_in_dim(joint_parts, 1 - core, 1, keepdims=False)
    joint_other = lax.ppermute(joint_other, "core", swap)

    def joint_part(s, half):
        mine = lax.dynamic_slice(joint_parts, (places[s], core, 0, 0), (1, 1, *joint_parts.shape[2:]))[0, 0]
        other = joint_first if s == columns else lax.dynamic_index_in_dim(joint_other, places[s], 0, keepdims=False)
        return halves(mine, half).astype(F32) + halves(other, half).astype(F32)

    joint_ring = RingScatter(joint_part, columns)
    input_gradient = exchange(input_part, ROW).reshape(rows * own, -1).astype(F32)
    joint_summed = joint_ring.finish()
    narrow, joined = ATT // columns, joint_weight.shape[1]
    return (
        layer_output,
        input_gradient,
        joint_summed[:, joined],
        joint_summed[:, :joined],
        output_summed[:, :narrow].T,
        output_summed[:, narrow],
        feed_summed[:, :width],
        feed_summed[:, width : 2 * width],
        feed_summed[:, 2 * width :].T,
    )


def solution(mesh):
    leaves, rows, columns = (mesh.shape[name] for name in ("leaf", "row", "col"))
    split = Mesh(mesh.devices.reshape(leaves, rows // 2, 2, columns), ("leaf", "high", "core", "col"))
    return jax.shard_map(
        per_device,
        mesh=split,
        in_specs=(
            P(("leaf", "col"), ROW),
            P(ROW),
            P(ROW, "col"),
            P("col", ROW),
            P(ROW),
            P(ROW, "col"),
            P(ROW, "col"),
            P("col", ROW),
            P(("leaf", "col"), ROW),
            P("leaf"),
            P("leaf"),
        ),
        out_specs=(
            P(("leaf", "col"), ROW),
            P(("leaf", "col"), ROW),
            P(("leaf", *ROW)),
            P(("leaf", *ROW), "col"),
            P(("leaf", "col"), ROW),
            P(("leaf", *ROW)),
            P(("leaf", *ROW), "col"),
            P(("leaf", *ROW), "col"),
            P(("leaf", "col"), ROW),
        ),
        check_vma=False,
    )
```
